512 devices in a mesh: slab: 32 (over z, core), sub: 16 (over x, y).
Axes of the slice: x: 4, y: 4, z: 16, core: 2. Of those that a mesh axis runs over, the one named last changes fastest.
Arguments:
- fields: float32 [6, 20, 131072], P(None, None, ('slab', 'sub')), may hold values from -6 to 6
- geometry: float32 [11, 131072], P(None, ('slab', 'sub')), as said below
- migrate_list: int32 [512, 32, 12], P(('slab', 'sub')), may hold values from -1 to 255, as said below
- trace_list: int32 [512, 16, 16], P(('slab', 'sub')), may hold values from 0 to 1535, as said below
- face_link: int32 [4, 196608], P(None, ('slab', 'sub')), may hold values from 0 to 1791, as said below
- face_orient: int32 [4, 196608], P(None, ('slab', 'sub')), may hold values from 0 to 6, as said below
Outputs:
- advanced: float32 [6, 20, 196608], P(None, None, ('slab', 'sub'))
- section_residual: float32 [6, 20, 196608], P(None, None, ('slab', 'sub'))
The draws below stay inside these ranges and needn't reach their ends.
Inputs may be any that keep to these rules, and one draw needn't show every extreme that they name: `migrate_list`: for each device and destination slab, the first entries (at least one) are distinct local element indices and the rest are -1; over the 32 destinations each of the device's elements appears exactly once; one slab position receives 12 elements from every device. `trace_list`: face codes f * 384 + e of the sending device, all distinct within a device; they name occupied slots. `face_link`: codes below 1536 name a face of the device's own occupied slots; each code from 1536 on is named by exactly one face of the device; walls and empty slots hold 0. `face_orient`: every face of an empty slot is 6. `geometry`: each diagonal entry of G is positive and at least three times any other entry of G in magnitude; eps and mu are positive.
All inputs are finite; a program needn't handle non-finite values.
Results may differ from the reference program's by a relative error of at most 0.0003.
Values sent between devices are 32-bit elements; how exact they have to be, the bound alone decides.
No kernel may reach another device: no remote copies, remote signals or barrier semaphores. Data moves between devices by JAX's collectives and lax.ppermute only.
A program may use at most 64 MiB of HBM per device.

```python
import math
import jax
import jax.numpy as jnp
from jax import lax

FIELDS = 6
NP = 20
ELEM_DEV = 256
CAP = 12
NEW_DEV = 384
TCAP = 16
ELEMS = 131072
N_SLAB = 32
N_SUB = 16


def shuffled(key, shape):
    row_width = shape[-1]
    random_noise = jax.random.randint(key, shape, 0, (1 << 30) // row_width)
    scores = random_noise * row_width + jnp.arange(row_width, dtype=jnp.int32)
    return jnp.argsort(scores, axis=-1).astype(jnp.int32)


def migration_counts(key):
    device_total = N_SLAB * N_SUB
    others = N_SLAB - 1
    spare_rows = ELEM_DEV - CAP
    even_share = spare_rows // others
    remainder = spare_rows - even_share * others
    move_limit = min(even_share // 2, CAP - even_share - 2)
    hot_slab = jax.random.randint(jax.random.fold_in(key, 101), (), 0, N_SLAB)
    rank_order = shuffled(jax.random.fold_in(key, 102), (device_total, others))
    pair_order = shuffled(jax.random.fold_in(key, 103), (device_total, others))
    move_sizes = jax.random.randint(jax.random.fold_in(key, 104), (device_total, others // 2 + 1), 0, move_limit + 1)
    pair_id = pair_order // 2
    paired = pair_id < others // 2
    move_step = jnp.take_along_axis(move_sizes, pair_id, axis=1)
    move_sign = 1 - 2 * (pair_order % 2)
    counts_other = even_share + (rank_order < remainder).astype(jnp.int32) + jnp.where(paired, move_sign * move_step, 0)
    slab_ids = jnp.arange(N_SLAB, dtype=jnp.int32)
    position = jnp.clip(slab_ids - (slab_ids > hot_slab).astype(jnp.int32), 0, others - 1)
    counts = jnp.where(slab_ids[None, :] == hot_slab, CAP, counts_other[:, position])
    return counts.astype(jnp.int32)


def live_slot_mask(key):
    counts = migration_counts(key)
    count_grid = counts.reshape(N_SLAB, N_SUB, N_SLAB).transpose(2, 1, 0)
    slot_ids = jnp.arange(CAP, dtype=jnp.int32)
    filled = slot_ids[None, None, None, :] < count_grid[:, :, :, None]
    return filled.reshape(N_SLAB * N_SUB, NEW_DEV)


def live_first(key, face_live):
    face_width = face_live.shape[1]
    mixed = shuffled(key, face_live.shape)
    scores = (1 - face_live.astype(jnp.int32)) * face_width + mixed
    return jnp.argsort(scores, axis=1).astype(jnp.int32)


def face_plan(key):
    live_slots = live_slot_mask(key)
    device_total = N_SLAB * N_SUB
    face_width = 4 * NEW_DEV
    face_live = jnp.tile(live_slots, (1, 4))
    ordering = live_first(jax.random.fold_in(key, 201), face_live)
    remote_total = N_SUB * TCAP
    device_rows = jnp.arange(device_total, dtype=jnp.int32)[:, None]
    targets = ordering[:, :remote_total]
    remote_codes = jnp.broadcast_to(face_width + jnp.arange(remote_total, dtype=jnp.int32)[None, :], targets.shape)
    link_codes = jnp.zeros((device_total, face_width), jnp.int32).at[device_rows, targets].set(remote_codes)
    is_remote = jnp.zeros((device_total, face_width), jnp.bool_).at[device_rows, targets].set(True)
    live_faces = 4 * jnp.sum(live_slots.astype(jnp.int32), axis=1)
    partner_order = live_first(jax.random.fold_in(key, 202), face_live)
    partner_index = jax.random.randint(jax.random.fold_in(key, 203), (device_total, face_width), 0, live_faces[:, None])
    partners = jnp.take_along_axis(partner_order, partner_index, axis=1)
    wall_faces = jax.random.randint(jax.random.fold_in(key, 204), (device_total, face_width), 0, 8) == 0
    turn_draw = jax.random.randint(jax.random.fold_in(key, 205), (device_total, face_width), 0, 6)
    inner = jnp.logical_and(face_live, jnp.logical_not(wall_faces))
    link_codes = jnp.where(is_remote, link_codes, jnp.where(inner, partners, 0))
    orient_codes = jnp.where(jnp.logical_or(is_remote, inner), turn_draw, 6)
    link_codes = link_codes.reshape(device_total, 4, NEW_DEV).transpose(1, 0, 2).reshape(4, -1)
    orient_codes = orient_codes.reshape(device_total, 4, NEW_DEV).transpose(1, 0, 2).reshape(4, -1)
    return (link_codes.astype(jnp.int32), orient_codes.astype(jnp.int32))


def draw_migrate_list(key, part):
    counts = migration_counts(key)
    key = jax.random.fold_in(key, 1)
    device_total = N_SLAB * N_SUB
    element_order = shuffled(key, (device_total, ELEM_DEV))
    starts = jnp.cumsum(counts, axis=1) - counts
    slot_ids = jnp.arange(CAP, dtype=jnp.int32)
    where_at = jnp.minimum(starts[:, :, None] + slot_ids[None, None, :], ELEM_DEV - 1)
    picked = jnp.take_along_axis(element_order, where_at.reshape(device_total, -1), axis=1).reshape(device_total, N_SLAB, CAP)
    return jnp.where(slot_ids[None, None, :] < counts[:, :, None], picked, -1).astype(jnp.int32)


def draw_trace_list(key, part):
    live_slots = live_slot_mask(key)
    key = jax.random.fold_in(key, 2)
    face_live = jnp.tile(live_slots, (1, 4))
    ordering = live_first(key, face_live)
    return ordering[:, :N_SUB * TCAP].reshape(N_SLAB * N_SUB, N_SUB, TCAP).astype(jnp.int32)


def draw_face_link(key, part):
    link_codes, orient_codes = face_plan(key)
    return link_codes


def draw_face_orient(key, part):
    link_codes, orient_codes = face_plan(key)
    return orient_codes


def draw_geometry(key, part):
    key = jax.random.fold_in(key, 7)
    key_list = jax.random.split(key, 5)
    sizes_log = jax.random.uniform(key_list[0], (ELEMS,), jnp.float32, -0.7, 0.7)
    element_scale = jnp.exp(sizes_log)
    spread = jax.random.uniform(key_list[1], (9, ELEMS), jnp.float32, -1.0, 1.0)
    identity_rows = jnp.eye(3, dtype=jnp.float32).reshape(9)
    inverse_jac = element_scale[None, :] * (identity_rows[:, None] + 0.25 * spread)
    permittivity = jax.random.uniform(key_list[3], (1, ELEMS), jnp.float32, 1.0, 4.0)
    permeability = jax.random.uniform(key_list[4], (1, ELEMS), jnp.float32, 0.8, 1.6)
    return jnp.concatenate([inverse_jac, permittivity, permeability], axis=0).astype(jnp.float32)


def shard_levels(key, dims, shards, least, top_value):
    def one(dim, blocks):
        steps = jax.random.uniform(jax.random.fold_in(jax.random.fold_in(key, 6), dim), (blocks,), jnp.float32, least / len(shards), top_value / len(shards))
        return jnp.repeat(jnp.exp(steps), dims[dim] // blocks).reshape((-1,) + (1,) * (len(dims) - dim - 1))

    level = one(*shards[0])
    for cut in shards[1:]:
        level = level * one(*cut)
    return level


def normal_values(own_key, shape, scale, limit, shards=(), kind=jnp.bfloat16):
    result = scale * jax.random.normal(own_key, shape, jnp.float32)
    if shards:
        result = result * shard_levels(own_key, shape, shards, -0.22, 0.18)
    return jnp.clip(result, -limit, limit).astype(kind)


def setup_inputs(seed: int = 0) -> dict:
    arg_keys = jax.random.split(jax.random.key(seed), 7)
    fields = normal_values(arg_keys[0], (FIELDS, NP, ELEMS), 1.0, 6.0, ((2, 512),), jnp.float32)
    geometry = draw_geometry(jax.random.fold_in(arg_keys[6], 71), 0)
    migrate_list = draw_migrate_list(jax.random.fold_in(arg_keys[6], 71), 0)
    trace_list = draw_trace_list(jax.random.fold_in(arg_keys[6], 71), 0)
    face_link = draw_face_link(jax.random.fold_in(arg_keys[6], 71), 0)
    face_orient = draw_face_orient(jax.random.fold_in(arg_keys[6], 71), 0)
    return {"fields": fields, "geometry": geometry, "migrate_list": migrate_list, "trace_list": trace_list, "face_link": face_link, "face_orient": face_orient}


time_step = 0.004
section_a2 = -0.4178904745
section_b1 = 0.1496590219993
section_b2 = 0.3792103129999
highest = lax.Precision.HIGHEST
coordinate_perms = ((0, 1, 2), (1, 2, 0), (2, 0, 1), (0, 2, 1), (2, 1, 0), (1, 0, 2))
reference_normals = ((0.0, 0.0, -1.0), (0.0, -1.0, 0.0), (1.0, 1.0, 1.0), (-1.0, 0.0, 0.0))

def volume_triples():
    result_list = []
    for first_idx in range(4):
        for second_idx in range(4 - first_idx):
            for third_idx in range(4 - first_idx - second_idx):
                result_list.append((first_idx, second_idx, third_idx))
    return result_list

def planar_pairs():
    result_list = []
    for first_idx in range(4):
        for second_idx in range(4 - first_idx):
            result_list.append((first_idx, second_idx))
    return result_list

def monomial_matrix(points, powers):
    result_rows = []
    for point_item in points:
        row_values = []
        for power_item in powers:
            product_value = 1.0
            for axis_id in range(len(power_item)):
                product_value = product_value * point_item[axis_id] ** power_item[axis_id]
            row_values.append(product_value)
        result_rows.append(row_values)
    return result_rows

def mat_mul(left_rows, right_rows):
    inner_count = len(right_rows)
    col_count = len(right_rows[0])
    return [[sum((left_row[k_id] * right_rows[k_id][c_id] for k_id in range(inner_count))) for c_id in range(col_count)] for left_row in left_rows]

def transposed(matrix_rows):
    return [list(row_item) for row_item in zip(*matrix_rows)]

def invert(matrix_rows):
    order = len(matrix_rows)
    work_rows = [list(matrix_rows[r_id]) + [1.0 if r_id == c_id else 0.0 for c_id in range(order)] for r_id in range(order)]
    for col_id in range(order):
        pivot_row = max(range(col_id, order), key=lambda r_id: abs(work_rows[r_id][col_id]))
        work_rows[col_id], work_rows[pivot_row] = (work_rows[pivot_row], work_rows[col_id])
        pivot_value = work_rows[col_id][col_id]
        work_rows[col_id] = [value / pivot_value for value in work_rows[col_id]]
        for r_id in range(order):
            if r_id != col_id:
                factor = work_rows[r_id][col_id]
                if factor != 0.0:
                    work_rows[r_id] = [work_rows[r_id][c_id] - factor * work_rows[col_id][c_id] for c_id in range(2 * order)]
    return [row_item[order:] for row_item in work_rows]

def moment_matrix(powers, extra_dim):
    total_terms = len(powers)
    result_matrix = [[0.0] * total_terms for _ in range(total_terms)]
    for row_id in range(total_terms):
        for col_id in range(total_terms):
            joined = [powers[row_id][a_id] + powers[col_id][a_id] for a_id in range(len(powers[row_id]))]
            numerator = 1.0
            for exponent in joined:
                numerator = numerator * math.factorial(exponent)
            result_matrix[row_id][col_id] = numerator / math.factorial(sum(joined) + extra_dim)
    return result_matrix

def dg_tables():
    triples = volume_triples()
    points = [tuple((value / 3.0 for value in triple)) for triple in triples]
    inverse = invert(monomial_matrix(points, triples))
    slopes = []
    for axis_id in range(3):
        lowered = [tuple((max(triple[a_id] - 1, 0) if a_id == axis_id else triple[a_id] for a_id in range(3))) for triple in triples]
        base_rows = monomial_matrix(points, lowered)
        slope_values = [[triples[c_id][axis_id] * base_rows[r_id][c_id] for c_id in range(20)] for r_id in range(20)]
        slopes.append(mat_mul(slope_values, inverse))
    volume_mass = mat_mul(mat_mul(transposed(inverse), moment_matrix(triples, 3)), inverse)
    planar = planar_pairs()
    face_points = [tuple((value / 3.0 for value in pair_item)) for pair_item in planar]
    face_inverse = invert(monomial_matrix(face_points, planar))
    face_mass = mat_mul(mat_mul(transposed(face_inverse), moment_matrix(planar, 2)), face_inverse)
    face_axes = ((0, 1), (0, 2), (0, 1), (1, 2))
    face_mask = [[0] * 10 for _ in range(4)]
    for face_id in range(4):
        for node_id, triple in enumerate(triples):
            on_face = (triple[2] == 0, triple[1] == 0, triple[0] + triple[1] + triple[2] == 3, triple[0] == 0)[face_id]
            if on_face:
                key_pair = (triple[face_axes[face_id][0]], triple[face_axes[face_id][1]])
                face_mask[face_id][planar.index(key_pair)] = node_id
    surface = [[0.0] * 40 for _ in range(20)]
    for face_id in range(4):
        for row_id in range(10):
            for col_id in range(10):
                surface[face_mask[face_id][row_id]][face_id * 10 + col_id] += face_mass[row_id][col_id]
    lifting = mat_mul(invert(volume_mass), surface)
    lift_alt = [[lifting[n_id][f_id * 10 + j_id] for j_id in range(10) for f_id in range(4)] for n_id in range(20)]
    node_perms = []
    for turn_id in range(6):
        perm_row = []
        for pair_item in planar:
            triple_face = (pair_item[0], pair_item[1], 3 - pair_item[0] - pair_item[1])
            moved_triple = [triple_face[coordinate_perms[turn_id][axis_id]] for axis_id in range(3)]
            perm_row.append(planar.index((moved_triple[0], moved_triple[1])))
        node_perms.append(perm_row)
    node_picks = [face_mask[f_id][j_id] for j_id in range(10) for f_id in range(4)]
    return (jnp.asarray(slopes, dtype=jnp.float32), jnp.asarray(lift_alt, dtype=jnp.float32), node_picks, node_perms)

def derive_geometry(raw_geometry):
    elements = raw_geometry.shape[1]
    inverse_jac = raw_geometry[:9].reshape(3, 3, elements)
    normal_table = jnp.asarray(reference_normals, dtype=jnp.float32)
    outward = jnp.einsum('fi,ijk->jfk', normal_table, inverse_jac, precision=highest)
    lengths = jnp.sqrt(lax.optimization_barrier(jnp.sum(outward * outward, axis=0)))
    unit_normals = outward / lengths[None]
    return jnp.concatenate([raw_geometry[:9], unit_normals.reshape(12, elements), lengths, raw_geometry[9:11]], axis=0)

def identity_geometry():
    return jnp.concatenate([jnp.eye(3, dtype=jnp.float32).reshape(9, 1), jnp.ones((2, 1), jnp.float32)], axis=0)

def cross_product(first_vec, second_vec):
    return jnp.stack([first_vec[1] * second_vec[2] - first_vec[2] * second_vec[1], first_vec[2] * second_vec[0] - first_vec[0] * second_vec[2], first_vec[0] * second_vec[1] - first_vec[1] * second_vec[0]])

def device_rhs(state, extended, link_codes, orient_codes, derived, tables):
    slopes, lift_alt, node_picks, node_perms = tables
    components = state.shape[0]
    elements = state.shape[2]
    face_nodes = len(node_perms[0])
    interior = extended[:, :, :4 * elements].reshape(components, face_nodes, 4, elements)
    gathered = extended[:, :, link_codes]
    picked = gathered
    for turn_id in range(6):
        picked = jnp.where((orient_codes == turn_id)[None, None], gathered[:, node_perms[turn_id]], picked)
    wall_signs = jnp.array([1.0, 1.0, 1.0, -1.0, -1.0, -1.0], jnp.float32)[:, None, None, None]
    outside = jnp.where((orient_codes == 6)[None, None], wall_signs * interior, picked)
    inverse_jac = derived[:9].reshape(3, 3, elements)
    normals = derived[9:21].reshape(3, 1, 4, elements)
    lengths = derived[21:25]
    permittivity = derived[25]
    permeability = derived[26]
    local_slopes = jnp.einsum('amn,fnk->afmk', slopes, state, precision=highest)
    gradients = [inverse_jac[0, axis_id][None, None] * local_slopes[0] + inverse_jac[1, axis_id][None, None] * local_slopes[1] + inverse_jac[2, axis_id][None, None] * local_slopes[2] for axis_id in range(3)]
    curl_h = jnp.stack([gradients[1][2] - gradients[2][1], gradients[2][0] - gradients[0][2], gradients[0][1] - gradients[1][0]])
    curl_e = jnp.stack([gradients[1][5] - gradients[2][4], gradients[2][3] - gradients[0][5], gradients[0][4] - gradients[1][3]])
    jump_all = outside - interior
    jump_h = jump_all[:3]
    jump_e = jump_all[3:]
    along_h = lax.optimization_barrier(jnp.sum(normals * jump_h, axis=0))
    along_e = lax.optimization_barrier(jnp.sum(normals * jump_e, axis=0))
    flux_h = -cross_product(normals, jump_e) + jump_h - normals * along_h
    flux_e = cross_product(normals, jump_h) + jump_e - normals * along_e
    scaled = jnp.concatenate([flux_h, flux_e], axis=0) * (0.5 * lengths)[None, None]
    lifted = jnp.einsum('nc,fck->fnk', lift_alt, scaled.reshape(components, 4 * face_nodes, elements), precision=highest)
    change_h = (lifted[:3] - curl_e) / permeability
    change_e = (curl_h + lifted[3:]) / permittivity
    return jnp.concatenate([change_h, change_e], axis=0)

def slab_rhs(states, derived, link_blocks, orient_blocks, trace_lists, tables):
    node_picks = tables[2]
    face_nodes = len(tables[3][0])
    sub_total = states.shape[0]
    components = states.shape[1]
    elements = states.shape[3]
    face_values = states[:, :, node_picks, :].reshape(sub_total, components, face_nodes, 4 * elements)

    def collect(target):
        chosen = trace_lists[:, target, :]
        pieces = jax.vmap(lambda table_one, select_one: table_one[:, :, select_one])(face_values, chosen)
        return pieces.transpose(1, 2, 0, 3).reshape(components, face_nodes, -1)
    incoming = jax.vmap(collect)(jnp.arange(sub_total, dtype=jnp.int32))
    extended = jnp.concatenate([face_values, incoming], axis=3)
    return jax.vmap(lambda one_state, one_ext, one_link, one_orient, one_geo: device_rhs(one_state, one_ext, one_link, one_orient, one_geo, tables))(states, extended, link_blocks, orient_blocks, derived)

def reference(fields, geometry, migrate_list, trace_list, face_link, face_orient):
    tables = dg_tables()
    components = fields.shape[0]
    node_count = fields.shape[1]
    field_rows = components * node_count
    payload = jnp.concatenate([fields.reshape(field_rows, -1), derive_geometry(geometry)], axis=0)
    fallback = jnp.concatenate([jnp.zeros((field_rows, 1), jnp.float32), derive_geometry(identity_geometry())], axis=0)
    send_lists = migrate_list.reshape(N_SLAB, N_SUB, N_SLAB, CAP)
    offsets = (jnp.arange(N_SLAB, dtype=jnp.int32)[:, None] * N_SUB + jnp.arange(N_SUB, dtype=jnp.int32)[None, :]) * ELEM_DEV
    link_blocks = face_link.reshape(4, N_SLAB, N_SUB, NEW_DEV).transpose(1, 2, 0, 3)
    orient_blocks = face_orient.reshape(4, N_SLAB, N_SUB, NEW_DEV).transpose(1, 2, 0, 3)
    trace_lists = trace_list.reshape(N_SLAB, N_SUB, N_SUB, TCAP)

    def one_slab(slab_id):
        chosen_slots = send_lists[:, :, slab_id, :]
        columns = (offsets[:, :, None] + jnp.maximum(chosen_slots, 0)).transpose(1, 0, 2).reshape(-1).astype(jnp.int32)
        filled = (chosen_slots >= 0).transpose(1, 0, 2).reshape(-1)
        moved_rows = jnp.where(filled[None], jnp.take(payload, columns, axis=1), fallback)
        blocks = moved_rows.reshape(moved_rows.shape[0], N_SUB, NEW_DEV).transpose(1, 0, 2)
        states = blocks[:, :field_rows].reshape(N_SUB, components, node_count, NEW_DEV)
        derived = blocks[:, field_rows:]
        link_here = link_blocks[slab_id]
        orient_here = orient_blocks[slab_id]
        list_here = trace_lists[slab_id]
        first_res = time_step * slab_rhs(states, derived, link_here, orient_here, list_here, tables)
        middle = states + section_b1 * first_res
        second_res = section_a2 * first_res + time_step * slab_rhs(middle, derived, link_here, orient_here, list_here, tables)
        return (middle + section_b2 * second_res, second_res)
    advanced, residual = lax.map(one_slab, jnp.arange(N_SLAB, dtype=jnp.int32))
    advanced = advanced.transpose(2, 3, 0, 1, 4).reshape(components, node_count, -1)
    residual = residual.transpose(2, 3, 0, 1, 4).reshape(components, node_count, -1)
    return (advanced, residual)
```

```python
import math

import jax
import jax.numpy as jnp
import ml_dtypes
import numpy as np
from jax import lax
from jax.experimental import pallas as pl
from jax.experimental.pallas import tpu as pltpu
from jax.sharding import PartitionSpec as P

time_step = 0.004
section_a2 = -0.4178904745
section_b1 = 0.1496590219993
section_b2 = 0.3792103129999
coordinate_perms = ((0, 1, 2), (1, 2, 0), (2, 0, 1), (0, 2, 1), (2, 1, 0), (1, 0, 2))
components = 6
node_count = 20
face_nodes = 10
faces = 4
old_count = 256
slots = 12
slabs = 32
subs = 16
traces = 16
new_count = slots * slabs
column_count = faces * new_count
remote_count = subs * traces
lane = 128
tiles = new_count // lane
block_rows = slots + 1


def volume_triples():
    result_list = []
    for first_idx in range(4):
        for second_idx in range(4 - first_idx):
            for third_idx in range(4 - first_idx - second_idx):
                result_list.append((first_idx, second_idx, third_idx))
    return result_list


def planar_pairs():
    result_list = []
    for first_idx in range(4):
        for second_idx in range(4 - first_idx):
            result_list.append((first_idx, second_idx))
    return result_list


def monomial_matrix(points, powers):
    result_rows = []
    for point_item in points:
        row_values = []
        for power_item in powers:
            product_value = 1.0
            for axis_id in range(len(power_item)):
                product_value = product_value * point_item[axis_id] ** power_item[axis_id]
            row_values.append(product_value)
        result_rows.append(row_values)
    return result_rows


def mat_mul(left_rows, right_rows):
    inner_count = len(right_rows)
    col_count = len(right_rows[0])
    return [
        [
            sum((left_row[k_id] * right_rows[k_id][c_id] for k_id in range(inner_count)))
            for c_id in range(col_count)
        ]
        for left_row in left_rows
    ]


def transposed(matrix_rows):
    return [list(row_item) for row_item in zip(*matrix_rows)]


def invert(matrix_rows):
    order = len(matrix_rows)
    work_rows = [
        list(matrix_rows[r_id]) + [1.0 if r_id == c_id else 0.0 for c_id in range(order)]
        for r_id in range(order)
    ]
    for col_id in range(order):
        pivot_row = max(range(col_id, order), key=lambda r_id: abs(work_rows[r_id][col_id]))
        work_rows[col_id], work_rows[pivot_row] = (work_rows[pivot_row], work_rows[col_id])
        pivot_value = work_rows[col_id][col_id]
        work_rows[col_id] = [value / pivot_value for value in work_rows[col_id]]
        for r_id in range(order):
            if r_id != col_id:
                factor = work_rows[r_id][col_id]
                if factor != 0.0:
                    work_rows[r_id] = [
                        work_rows[r_id][c_id] - factor * work_rows[col_id][c_id]
                        for c_id in range(2 * order)
                    ]
    return [row_item[order:] for row_item in work_rows]


def moment_matrix(powers, extra_dim):
    total_terms = len(powers)
    result_matrix = [[0.0] * total_terms for _ in range(total_terms)]
    for row_id in range(total_terms):
        for col_id in range(total_terms):
            joined = [
                powers[row_id][a_id] + powers[col_id][a_id] for a_id in range(len(powers[row_id]))
            ]
            numerator = 1.0
            for exponent in joined:
                numerator = numerator * math.factorial(exponent)
            result_matrix[row_id][col_id] = numerator / math.factorial(sum(joined) + extra_dim)
    return result_matrix


def dg_tables():
    triples = volume_triples()
    points = [tuple((value / 3.0 for value in triple)) for triple in triples]
    inverse = invert(monomial_matrix(points, triples))
    slopes = []
    for axis_id in range(3):
        lowered = [
            tuple(
                (max(triple[a_id] - 1, 0) if a_id == axis_id else triple[a_id] for a_id in range(3))
            )
            for triple in triples
        ]
        base_rows = monomial_matrix(points, lowered)
        slope_values = [
            [triples[c_id][axis_id] * base_rows[r_id][c_id] for c_id in range(20)]
            for r_id in range(20)
        ]
        slopes.append(mat_mul(slope_values, inverse))
    volume_mass = mat_mul(mat_mul(transposed(inverse), moment_matrix(triples, 3)), inverse)
    planar = planar_pairs()
    face_points = [tuple((value / 3.0 for value in pair_item)) for pair_item in planar]
    face_inverse = invert(monomial_matrix(face_points, planar))
    face_mass = mat_mul(mat_mul(transposed(face_inverse), moment_matrix(planar, 2)), face_inverse)
    face_axes = ((0, 1), (0, 2), (0, 1), (1, 2))
    face_mask = [[0] * 10 for _ in range(4)]
    for face_id in range(4):
        for node_id, triple in enumerate(triples):
            on_face = (
                triple[2] == 0,
                triple[1] == 0,
                triple[0] + triple[1] + triple[2] == 3,
                triple[0] == 0,
            )[face_id]
            if on_face:
                key_pair = (triple[face_axes[face_id][0]], triple[face_axes[face_id][1]])
                face_mask[face_id][planar.index(key_pair)] = node_id
    surface = [[0.0] * 40 for _ in range(20)]
    for face_id in range(4):
        for row_id in range(10):
            for col_id in range(10):
                surface[face_mask[face_id][row_id]][face_id * 10 + col_id] += face_mass[row_id][
                    col_id
                ]
    lifting = mat_mul(invert(volume_mass), surface)
    lift_alt = [
        [lifting[n_id][f_id * 10 + j_id] for j_id in range(10) for f_id in range(4)]
        for n_id in range(20)
    ]
    node_perms = []
    for turn_id in range(6):
        perm_row = []
        for pair_item in planar:
            triple_face = (pair_item[0], pair_item[1], 3 - pair_item[0] - pair_item[1])
            moved_triple = [triple_face[coordinate_perms[turn_id][axis_id]] for axis_id in range(3)]
            perm_row.append(planar.index((moved_triple[0], moved_triple[1])))
        node_perms.append(perm_row)
    node_picks = [face_mask[f_id][j_id] for j_id in range(10) for f_id in range(4)]
    return slopes, lifting, face_mask, node_perms


def bf16_pair(matrix):
    wide = np.asarray(matrix, np.float32)
    high = wide.astype(ml_dtypes.bfloat16)
    rest = (wide - high.astype(np.float32)).astype(ml_dtypes.bfloat16)
    return high, rest


slope_table, lift_table, face_mask, node_perms = dg_tables()


def slope_operand():
    stacked = np.zeros((80, 32), np.float64)
    for axis_id in range(3):
        first_row = axis_id * 24
        stacked[first_row : first_row + node_count, :node_count] = slope_table[axis_id]
    high, rest = bf16_pair(stacked)
    return jnp.asarray(np.concatenate([high, high, rest], axis=1))


def lift_operand():
    stacked = np.zeros((32, 48), np.float64)
    for face_id in range(faces):
        for node_id in range(face_nodes):
            for row_id in range(node_count):
                stacked[row_id, node_id * faces + face_id] = lift_table[row_id][
                    face_id * face_nodes + node_id
                ]
    high, rest = bf16_pair(stacked)
    return jnp.asarray(np.concatenate([high, high, rest], axis=1))


def select_operand():
    table = np.zeros((2, faces * 2 * lane, lane), np.float32)
    for half in range(2):
        for face_id in range(faces):
            for part_id in range(2):
                for node_id in range(face_nodes):
                    for comp_id in range(components):
                        row_id = (face_id * 2 + part_id) * lane
                        row_id += comp_id * node_count + face_mask[face_id][node_id]
                        table[half, row_id, half * 64 + node_id * components + comp_id] = 1.0
    return jnp.asarray(table.astype(ml_dtypes.bfloat16))


def split_two(value):
    high = value.astype(jnp.bfloat16)
    rest = (value - high.astype(jnp.float32)).astype(jnp.bfloat16)
    return high, rest


def split_three(value):
    high = value.astype(jnp.bfloat16)
    left = value - high.astype(jnp.float32)
    middle = left.astype(jnp.bfloat16)
    rest = (left - middle.astype(jnp.float32)).astype(jnp.bfloat16)
    return high, middle, rest


def dot_rows(left, right):
    return lax.dot_general(
        left, right, (((1,), (0,)), ((), ())), preferred_element_type=jnp.float32
    )


def dot_lanes(left, right):
    return lax.dot_general(
        left, right, (((1,), (1,)), ((), ())), preferred_element_type=jnp.float32
    )


def one_hot(mask):
    return jnp.where(mask, 1.0, 0.0).astype(jnp.bfloat16)


def face_of(codes):
    return sum((codes >= step * new_count).astype(jnp.int32) for step in range(1, faces))


def pack_kernel(fields_ref, geometry_ref, list_ref, out_ref, held_ref):
    field_rows = components * node_count
    for comp_id in range(components):
        held_ref[comp_id * node_count : (comp_id + 1) * node_count, :] = fields_ref[comp_id]
    held_ref[field_rows : field_rows + 11, :] = geometry_ref[...]
    held_ref[field_rows + 11 :, :] = jnp.zeros((13, old_count), jnp.float32)
    parts = jnp.concatenate(split_three(held_ref[...]), axis=1)
    parts = jnp.concatenate([parts, jnp.zeros((112, 3 * old_count), jnp.bfloat16)], axis=0)
    codes = list_ref[0]
    lanes = lax.broadcasted_iota(jnp.int32, (slabs, old_count), 1)
    picks = jnp.concatenate(
        [one_hot(codes[:, slot_id : slot_id + 1] == lanes) for slot_id in range(slots)], axis=0
    )
    moved = dot_lanes(jnp.concatenate([picks, picks, picks], axis=1), parts)
    short = lax.broadcasted_iota(jnp.int32, (slabs, lane), 1)
    diagonal = (short == field_rows) | (short == field_rows + 4)
    tail = jnp.zeros((slabs, lane), jnp.float32)
    for slot_id in range(slots):
        empty = codes[:, slot_id : slot_id + 1] < 0
        block = moved[slot_id * slabs : (slot_id + 1) * slabs]
        out_ref[pl.ds(slot_id, slabs, stride=block_rows), :] = jnp.where(
            empty & diagonal, 1.0, block[:, :lane]
        )
        ending = jnp.where(empty & (short < 3), 1.0, block[:, lane:])
        if slot_id:
            ending = pltpu.roll(ending, 3 * slot_id, 1)
        tail = tail + ending
    out_ref[pl.ds(slots, slabs, stride=block_rows), :] = tail


def trace_rows(values, codes, select_ref, trace_ref):
    high, rest = split_two(values)
    face = face_of(codes)
    element = codes - new_count * face
    lanes = lax.broadcasted_iota(jnp.int32, (subs, new_count), 1)
    picks = jnp.concatenate(
        [one_hot(element[:, idx : idx + 1] == lanes) for idx in range(traces)], axis=0
    )
    found = dot_lanes(picks, jnp.concatenate([high, rest], axis=0)).astype(jnp.bfloat16)
    face_rows = jnp.concatenate(
        [
            jnp.broadcast_to(face[:, idx : idx + 1], (subs, 2 * lane))
            for idx in range(traces)
        ],
        axis=0,
    )
    zeros = jnp.zeros(found.shape, jnp.float32)
    wide = found.astype(jnp.float32)
    spread = jnp.concatenate(
        [
            jnp.where(face_rows == face_id, wide, zeros).astype(jnp.bfloat16)
            for face_id in range(faces)
        ],
        axis=1,
    )
    half = remote_count // 2
    rows = dot_rows(spread[:half], select_ref[0]) + dot_rows(spread[half:], select_ref[1])
    for idx in range(traces // 2):
        trace_ref[pl.ds(idx, subs, stride=traces // 2), :] = rows[idx * subs : (idx + 1) * subs]


def unpack_kernel(
    came_ref, list_ref, select_ref, state_ref, derived_ref, trace_ref, rows_ref, tail_ref, main_ref
):
    field_rows = components * node_count
    tail = came_ref[pl.ds(slots, slabs, stride=block_rows), :]
    for slot_id in range(slots):
        rows_ref[pl.ds(slot_id, slabs, stride=slots), :] = came_ref[
            pl.ds(slot_id, slabs, stride=block_rows), :
        ]
        shifted = pltpu.roll(tail, lane - 3 * slot_id, 1) if slot_id else tail
        tail_ref[pl.ds(slot_id, slabs, stride=slots), :] = shifted
    main = jnp.transpose(rows_ref[...])
    trace_rows(main, list_ref[0], select_ref, trace_ref)
    main_ref[...] = main
    extra = jnp.transpose(tail_ref[...])[:8]
    for comp_id in range(components):
        state_ref[comp_id] = main_ref[comp_id * node_count : (comp_id + 1) * node_count, :]
    geo = [main_ref[field_rows + row_id : field_rows + row_id + 1, :] for row_id in range(8)]
    geo.append(extra[0:1])
    derived_ref[0:8, :] = main_ref[field_rows : field_rows + 8, :]
    derived_ref[8:9, :] = extra[0:1]
    derived_ref[9:10, :] = 1.0 / extra[1:2]
    derived_ref[10:11, :] = 1.0 / extra[2:3]
    total = None
    for axis_id in range(3):
        first, second, third = geo[axis_id], geo[3 + axis_id], geo[6 + axis_id]
        normal = 0.5 * jnp.concatenate([-third, -second, first + second + third, -first], axis=0)
        square = normal * normal
        total = square if total is None else total + square
        normal_rows = jnp.concatenate([normal, normal], axis=0)
        derived_ref[16 + 8 * axis_id : 24 + 8 * axis_id, :] = normal_rows
    length = jnp.sqrt(total)
    derived_ref[40:48, :] = jnp.concatenate([length, length], axis=0)
    inverse = 1.0 / length
    derived_ref[48:56, :] = jnp.concatenate([inverse, inverse], axis=0)


def oriented(planes, orient):
    masks = [orient == turn_id for turn_id in range(6)]
    result = []
    for node_id in range(face_nodes):
        sources = {}
        for turn_id in range(6):
            sources.setdefault(node_perms[turn_id][node_id], []).append(turn_id)
        value = None
        for source, turn_ids in sources.items():
            if value is None:
                value = planes[source]
                continue
            mask = masks[turn_ids[0]]
            for turn_id in turn_ids[1:]:
                mask = mask | masks[turn_id]
            value = jnp.where(mask, planes[source], value)
        result.append(value)
    return result


def lifted_flux(jump_ref, flux_ref, derived_ref, lift_ref):
    groups = faces * face_nodes // 8

    def jump_of(comp_id):
        rows = strided_load(jump_ref, comp_id, faces * face_nodes, 8)
        return rows.reshape(groups, 8, new_count)

    jump_h = [jump_of(comp_id) for comp_id in range(3)]
    jump_e = [jump_of(comp_id) for comp_id in range(3, 6)]
    normal = [derived_ref[16 + 8 * axis_id : 24 + 8 * axis_id, :][None] for axis_id in range(3)]
    length = derived_ref[40:48, :][None]
    inverse = derived_ref[48:56, :][None]

    def along(jump):
        total = normal[0] * jump[0] + normal[1] * jump[1] + normal[2] * jump[2]
        return total * inverse

    along_h = along(jump_h)
    along_e = along(jump_e)
    for axis_id in range(3):
        after, last = (axis_id + 1) % 3, (axis_id + 2) % 3
        cross_e = normal[after] * jump_e[last] - normal[last] * jump_e[after]
        cross_h = normal[after] * jump_h[last] - normal[last] * jump_h[after]
        flux_h = length * jump_h[axis_id] - normal[axis_id] * along_h - cross_e
        flux_e = length * jump_e[axis_id] - normal[axis_id] * along_e + cross_h
        for comp_id, value in ((axis_id, flux_h), (3 + axis_id, flux_e)):
            flux_ref[0:40, comp_id * new_count : (comp_id + 1) * new_count] = value.reshape(
                faces * face_nodes, new_count
            )
    flux_ref[40:48, :] = jnp.zeros((8, components * new_count), jnp.float32)
    high, rest = split_two(flux_ref[...])
    return dot_rows(lift_ref[...], jnp.concatenate([high, rest, high], axis=0))


def strided_load(ref, start, size, stride):
    return jnp.concatenate(
        [ref[tile, pl.ds(start, size, stride=stride), :] for tile in range(tiles)], axis=1
    )


def tiled_store(ref, rows, value):
    for tile in range(tiles):
        ref[tile, rows, :] = value[:, tile * lane : (tile + 1) * lane]


def tiled_load(ref, rows):
    return jnp.concatenate([ref[tile, rows, :] for tile in range(tiles)], axis=1)


def column_block(matrix, comp_id):
    return matrix[:24, comp_id * new_count : (comp_id + 1) * new_count]


def local_kernel(
    state_ref,
    derived_ref,
    link_ref,
    orient_ref,
    slope_ref,
    lift_ref,
    part_ref,
    nodes_ref,
    flat_ref,
    jump_ref,
    flux_ref,
):
    nodes_ref[...] = jnp.zeros(nodes_ref.shape, jnp.float32)
    flat_ref[node_count:32, :] = jnp.zeros((12, components * new_count), jnp.float32)
    for comp_id in range(components):
        current = state_ref[comp_id]
        tiled_store(nodes_ref, pl.ds(comp_id, node_count, stride=8), current)
        flat_ref[0:node_count, comp_id * new_count : (comp_id + 1) * new_count] = current
    stacked = jnp.concatenate(split_two(tiled_load(nodes_ref, slice(None))), axis=0)
    rows = lax.broadcasted_iota(jnp.int32, (new_count, new_count), 0)
    comp_rows = lax.broadcasted_iota(jnp.int32, (8, new_count), 0)
    wall_gain = jnp.where(comp_rows >= 3, -2.0, 0.0)
    for face_id in range(faces):
        link = link_ref[face_id : face_id + 1, :]
        orient = orient_ref[face_id : face_id + 1, :]
        owner = face_of(link)
        element = jnp.where(link < column_count, link - new_count * owner, -1)
        found = dot_rows(stacked, one_hot(rows == element))
        found = found[: 8 * node_count] + found[8 * node_count :]
        owner_masks = [owner == other for other in range(faces)]
        planes = []
        for node_id in range(face_nodes):
            value = None
            for other in range(faces):
                first_row = 8 * face_mask[other][node_id]
                plane = found[first_row : first_row + 8]
                value = plane if value is None else jnp.where(owner_masks[other], plane, value)
            planes.append(value)
        outside = oriented(planes, orient)
        wall = orient == 6
        for node_id in range(face_nodes):
            first_row = 8 * face_mask[face_id][node_id]
            inside = tiled_load(nodes_ref, slice(first_row, first_row + 8))
            jump = jnp.where(wall, wall_gain * inside, outside[node_id] - inside)
            target = 8 * (node_id * faces + face_id)
            tiled_store(jump_ref, slice(target, target + 8), jump)
    lifted = lifted_flux(jump_ref, flux_ref, derived_ref, lift_ref)
    high, rest = split_two(flat_ref[...])
    slopes = dot_rows(slope_ref[...], jnp.concatenate([high, rest, high], axis=0))
    inverse_jac = [
        [derived_ref[3 * row_id + axis_id : 3 * row_id + axis_id + 1, :] for axis_id in range(3)]
        for row_id in range(3)
    ]

    def gradient(axis_id, comp_id):
        columns = slice(comp_id * new_count, (comp_id + 1) * new_count)
        return (
            inverse_jac[0][axis_id] * slopes[0:24, columns]
            + inverse_jac[1][axis_id] * slopes[24:48, columns]
            + inverse_jac[2][axis_id] * slopes[48:72, columns]
        )

    inverse_eps = derived_ref[9:10, :]
    inverse_mu = derived_ref[10:11, :]
    for axis_id in range(3):
        after, last = (axis_id + 1) % 3, (axis_id + 2) % 3
        curl_h = gradient(after, last) - gradient(last, after)
        curl_e = gradient(after, 3 + last) - gradient(last, 3 + after)
        change_h = (column_block(lifted, axis_id) - curl_e) * inverse_mu
        change_e = (column_block(lifted, 3 + axis_id) + curl_h) * inverse_eps
        part_ref[axis_id] = change_h[:node_count]
        part_ref[3 + axis_id] = change_e[:node_count]


def remote_part(came_ref, link_ref, orient_ref, derived_ref, lift_ref, turned_ref, table_ref, jump_ref, flux_ref):
    turned_ref[...] = jnp.transpose(came_ref[...])
    table_ref[...] = jnp.zeros(table_ref.shape, jnp.float32)
    for half in range(2):
        for node_id in range(face_nodes):
            first_row = half * 64 + node_id * components
            table_ref[8 * node_id : 8 * node_id + components, half * lane : (half + 1) * lane] = (
                turned_ref[first_row : first_row + components, :]
            )
    stacked = jnp.concatenate(split_two(table_ref[...]), axis=0)
    rows = lax.broadcasted_iota(jnp.int32, (remote_count, new_count), 0)
    for face_id in range(faces):
        far = link_ref[face_id : face_id + 1, :] - column_count
        orient = orient_ref[face_id : face_id + 1, :]
        column = ((far >> 3) & 1) * lane + (far >> 4) * 8 + (far & 7)
        column = jnp.where((far >= 0) & (orient < 6), column, -1)
        found = dot_rows(stacked, one_hot(rows == column))
        found = found[: 8 * face_nodes] + found[8 * face_nodes :]
        planes = [found[8 * node_id : 8 * node_id + 8] for node_id in range(face_nodes)]
        outside = oriented(planes, orient)
        for node_id in range(face_nodes):
            target = 8 * (node_id * faces + face_id)
            tiled_store(jump_ref, slice(target, target + 8), outside[node_id])
    lifted = lifted_flux(jump_ref, flux_ref, derived_ref, lift_ref)
    inverse_eps = derived_ref[9:10, :]
    inverse_mu = derived_ref[10:11, :]
    changes = []
    for comp_id in range(components):
        scale = inverse_mu if comp_id < 3 else inverse_eps
        changes.append((column_block(lifted, comp_id) * scale)[:node_count])
    return changes


def first_kernel(
    came_ref,
    part_ref,
    state_ref,
    derived_ref,
    link_ref,
    orient_ref,
    lift_ref,
    list_ref,
    select_ref,
    residual_ref,
    middle_ref,
    trace_ref,
    turned_ref,
    table_ref,
    jump_ref,
    flux_ref,
    main_ref,
):
    changes = remote_part(
        came_ref, link_ref, orient_ref, derived_ref, lift_ref, turned_ref, table_ref, jump_ref, flux_ref
    )
    for comp_id in range(components):
        residual = time_step * (part_ref[comp_id] + changes[comp_id])
        middle = state_ref[comp_id] + section_b1 * residual
        residual_ref[comp_id] = residual
        middle_ref[comp_id] = middle
        main_ref[comp_id * node_count : (comp_id + 1) * node_count, :] = middle
    main_ref[components * node_count :, :] = jnp.zeros((8, new_count), jnp.float32)
    trace_rows(main_ref[...], list_ref[0], select_ref, trace_ref)


def second_kernel(
    came_ref,
    part_ref,
    middle_ref,
    first_ref,
    derived_ref,
    link_ref,
    orient_ref,
    lift_ref,
    advanced_ref,
    residual_ref,
    turned_ref,
    table_ref,
    jump_ref,
    flux_ref,
):
    changes = remote_part(
        came_ref, link_ref, orient_ref, derived_ref, lift_ref, turned_ref, table_ref, jump_ref, flux_ref
    )
    for comp_id in range(components):
        residual = section_a2 * first_ref[comp_id] + time_step * (
            part_ref[comp_id] + changes[comp_id]
        )
        residual_ref[comp_id] = residual
        advanced_ref[comp_id] = middle_ref[comp_id] + section_b2 * residual


def floats(*shape):
    return jax.ShapeDtypeStruct(shape, jnp.float32)


def scratch(*shape):
    return pltpu.VMEM(shape, jnp.float32)


def run(kernel, name, outs, scratches, operands, flops=10**8):
    return pl.pallas_call(
        kernel,
        name=name,
        out_shape=outs,
        scratch_shapes=scratches,
        compiler_params=pltpu.CompilerParams(vmem_limit_bytes=24 * 2**20),
        cost_estimate=pl.CostEstimate(flops=flops, bytes_accessed=10**6, transcendentals=0),
    )(*operands)


def shards(fields, geometry, migrate_list, trace_list, face_link, face_orient):
    slopes = slope_operand()
    lift = lift_operand()
    select = select_operand()
    state_shape = floats(components, node_count, new_count)
    trace_shape = floats(subs * traces // 2, lane)
    remote_scratch = [
        scratch(lane, lane),
        scratch(8 * face_nodes, remote_count),
        scratch(tiles, 8 * faces * face_nodes, lane),
        scratch(48, components * new_count),
    ]
    parcel = run(
        pack_kernel,
        "pack",
        floats(slabs * block_rows, lane),
        [scratch(144, old_count)],
        (fields, geometry, migrate_list),
    )
    arrived = lax.all_to_all(
        parcel.reshape(slabs, block_rows * lane), "slab", split_axis=0, concat_axis=0, tiled=True
    ).reshape(slabs * block_rows, lane)
    state, derived, outgoing = run(
        unpack_kernel,
        "unpack",
        (state_shape, floats(64, new_count), trace_shape),
        [scratch(new_count, lane), scratch(new_count, lane), scratch(lane, new_count)],
        (arrived, trace_list, select),
    )

    def local(current):
        return run(
            local_kernel,
            "local",
            state_shape,
            [
                scratch(tiles, 8 * node_count, lane),
                scratch(32, components * new_count),
                scratch(tiles, 8 * faces * face_nodes, lane),
                scratch(48, components * new_count),
            ],
            (current, derived, face_link, face_orient, slopes, lift),
        )

    def exchange(rows):
        blocks = rows.reshape(subs, traces // 2, lane)
        came = lax.all_to_all(blocks, "sub", split_axis=0, concat_axis=0, tiled=True)
        return came.reshape(subs * traces // 2, lane)

    incoming = exchange(outgoing)
    part = local(state)
    first_res, middle, outgoing = run(
        first_kernel,
        "first",
        (state_shape, state_shape, trace_shape),
        remote_scratch + [scratch(lane, new_count)],
        (incoming, part, state, derived, face_link, face_orient, lift, trace_list, select),
    )
    incoming = exchange(outgoing)
    part = local(middle)
    return run(
        second_kernel,
        "second",
        (state_shape, state_shape),
        remote_scratch,
        (incoming, part, middle, first_res, derived, face_link, face_orient, lift),
    )


def solution(mesh):
    return jax.shard_map(
        shards,
        mesh=mesh,
        in_specs=(
            P(None, None, ("slab", "sub")),
            P(None, ("slab", "sub")),
            P(("slab", "sub"), None, None),
            P(("slab", "sub"), None, None),
            P(None, ("slab", "sub")),
            P(None, ("slab", "sub")),
        ),
        out_specs=(P(None, None, ("slab", "sub")), P(None, None, ("slab", "sub"))),
        check_vma=False,
    )
```

```python
import math

import jax
import jax.numpy as jnp
import ml_dtypes
import numpy as np
from jax import lax
from jax.experimental import pallas as pl
from jax.experimental.pallas import tpu as pltpu
from jax.sharding import PartitionSpec as P

time_step = 0.004
section_a2 = -0.4178904745
section_b1 = 0.1496590219993
section_b2 = 0.3792103129999
coordinate_perms = ((0, 1, 2), (1, 2, 0), (2, 0, 1), (0, 2, 1), (2, 1, 0), (1, 0, 2))
components = 6
node_count = 20
face_nodes = 10
faces = 4
old_count = 256
slots = 12
slabs = 32
subs = 16
traces = 16
new_count = slots * slabs
column_count = faces * new_count
remote_count = subs * traces
lane = 128
half_lane = lane // 2
tiles = new_count // lane
block_rows = slots + 1


def volume_triples():
    result_list = []
    for first_idx in range(4):
        for second_idx in range(4 - first_idx):
            for third_idx in range(4 - first_idx - second_idx):
                result_list.append((first_idx, second_idx, third_idx))
    return result_list


def planar_pairs():
    result_list = []
    for first_idx in range(4):
        for second_idx in range(4 - first_idx):
            result_list.append((first_idx, second_idx))
    return result_list


def monomial_matrix(points, powers):
    result_rows = []
    for point_item in points:
        row_values = []
        for power_item in powers:
            product_value = 1.0
            for axis_id in range(len(power_item)):
                product_value = product_value * point_item[axis_id] ** power_item[axis_id]
            row_values.append(product_value)
        result_rows.append(row_values)
    return result_rows


def mat_mul(left_rows, right_rows):
    inner_count = len(right_rows)
    col_count = len(right_rows[0])
    return [
        [
            sum((left_row[k_id] * right_rows[k_id][c_id] for k_id in range(inner_count)))
            for c_id in range(col_count)
        ]
        for left_row in left_rows
    ]


def transposed(matrix_rows):
    return [list(row_item) for row_item in zip(*matrix_rows)]


def invert(matrix_rows):
    order = len(matrix_rows)
    work_rows = [
        list(matrix_rows[r_id]) + [1.0 if r_id == c_id else 0.0 for c_id in range(order)]
        for r_id in range(order)
    ]
    for col_id in range(order):
        pivot_row = max(range(col_id, order), key=lambda r_id: abs(work_rows[r_id][col_id]))
        work_rows[col_id], work_rows[pivot_row] = (work_rows[pivot_row], work_rows[col_id])
        pivot_value = work_rows[col_id][col_id]
        work_rows[col_id] = [value / pivot_value for value in work_rows[col_id]]
        for r_id in range(order):
            if r_id != col_id:
                factor = work_rows[r_id][col_id]
                if factor != 0.0:
                    work_rows[r_id] = [
                        work_rows[r_id][c_id] - factor * work_rows[col_id][c_id]
                        for c_id in range(2 * order)
                    ]
    return [row_item[order:] for row_item in work_rows]


def moment_matrix(powers, extra_dim):
    total_terms = len(powers)
    result_matrix = [[0.0] * total_terms for _ in range(total_terms)]
    for row_id in range(total_terms):
        for col_id in range(total_terms):
            joined = [
                powers[row_id][a_id] + powers[col_id][a_id] for a_id in range(len(powers[row_id]))
            ]
            numerator = 1.0
            for exponent in joined:
                numerator = numerator * math.factorial(exponent)
            result_matrix[row_id][col_id] = numerator / math.factorial(sum(joined) + extra_dim)
    return result_matrix


def dg_tables():
    triples = volume_triples()
    points = [tuple((value / 3.0 for value in triple)) for triple in triples]
    inverse = invert(monomial_matrix(points, triples))
    slopes = []
    for axis_id in range(3):
        lowered = [
            tuple(
                (max(triple[a_id] - 1, 0) if a_id == axis_id else triple[a_id] for a_id in range(3))
            )
            for triple in triples
        ]
        base_rows = monomial_matrix(points, lowered)
        slope_values = [
            [triples[c_id][axis_id] * base_rows[r_id][c_id] for c_id in range(20)]
            for r_id in range(20)
        ]
        slopes.append(mat_mul(slope_values, inverse))
    volume_mass = mat_mul(mat_mul(transposed(inverse), moment_matrix(triples, 3)), inverse)
    planar = planar_pairs()
    face_points = [tuple((value / 3.0 for value in pair_item)) for pair_item in planar]
    face_inverse = invert(monomial_matrix(face_points, planar))
    face_mass = mat_mul(mat_mul(transposed(face_inverse), moment_matrix(planar, 2)), face_inverse)
    face_axes = ((0, 1), (0, 2), (0, 1), (1, 2))
    face_mask = [[0] * 10 for _ in range(4)]
    for face_id in range(4):
        for node_id, triple in enumerate(triples):
            on_face = (
                triple[2] == 0,
                triple[1] == 0,
                triple[0] + triple[1] + triple[2] == 3,
                triple[0] == 0,
            )[face_id]
            if on_face:
                key_pair = (triple[face_axes[face_id][0]], triple[face_axes[face_id][1]])
                face_mask[face_id][planar.index(key_pair)] = node_id
    surface = [[0.0] * 40 for _ in range(20)]
    for face_id in range(4):
        for row_id in range(10):
            for col_id in range(10):
                surface[face_mask[face_id][row_id]][face_id * 10 + col_id] += face_mass[row_id][
                    col_id
                ]
    lifting = mat_mul(invert(volume_mass), surface)
    lift_alt = [
        [lifting[n_id][f_id * 10 + j_id] for j_id in range(10) for f_id in range(4)]
        for n_id in range(20)
    ]
    node_perms = []
    for turn_id in range(6):
        perm_row = []
        for pair_item in planar:
            triple_face = (pair_item[0], pair_item[1], 3 - pair_item[0] - pair_item[1])
            moved_triple = [triple_face[coordinate_perms[turn_id][axis_id]] for axis_id in range(3)]
            perm_row.append(planar.index((moved_triple[0], moved_triple[1])))
        node_perms.append(perm_row)
    node_picks = [face_mask[f_id][j_id] for j_id in range(10) for f_id in range(4)]
    return slopes, lifting, face_mask, node_perms


def bf16_pair(matrix):
    wide = np.asarray(matrix, np.float32)
    high = wide.astype(ml_dtypes.bfloat16)
    rest = (wide - high.astype(np.float32)).astype(ml_dtypes.bfloat16)
    return high, rest


slope_table, lift_table, face_mask, node_perms = dg_tables()


def slope_operand():
    stacked = np.zeros((80, 32), np.float64)
    for axis_id in range(3):
        first_row = axis_id * 24
        stacked[first_row : first_row + node_count, :node_count] = slope_table[axis_id]
    high, rest = bf16_pair(stacked)
    return jnp.asarray(np.concatenate([high, high, rest], axis=1))


def lift_operand():
    stacked = np.zeros((32, 48), np.float64)
    for face_id in range(faces):
        for node_id in range(face_nodes):
            for row_id in range(node_count):
                stacked[row_id, node_id * faces + face_id] = lift_table[row_id][
                    face_id * face_nodes + node_id
                ]
    high, rest = bf16_pair(stacked)
    return jnp.asarray(np.concatenate([high, high, rest], axis=1))


def remote_lift_operand():
    stacked = np.zeros((32, 16 * faces), np.float64)
    for face_id in range(faces):
        for node_id in range(face_nodes):
            for row_id in range(node_count):
                stacked[row_id, face_id * 16 + node_id] = lift_table[row_id][
                    face_id * face_nodes + node_id
                ]
    high, rest = bf16_pair(stacked)
    return jnp.asarray(np.concatenate([high, high, rest], axis=1))


def select_operand():
    table = np.zeros((2 * lane, faces * half_lane), np.float32)
    for face_id in range(faces):
        for part_id in range(2):
            for node_id in range(face_nodes):
                for comp_id in range(components):
                    row_id = part_id * lane + comp_id * node_count + face_mask[face_id][node_id]
                    table[row_id, face_id * half_lane + node_id * components + comp_id] = 1.0
    return jnp.asarray(table.astype(ml_dtypes.bfloat16))


def split_two(value):
    high = value.astype(jnp.bfloat16)
    rest = (value - high.astype(jnp.float32)).astype(jnp.bfloat16)
    return high, rest


def dot_rows(left, right):
    return lax.dot_general(
        left, right, (((1,), (0,)), ((), ())), preferred_element_type=jnp.float32
    )


def dot_lanes(left, right):
    return lax.dot_general(
        left, right, (((1,), (1,)), ((), ())), preferred_element_type=jnp.float32
    )


def one_hot(mask):
    return jnp.where(mask, 1.0, 0.0).astype(jnp.bfloat16)


def face_of(codes):
    return sum((codes >= step * new_count).astype(jnp.int32) for step in range(1, faces))


def pack_kernel(fields_ref, geometry_ref, list_ref, out_ref, took_ref, geo_ref, codes_ref, held_ref, sems):
    field_rows = components * node_count
    copies = [
        pltpu.make_async_copy(list_ref, codes_ref, sems.at[0]),
        pltpu.make_async_copy(fields_ref, took_ref, sems.at[1]),
        pltpu.make_async_copy(geometry_ref, geo_ref, sems.at[2]),
    ]
    for copy in copies:
        copy.start()
    copies[0].wait()
    turned = jnp.concatenate([codes_ref[slot_id] for slot_id in range(slots)], axis=0)
    turned = jnp.concatenate([turned, jnp.zeros((lane - slots, slabs), jnp.int32)], axis=0)
    turned = jnp.concatenate([turned, jnp.zeros((lane, lane - slabs), jnp.int32)], axis=1)
    codes = jnp.transpose(turned)[:slabs]
    lanes = lax.broadcasted_iota(jnp.int32, (slabs, old_count), 1)
    picks = jnp.concatenate(
        [one_hot(codes[:, slot_id : slot_id + 1] == lanes) for slot_id in range(slots)], axis=0
    )
    copies[1].wait()
    copies[2].wait()
    for comp_id in range(components):
        held_ref[comp_id * node_count : (comp_id + 1) * node_count, :] = took_ref[comp_id]
    held_ref[field_rows : field_rows + 11, :] = geo_ref[...]
    held_ref[field_rows + 11 :, :] = jnp.zeros((13, old_count), jnp.float32)
    parts = jnp.concatenate(split_two(held_ref[...]), axis=1)
    parts = jnp.concatenate([parts, jnp.zeros((112, 2 * old_count), jnp.bfloat16)], axis=0)
    moved = dot_lanes(jnp.concatenate([picks, picks], axis=1), parts)
    short = lax.broadcasted_iota(jnp.int32, (slabs, lane), 1)
    diagonal = (short == field_rows) | (short == field_rows + 4)
    tail = jnp.zeros((slabs, lane), jnp.float32)
    for slot_id in range(slots):
        empty = codes[:, slot_id : slot_id + 1] < 0
        block = moved[slot_id * slabs : (slot_id + 1) * slabs]
        out_ref[pl.ds(slot_id, slabs, stride=block_rows), :] = jnp.where(
            empty & diagonal, 1.0, block[:, :lane]
        )
        ending = jnp.where(empty & (short < 3), 1.0, block[:, lane:])
        if slot_id:
            ending = pltpu.roll(ending, 3 * slot_id, 1)
        tail = tail + ending
    out_ref[pl.ds(slots, slabs, stride=block_rows), :] = tail


def plan_kernel(
    list_ref, link_ref, orient_ref, came_pick_ref, slot_pick_ref, face_ref, spread_ref, about_ref, codes_ref
):
    codes = list_ref[0]
    half = traces // 2
    for idx in range(traces):
        rows = pl.ds((idx // half) * lane + idx % half, subs, stride=half)
        codes_ref[rows, :] = jnp.broadcast_to(codes[:, idx : idx + 1], (subs, lane))
    codes = codes_ref[...]
    face = face_of(codes)
    element = codes - new_count * face
    face_ref[...] = face
    lanes = lax.broadcasted_iota(jnp.int32, (remote_count, lane), 1)
    slot_pick_ref[...] = jnp.concatenate(
        [one_hot(element == lanes + tile * lane) for tile in range(tiles)], axis=1
    )
    came_row = element + ((element * 5462) >> 16)
    came_pick_ref[...] = jnp.concatenate(
        [one_hot(came_row == lanes + tile * lane) for tile in range(tiles + 1)], axis=1
    )
    rows = lax.broadcasted_iota(jnp.int32, (remote_count, new_count), 0)
    about_rows = lax.broadcasted_iota(jnp.int32, (16, new_count), 0)
    about = None
    spread = None
    for face_id in range(faces):
        far = link_ref[face_id : face_id + 1, :] - column_count
        orient = orient_ref[face_id : face_id + 1, :]
        column = ((far >> 3) & 1) * lane + (far >> 4) * 8 + (far & 7)
        column = jnp.where((far >= 0) & (orient < 6), column, -1)
        picks = one_hot(rows == column)
        facts = jnp.where(about_rows == 0, orient, jnp.where(about_rows == 1, face_id, 0))
        term = dot_lanes(facts.astype(jnp.float32).astype(jnp.bfloat16), picks)
        about = term if about is None else about + term
        spread = picks if spread is None else spread + picks
    spread_ref[...] = spread
    about_ref[...] = about[:8]


def trace_rows(found, face, select_ref, trace_ref):
    wide = dot_rows(found.astype(jnp.bfloat16), select_ref[...])
    near = jnp.where(face >= 2, wide[:, lane:], wide[:, :lane])
    odd = (face & 1) == 1
    half = remote_count // 2
    upper, lower = near[:half], near[half:]
    upper = jnp.where(odd[:half], pltpu.roll(upper, half_lane, 1), upper)
    lower = jnp.where(odd[half:], lower, pltpu.roll(lower, half_lane, 1))
    lanes = lax.broadcasted_iota(jnp.int32, (half, lane), 1)
    trace_ref[...] = jnp.where(lanes < half_lane, upper, lower)


def start_kernel(came_ref, pick_ref, face_ref, select_ref, trace_ref):
    parts = jnp.concatenate(split_two(came_ref[...]), axis=1)
    parts = jnp.concatenate(
        [parts, jnp.zeros((4 * lane - slabs * block_rows, 2 * lane), jnp.bfloat16)], axis=0
    )
    trace_rows(dot_rows(pick_ref[...], parts), face_ref[...], select_ref, trace_ref)


def unpack(came_ref, state_ref, derived_ref, rows_ref, tail_ref, main_ref):
    field_rows = components * node_count
    tail = came_ref[pl.ds(slots, slabs, stride=block_rows), :]
    for slot_id in range(slots):
        rows_ref[pl.ds(slot_id, slabs, stride=slots), :] = came_ref[
            pl.ds(slot_id, slabs, stride=block_rows), :
        ]
        shifted = pltpu.roll(tail, lane - 3 * slot_id, 1) if slot_id else tail
        tail_ref[pl.ds(slot_id, slabs, stride=slots), :] = shifted
    main_ref[...] = jnp.transpose(rows_ref[...])
    extra = jnp.transpose(tail_ref[...])[:8]
    for comp_id in range(components):
        state_ref[comp_id] = main_ref[comp_id * node_count : (comp_id + 1) * node_count, :]
    geo = [main_ref[field_rows + row_id : field_rows + row_id + 1, :] for row_id in range(8)]
    geo.append(extra[0:1])
    derived_ref[0:8, :] = main_ref[field_rows : field_rows + 8, :]
    derived_ref[8:9, :] = extra[0:1]
    derived_ref[9:10, :] = 1.0 / extra[1:2]
    derived_ref[10:11, :] = 1.0 / extra[2:3]
    total = None
    for axis_id in range(3):
        first, second, third = geo[axis_id], geo[3 + axis_id], geo[6 + axis_id]
        normal = 0.5 * jnp.concatenate([-third, -second, first + second + third, -first], axis=0)
        square = normal * normal
        total = square if total is None else total + square
        normal_rows = jnp.concatenate([normal, normal], axis=0)
        derived_ref[16 + 8 * axis_id : 24 + 8 * axis_id, :] = normal_rows
    length = jnp.sqrt(total)
    derived_ref[40:48, :] = jnp.concatenate([length, length], axis=0)
    inverse = 1.0 / length
    derived_ref[48:56, :] = jnp.concatenate([inverse, inverse], axis=0)


def compact(derived_ref, spread_ref, about_ref, far_ref):
    stacked = jnp.concatenate(split_two(derived_ref[16:64, :]), axis=0)
    found = dot_lanes(stacked, spread_ref[...])
    found = found[:48] + found[48:]
    face = about_ref[1:2, :]
    for block in range(5):
        first_row = 8 * block
        value = found[first_row : first_row + 1]
        for face_id in range(1, faces):
            row_id = first_row + face_id
            value = jnp.where(face == face_id, found[row_id : row_id + 1], value)
        far_ref[block : block + 1, :] = value
    far_ref[5:7, :] = about_ref[0:2, :]
    far_ref[7:8, :] = jnp.zeros((1, remote_count), jnp.float32)


def oriented(planes, orient):
    masks = [orient == turn_id for turn_id in range(6)]
    result = []
    for node_id in range(face_nodes):
        sources = {}
        for turn_id in range(6):
            sources.setdefault(node_perms[turn_id][node_id], []).append(turn_id)
        value = None
        for source, turn_ids in sources.items():
            if value is None:
                value = planes[source]
                continue
            mask = masks[turn_ids[0]]
            for turn_id in turn_ids[1:]:
                mask = mask | masks[turn_id]
            value = jnp.where(mask, planes[source], value)
        result.append(value)
    return result


def face_flux(jump_of, normal, length, inverse):
    jump_h = [jump_of(comp_id) for comp_id in range(3)]
    jump_e = [jump_of(comp_id) for comp_id in range(3, 6)]

    def along(jump):
        total = normal[0] * jump[0] + normal[1] * jump[1] + normal[2] * jump[2]
        return total * inverse

    along_h = along(jump_h)
    along_e = along(jump_e)
    flux_h, flux_e = [], []
    for axis_id in range(3):
        after, last = (axis_id + 1) % 3, (axis_id + 2) % 3
        cross_e = normal[after] * jump_e[last] - normal[last] * jump_e[after]
        cross_h = normal[after] * jump_h[last] - normal[last] * jump_h[after]
        flux_h.append(length * jump_h[axis_id] - normal[axis_id] * along_h - cross_e)
        flux_e.append(length * jump_e[axis_id] - normal[axis_id] * along_e + cross_h)
    return flux_h + flux_e


def lifted_flux(jump_ref, flux_ref, derived_ref, lift_ref):
    groups = faces * face_nodes // 8

    def jump_of(comp_id):
        rows = strided_load(jump_ref, comp_id, faces * face_nodes, 8)
        return rows.reshape(groups, 8, new_count)

    normal = [derived_ref[16 + 8 * axis_id : 24 + 8 * axis_id, :][None] for axis_id in range(3)]
    fluxes = face_flux(jump_of, normal, derived_ref[40:48, :][None], derived_ref[48:56, :][None])
    for comp_id, value in enumerate(fluxes):
        flux_ref[0:40, comp_id * new_count : (comp_id + 1) * new_count] = value.reshape(
            faces * face_nodes, new_count
        )
    flux_ref[40:48, :] = jnp.zeros((8, components * new_count), jnp.float32)
    high, rest = split_two(flux_ref[...])
    return dot_rows(lift_ref[...], jnp.concatenate([high, rest, high], axis=0))


def strided_load(ref, start, size, stride):
    return jnp.concatenate(
        [ref[tile, pl.ds(start, size, stride=stride), :] for tile in range(ref.shape[0])], axis=1
    )


def tiled_store(ref, rows, value):
    for tile in range(ref.shape[0]):
        ref[tile, rows, :] = value[:, tile * lane : (tile + 1) * lane]


def tiled_load(ref, rows):
    return jnp.concatenate([ref[tile, rows, :] for tile in range(tiles)], axis=1)


def column_block(matrix, comp_id):
    return matrix[:24, comp_id * new_count : (comp_id + 1) * new_count]


def local_part(
    state_ref, derived_ref, link_ref, orient_ref, slope_ref, lift_ref, part_ref, nodes_ref, flat_ref, jump_ref, flux_ref
):
    nodes_ref[...] = jnp.zeros(nodes_ref.shape, jnp.float32)
    flat_ref[node_count:32, :] = jnp.zeros((12, components * new_count), jnp.float32)
    for comp_id in range(components):
        current = state_ref[comp_id]
        tiled_store(nodes_ref, pl.ds(comp_id, node_count, stride=8), current)
        flat_ref[0:node_count, comp_id * new_count : (comp_id + 1) * new_count] = current
    stacked = jnp.concatenate(split_two(tiled_load(nodes_ref, slice(None))), axis=0)
    rows = lax.broadcasted_iota(jnp.int32, (new_count, new_count), 0)
    comp_rows = lax.broadcasted_iota(jnp.int32, (8, new_count), 0)
    wall_gain = jnp.where(comp_rows >= 3, -2.0, 0.0)
    for face_id in range(faces):
        link = link_ref[face_id : face_id + 1, :]
        orient = orient_ref[face_id : face_id + 1, :]
        owner = face_of(link)
        element = jnp.where(link < column_count, link - new_count * owner, -1)
        found = dot_rows(stacked, one_hot(rows == element))
        found = found[: 8 * node_count] + found[8 * node_count :]
        owner_masks = [owner == other for other in range(faces)]
        planes = []
        for node_id in range(face_nodes):
            value = None
            for other in range(faces):
                first_row = 8 * face_mask[other][node_id]
                plane = found[first_row : first_row + 8]
                value = plane if value is None else jnp.where(owner_masks[other], plane, value)
            planes.append(value)
        outside = oriented(planes, orient)
        wall = orient == 6
        for node_id in range(face_nodes):
            first_row = 8 * face_mask[face_id][node_id]
            inside = tiled_load(nodes_ref, slice(first_row, first_row + 8))
            jump = jnp.where(wall, wall_gain * inside, outside[node_id] - inside)
            target = 8 * (node_id * faces + face_id)
            tiled_store(jump_ref, slice(target, target + 8), jump)
    lifted = lifted_flux(jump_ref, flux_ref, derived_ref, lift_ref)
    high, rest = split_two(flat_ref[...])
    slopes = dot_rows(slope_ref[...], jnp.concatenate([high, rest, high], axis=0))
    inverse_jac = [
        [derived_ref[3 * row_id + axis_id : 3 * row_id + axis_id + 1, :] for axis_id in range(3)]
        for row_id in range(3)
    ]

    def gradient(axis_id, comp_id):
        columns = slice(comp_id * new_count, (comp_id + 1) * new_count)
        return (
            inverse_jac[0][axis_id] * slopes[0:24, columns]
            + inverse_jac[1][axis_id] * slopes[24:48, columns]
            + inverse_jac[2][axis_id] * slopes[48:72, columns]
        )

    inverse_eps = derived_ref[9:10, :]
    inverse_mu = derived_ref[10:11, :]
    for axis_id in range(3):
        after, last = (axis_id + 1) % 3, (axis_id + 2) % 3
        curl_h = gradient(after, last) - gradient(last, after)
        curl_e = gradient(after, 3 + last) - gradient(last, 3 + after)
        change_h = (column_block(lifted, axis_id) - curl_e) * inverse_mu
        change_e = (column_block(lifted, 3 + axis_id) + curl_h) * inverse_eps
        part_ref[axis_id] = change_h[:node_count]
        part_ref[3 + axis_id] = change_e[:node_count]


def arrive_kernel(
    came_ref,
    link_ref,
    orient_ref,
    slope_ref,
    lift_ref,
    spread_ref,
    about_ref,
    state_ref,
    derived_ref,
    far_ref,
    part_ref,
    rows_ref,
    tail_ref,
    main_ref,
    *scratches,
):
    derived_ref[...] = jnp.zeros(derived_ref.shape, jnp.float32)
    unpack(came_ref, state_ref, derived_ref, rows_ref, tail_ref, main_ref)
    compact(derived_ref, spread_ref, about_ref, far_ref)
    local_part(state_ref, derived_ref, link_ref, orient_ref, slope_ref, lift_ref, part_ref, *scratches)


def local_kernel(*refs):
    local_part(*refs)


def remote_part(came_ref, far_ref, spread_ref, lift_ref, derived_ref, turned_ref, table_ref, jump_ref, flux_ref):
    turned_ref[...] = jnp.transpose(came_ref[...])
    table_ref[...] = jnp.zeros(table_ref.shape, jnp.float32)
    for half in range(2):
        for node_id in range(face_nodes):
            first_row = half * half_lane + node_id * components
            table_ref[half, 8 * node_id : 8 * node_id + components, :] = turned_ref[
                first_row : first_row + components, :
            ]
    planes = [
        jnp.concatenate(
            [table_ref[half, 8 * node_id : 8 * node_id + 8, :] for half in range(2)], axis=1
        )
        for node_id in range(face_nodes)
    ]
    outside = oriented(planes, far_ref[5:6, :])
    for node_id in range(face_nodes):
        tiled_store(jump_ref, slice(8 * node_id, 8 * node_id + 8), outside[node_id])
    fluxes = face_flux(
        lambda comp_id: strided_load(jump_ref, comp_id, face_nodes, 8),
        [far_ref[axis_id : axis_id + 1, :] for axis_id in range(3)],
        far_ref[3:4, :],
        far_ref[4:5, :],
    )
    flux_ref[...] = jnp.zeros(flux_ref.shape, jnp.float32)
    face = far_ref[6:7, :]
    for face_id in range(faces):
        here = face == face_id
        for comp_id, value in enumerate(fluxes):
            columns = slice(comp_id * remote_count, (comp_id + 1) * remote_count)
            flux_ref[16 * face_id : 16 * face_id + face_nodes, columns] = jnp.where(here, value, 0.0)
    high, rest = split_two(flux_ref[...])
    lifted = dot_rows(lift_ref[...], jnp.concatenate([high, rest, high], axis=0))
    stacked = jnp.concatenate(
        [
            lifted[:24, comp_id * remote_count : (comp_id + 1) * remote_count]
            for comp_id in range(components)
        ],
        axis=0,
    )
    placed = dot_rows(jnp.concatenate(split_two(stacked), axis=0), spread_ref[...])
    rows = 24 * components
    placed = placed[:rows] + placed[rows:]
    inverse_eps = derived_ref[9:10, :]
    inverse_mu = derived_ref[10:11, :]
    return [
        (placed[24 * comp_id : 24 * comp_id + 24] * (inverse_mu if comp_id < 3 else inverse_eps))[
            :node_count
        ]
        for comp_id in range(components)
    ]


def first_kernel(
    came_ref,
    part_ref,
    state_ref,
    derived_ref,
    far_ref,
    spread_ref,
    lift_ref,
    pick_ref,
    face_ref,
    select_ref,
    residual_ref,
    middle_ref,
    trace_ref,
    main_ref,
    *scratches,
):
    changes = remote_part(came_ref, far_ref, spread_ref, lift_ref, derived_ref, *scratches)
    main_ref[components * node_count :, :] = jnp.zeros((8, new_count), jnp.float32)
    for comp_id in range(components):
        residual = time_step * (part_ref[comp_id] + changes[comp_id])
        middle = state_ref[comp_id] + section_b1 * residual
        residual_ref[comp_id] = residual
        middle_ref[comp_id] = middle
        main_ref[comp_id * node_count : (comp_id + 1) * node_count, :] = middle
    parts = jnp.concatenate(split_two(main_ref[...]), axis=0)
    trace_rows(dot_lanes(pick_ref[...], parts), face_ref[...], select_ref, trace_ref)


def second_kernel(
    came_ref,
    part_ref,
    middle_ref,
    first_ref,
    derived_ref,
    far_ref,
    spread_ref,
    lift_ref,
    advanced_ref,
    residual_ref,
    *scratches,
):
    changes = remote_part(came_ref, far_ref, spread_ref, lift_ref, derived_ref, *scratches)
    for comp_id in range(components):
        residual = section_a2 * first_ref[comp_id] + time_step * (
            part_ref[comp_id] + changes[comp_id]
        )
        residual_ref[comp_id] = residual
        advanced_ref[comp_id] = middle_ref[comp_id] + section_b2 * residual


def floats(*shape):
    return jax.ShapeDtypeStruct(shape, jnp.float32)


def near(*shape):
    return pltpu.VMEM(shape, jnp.float32)


def halves(*shape):
    return jax.ShapeDtypeStruct(shape, jnp.bfloat16)


def scratch(*shape):
    return pltpu.VMEM(shape, jnp.float32)


def run(kernel, name, outs, scratches, operands, in_specs=None):
    return pl.pallas_call(
        kernel,
        name=name,
        out_shape=outs,
        in_specs=in_specs or [pl.BlockSpec(memory_space=pltpu.VMEM)] * len(operands),
        scratch_shapes=scratches,
        compiler_params=pltpu.CompilerParams(vmem_limit_bytes=24 * 2**20),
        cost_estimate=pl.CostEstimate(flops=10**8, bytes_accessed=10**6, transcendentals=0),
    )(*operands)


def shards(fields, geometry, migrate_list, trace_list, face_link, face_orient):
    slopes = slope_operand()
    lift = lift_operand()
    remote_lift = remote_lift_operand()
    select = select_operand()
    state_shape = floats(components, node_count, new_count)
    trace_shape = near(remote_count // 2, lane)
    local_scratch = [
        scratch(tiles, 8 * node_count, lane),
        scratch(32, components * new_count),
        scratch(tiles, 8 * faces * face_nodes, lane),
        scratch(48, components * new_count),
    ]
    remote_scratch = [
        scratch(lane, lane),
        scratch(2, 8 * face_nodes, lane),
        scratch(2, 8 * face_nodes, lane),
        scratch(16 * faces, components * remote_count),
    ]
    parcel = run(
        pack_kernel,
        "pack",
        near(slabs * block_rows, lane),
        [
            scratch(components, node_count, old_count),
            scratch(11, old_count),
            pltpu.VMEM((slots, 1, slabs), jnp.int32),
            scratch(144, old_count),
            pltpu.SemaphoreType.DMA((3,)),
        ],
        [
            pltpu.with_memory_space_constraint(operand, pltpu.HBM)
            for operand in (fields, geometry, jnp.transpose(migrate_list, (2, 0, 1)))
        ],
        [pl.BlockSpec(memory_space=pltpu.HBM)] * 3,
    )
    arrived = lax.all_to_all(
        parcel.reshape(slabs, block_rows * lane), "slab", split_axis=0, concat_axis=0, tiled=True
    ).reshape(slabs * block_rows, lane)
    came_pick, slot_pick, trace_face, spread, about = run(
        plan_kernel,
        "plan",
        (
            halves(remote_count, 4 * lane),
            halves(remote_count, new_count),
            jax.ShapeDtypeStruct((remote_count, lane), jnp.int32),
            halves(remote_count, new_count),
            floats(8, remote_count),
        ),
        [pltpu.VMEM((remote_count, lane), jnp.int32)],
        (trace_list, face_link, face_orient),
    )
    outgoing = run(
        start_kernel, "start", trace_shape, [], (arrived, came_pick, trace_face, select)
    )

    def exchange(rows):
        blocks = rows.reshape(subs, traces // 2, lane)
        came = lax.all_to_all(blocks, "sub", split_axis=0, concat_axis=0, tiled=True)
        return came.reshape(remote_count // 2, lane)

    incoming = exchange(outgoing)
    state, derived, far, part = run(
        arrive_kernel,
        "arrive",
        (state_shape, floats(64, new_count), floats(8, remote_count), state_shape),
        [scratch(new_count, lane), scratch(new_count, lane), scratch(lane, new_count)]
        + local_scratch,
        (arrived, face_link, face_orient, slopes, lift, spread, about),
    )
    first_res, middle, outgoing = run(
        first_kernel,
        "first",
        (state_shape, state_shape, trace_shape),
        [scratch(lane, new_count)] + remote_scratch,
        (
            incoming,
            part,
            state,
            derived,
            far,
            spread,
            remote_lift,
            slot_pick,
            trace_face,
            select,
        ),
    )
    incoming = exchange(outgoing)
    part = run(
        local_kernel,
        "local",
        state_shape,
        local_scratch,
        (middle, derived, face_link, face_orient, slopes, lift),
    )
    return run(
        second_kernel,
        "second",
        (state_shape, state_shape),
        remote_scratch,
        (incoming, part, middle, first_res, derived, far, spread, remote_lift),
    )


def solution(mesh):
    return jax.shard_map(
        shards,
        mesh=mesh,
        in_specs=(
            P(None, None, ("slab", "sub")),
            P(None, ("slab", "sub")),
            P(("slab", "sub"), None, None),
            P(("slab", "sub"), None, None),
            P(None, ("slab", "sub")),
            P(None, ("slab", "sub")),
        ),
        out_specs=(P(None, None, ("slab", "sub")), P(None, None, ("slab", "sub"))),
        check_vma=False,
    )
```

```python
import math

import jax
import jax.numpy as jnp
import ml_dtypes
import numpy as np
from jax import lax
from jax.experimental import pallas as pl
from jax.experimental.pallas import tpu as pltpu
from jax.sharding import PartitionSpec as P

time_step = 0.004
section_a2 = -0.4178904745
section_b1 = 0.1496590219993
section_b2 = 0.3792103129999
coordinate_perms = ((0, 1, 2), (1, 2, 0), (2, 0, 1), (0, 2, 1), (2, 1, 0), (1, 0, 2))
components = 6
node_count = 20
face_nodes = 10
faces = 4
old_count = 256
slots = 12
slabs = 32
subs = 16
traces = 16
new_count = slots * slabs
column_count = faces * new_count
remote_count = subs * traces
lane = 128
half_lane = lane // 2
tiles = new_count // lane
block_rows = slots + 1
slab_first = 22
sub_first = 10
slab_order = [(slab_first + place) % slabs for place in range(slabs)]
sub_order = [(sub_first + place) % subs for place in range(subs)]


def volume_triples():
    result_list = []
    for first_idx in range(4):
        for second_idx in range(4 - first_idx):
            for third_idx in range(4 - first_idx - second_idx):
                result_list.append((first_idx, second_idx, third_idx))
    return result_list


def planar_pairs():
    result_list = []
    for first_idx in range(4):
        for second_idx in range(4 - first_idx):
            result_list.append((first_idx, second_idx))
    return result_list


def monomial_matrix(points, powers):
    result_rows = []
    for point_item in points:
        row_values = []
        for power_item in powers:
            product_value = 1.0
            for axis_id in range(len(power_item)):
                product_value = product_value * point_item[axis_id] ** power_item[axis_id]
            row_values.append(product_value)
        result_rows.append(row_values)
    return result_rows


def mat_mul(left_rows, right_rows):
    inner_count = len(right_rows)
    col_count = len(right_rows[0])
    return [
        [
            sum((left_row[k_id] * right_rows[k_id][c_id] for k_id in range(inner_count)))
            for c_id in range(col_count)
        ]
        for left_row in left_rows
    ]


def transposed(matrix_rows):
    return [list(row_item) for row_item in zip(*matrix_rows)]


def invert(matrix_rows):
    order = len(matrix_rows)
    work_rows = [
        list(matrix_rows[r_id]) + [1.0 if r_id == c_id else 0.0 for c_id in range(order)]
        for r_id in range(order)
    ]
    for col_id in range(order):
        pivot_row = max(range(col_id, order), key=lambda r_id: abs(work_rows[r_id][col_id]))
        work_rows[col_id], work_rows[pivot_row] = (work_rows[pivot_row], work_rows[col_id])
        pivot_value = work_rows[col_id][col_id]
        work_rows[col_id] = [value / pivot_value for value in work_rows[col_id]]
        for r_id in range(order):
            if r_id != col_id:
                factor = work_rows[r_id][col_id]
                if factor != 0.0:
                    work_rows[r_id] = [
                        work_rows[r_id][c_id] - factor * work_rows[col_id][c_id]
                        for c_id in range(2 * order)
                    ]
    return [row_item[order:] for row_item in work_rows]


def moment_matrix(powers, extra_dim):
    total_terms = len(powers)
    result_matrix = [[0.0] * total_terms for _ in range(total_terms)]
    for row_id in range(total_terms):
        for col_id in range(total_terms):
            joined = [
                powers[row_id][a_id] + powers[col_id][a_id] for a_id in range(len(powers[row_id]))
            ]
            numerator = 1.0
            for exponent in joined:
                numerator = numerator * math.factorial(exponent)
            result_matrix[row_id][col_id] = numerator / math.factorial(sum(joined) + extra_dim)
    return result_matrix


def dg_tables():
    triples = volume_triples()
    points = [tuple((value / 3.0 for value in triple)) for triple in triples]
    inverse = invert(monomial_matrix(points, triples))
    slopes = []
    for axis_id in range(3):
        lowered = [
            tuple(
                (max(triple[a_id] - 1, 0) if a_id == axis_id else triple[a_id] for a_id in range(3))
            )
            for triple in triples
        ]
        base_rows = monomial_matrix(points, lowered)
        slope_values = [
            [triples[c_id][axis_id] * base_rows[r_id][c_id] for c_id in range(20)]
            for r_id in range(20)
        ]
        slopes.append(mat_mul(slope_values, inverse))
    volume_mass = mat_mul(mat_mul(transposed(inverse), moment_matrix(triples, 3)), inverse)
    planar = planar_pairs()
    face_points = [tuple((value / 3.0 for value in pair_item)) for pair_item in planar]
    face_inverse = invert(monomial_matrix(face_points, planar))
    face_mass = mat_mul(mat_mul(transposed(face_inverse), moment_matrix(planar, 2)), face_inverse)
    face_axes = ((0, 1), (0, 2), (0, 1), (1, 2))
    face_mask = [[0] * 10 for _ in range(4)]
    for face_id in range(4):
        for node_id, triple in enumerate(triples):
            on_face = (
                triple[2] == 0,
                triple[1] == 0,
                triple[0] + triple[1] + triple[2] == 3,
                triple[0] == 0,
            )[face_id]
            if on_face:
                key_pair = (triple[face_axes[face_id][0]], triple[face_axes[face_id][1]])
                face_mask[face_id][planar.index(key_pair)] = node_id
    surface = [[0.0] * 40 for _ in range(20)]
    for face_id in range(4):
        for row_id in range(10):
            for col_id in range(10):
                surface[face_mask[face_id][row_id]][face_id * 10 + col_id] += face_mass[row_id][
                    col_id
                ]
    lifting = mat_mul(invert(volume_mass), surface)
    lift_alt = [
        [lifting[n_id][f_id * 10 + j_id] for j_id in range(10) for f_id in range(4)]
        for n_id in range(20)
    ]
    node_perms = []
    for turn_id in range(6):
        perm_row = []
        for pair_item in planar:
            triple_face = (pair_item[0], pair_item[1], 3 - pair_item[0] - pair_item[1])
            moved_triple = [triple_face[coordinate_perms[turn_id][axis_id]] for axis_id in range(3)]
            perm_row.append(planar.index((moved_triple[0], moved_triple[1])))
        node_perms.append(perm_row)
    node_picks = [face_mask[f_id][j_id] for j_id in range(10) for f_id in range(4)]
    return slopes, lifting, face_mask, node_perms


def bf16_pair(matrix):
    wide = np.asarray(matrix, np.float32)
    high = wide.astype(ml_dtypes.bfloat16)
    rest = (wide - high.astype(np.float32)).astype(ml_dtypes.bfloat16)
    return high, rest


slope_table, lift_table, face_mask, node_perms = dg_tables()


def slope_operand():
    stacked = np.zeros((80, 32), np.float64)
    for axis_id in range(3):
        first_row = axis_id * 24
        stacked[first_row : first_row + node_count, :node_count] = slope_table[axis_id]
    high, rest = bf16_pair(stacked)
    return jnp.asarray(np.concatenate([high, high, rest], axis=1))


def lift_operand():
    stacked = np.zeros((32, 48), np.float64)
    for face_id in range(faces):
        for node_id in range(face_nodes):
            for row_id in range(node_count):
                stacked[row_id, node_id * faces + face_id] = lift_table[row_id][
                    face_id * face_nodes + node_id
                ]
    high, rest = bf16_pair(stacked)
    return jnp.asarray(np.concatenate([high, high, rest], axis=1))


def remote_lift_operand():
    stacked = np.zeros((32, 16 * faces), np.float64)
    for face_id in range(faces):
        for node_id in range(face_nodes):
            for row_id in range(node_count):
                stacked[row_id, face_id * 16 + node_id] = lift_table[row_id][
                    face_id * face_nodes + node_id
                ]
    high, rest = bf16_pair(stacked)
    return jnp.asarray(np.concatenate([high, high, rest], axis=1))


def select_operand():
    table = np.zeros((2 * lane, faces * half_lane), np.float32)
    for face_id in range(faces):
        for part_id in range(2):
            for node_id in range(face_nodes):
                for comp_id in range(components):
                    row_id = part_id * lane + comp_id * node_count + face_mask[face_id][node_id]
                    table[row_id, face_id * half_lane + node_id * components + comp_id] = 1.0
    return jnp.asarray(table.astype(ml_dtypes.bfloat16))


def split_two(value):
    high = value.astype(jnp.bfloat16)
    rest = (value - high.astype(jnp.float32)).astype(jnp.bfloat16)
    return high, rest


def dot_rows(left, right):
    return lax.dot_general(
        left, right, (((1,), (0,)), ((), ())), preferred_element_type=jnp.float32
    )


def dot_lanes(left, right):
    return lax.dot_general(
        left, right, (((1,), (1,)), ((), ())), preferred_element_type=jnp.float32
    )


def one_hot(mask):
    return jnp.where(mask, 1.0, 0.0).astype(jnp.bfloat16)


def face_of(codes):
    return sum((codes >= step * new_count).astype(jnp.int32) for step in range(1, faces))


def pack_kernel(fields_ref, geometry_ref, list_ref, out_ref, took_ref, geo_ref, codes_ref, held_ref, sems):
    field_rows = components * node_count
    copies = [
        pltpu.make_async_copy(list_ref, codes_ref, sems.at[0]),
        pltpu.make_async_copy(fields_ref, took_ref, sems.at[1]),
        pltpu.make_async_copy(geometry_ref, geo_ref, sems.at[2]),
    ]
    for copy in copies:
        copy.start()
    copies[0].wait()
    turned = jnp.concatenate([codes_ref[slot_id] for slot_id in range(slots)], axis=0)
    turned = jnp.concatenate([turned, jnp.zeros((lane - slots, slabs), jnp.int32)], axis=0)
    turned = jnp.concatenate([turned, jnp.zeros((lane, lane - slabs), jnp.int32)], axis=1)
    codes = jnp.transpose(turned)[:slabs]
    codes = jnp.concatenate([codes[slab_first:], codes[:slab_first]], axis=0)
    lanes = lax.broadcasted_iota(jnp.int32, (slabs, old_count), 1)
    picks = jnp.concatenate(
        [one_hot(codes[:, slot_id : slot_id + 1] == lanes) for slot_id in range(slots)], axis=0
    )
    copies[1].wait()
    copies[2].wait()
    for comp_id in range(components):
        held_ref[comp_id * node_count : (comp_id + 1) * node_count, :] = took_ref[comp_id]
    held_ref[field_rows : field_rows + 11, :] = geo_ref[...]
    held_ref[field_rows + 11 :, :] = jnp.zeros((13, old_count), jnp.float32)
    parts = jnp.concatenate(split_two(held_ref[...]), axis=1)
    parts = jnp.concatenate([parts, jnp.zeros((112, 2 * old_count), jnp.bfloat16)], axis=0)
    moved = dot_lanes(jnp.concatenate([picks, picks], axis=1), parts)
    short = lax.broadcasted_iota(jnp.int32, (slabs, lane), 1)
    diagonal = (short == field_rows) | (short == field_rows + 4)
    tail = jnp.zeros((slabs, lane), jnp.float32)
    for slot_id in range(slots):
        empty = codes[:, slot_id : slot_id + 1] < 0
        block = moved[slot_id * slabs : (slot_id + 1) * slabs]
        out_ref[pl.ds(slot_id, slabs, stride=block_rows), :] = jnp.where(
            empty & diagonal, 1.0, block[:, :lane]
        )
        ending = jnp.where(empty & (short < 3), 1.0, block[:, lane:])
        if slot_id:
            ending = pltpu.roll(ending, 3 * slot_id, 1)
        tail = tail + ending
    out_ref[pl.ds(slots, slabs, stride=block_rows), :] = tail


def plan_kernel(
    list_ref, link_ref, orient_ref, came_pick_ref, slot_pick_ref, face_ref, spread_ref, about_ref, codes_ref
):
    codes = list_ref[0]
    codes = jnp.concatenate([codes[sub_first:], codes[:sub_first]], axis=0)
    half = traces // 2
    for idx in range(traces):
        rows = pl.ds((idx // half) * lane + idx % half, subs, stride=half)
        codes_ref[rows, :] = jnp.broadcast_to(codes[:, idx : idx + 1], (subs, lane))
    codes = codes_ref[...]
    face = face_of(codes)
    element = codes - new_count * face
    face_ref[...] = face
    lanes = lax.broadcasted_iota(jnp.int32, (remote_count, lane), 1)
    slot_pick_ref[...] = jnp.concatenate(
        [one_hot(element == lanes + tile * lane) for tile in range(tiles)], axis=1
    )
    source = (element * 5462) >> 16
    place = (source + slabs - slab_first) & (slabs - 1)
    came_row = place * block_rows + element - source * slots
    came_pick_ref[...] = jnp.concatenate(
        [one_hot(came_row == lanes + tile * lane) for tile in range(tiles + 1)], axis=1
    )
    rows = lax.broadcasted_iota(jnp.int32, (remote_count, new_count), 0)
    about_rows = lax.broadcasted_iota(jnp.int32, (16, new_count), 0)
    about = None
    spread = None
    for face_id in range(faces):
        far = link_ref[face_id : face_id + 1, :] - column_count
        orient = orient_ref[face_id : face_id + 1, :]
        place = ((far >> 4) + subs - sub_first) & (subs - 1)
        column = ((far >> 3) & 1) * lane + place * 8 + (far & 7)
        column = jnp.where((far >= 0) & (orient < 6), column, -1)
        picks = one_hot(rows == column)
        facts = jnp.where(about_rows == 0, orient, jnp.where(about_rows == 1, face_id, 0))
        term = dot_lanes(facts.astype(jnp.float32).astype(jnp.bfloat16), picks)
        about = term if about is None else about + term
        spread = picks if spread is None else spread + picks
    spread_ref[...] = spread
    about_ref[...] = about[:8]


def trace_rows(found, face, select_ref, trace_ref):
    wide = dot_rows(found.astype(jnp.bfloat16), select_ref[...])
    near = jnp.where(face >= 2, wide[:, lane:], wide[:, :lane])
    odd = (face & 1) == 1
    half = remote_count // 2
    upper, lower = near[:half], near[half:]
    upper = jnp.where(odd[:half], pltpu.roll(upper, half_lane, 1), upper)
    lower = jnp.where(odd[half:], lower, pltpu.roll(lower, half_lane, 1))
    lanes = lax.broadcasted_iota(jnp.int32, (half, lane), 1)
    trace_ref[...] = jnp.where(lanes < half_lane, upper, lower)


def start_kernel(came_ref, pick_ref, face_ref, select_ref, trace_ref):
    parts = jnp.concatenate(split_two(came_ref[...]), axis=1)
    parts = jnp.concatenate(
        [parts, jnp.zeros((4 * lane - slabs * block_rows, 2 * lane), jnp.bfloat16)], axis=0
    )
    trace_rows(dot_rows(pick_ref[...], parts), face_ref[...], select_ref, trace_ref)


def unpack(came_ref, state_ref, derived_ref, rows_ref, tail_ref, main_ref):
    field_rows = components * node_count
    runs = ((slab_first, 0, slabs - slab_first), (0, slabs - slab_first, slab_first))
    tail = jnp.concatenate(
        [
            came_ref[pl.ds(place * block_rows + slots, count, stride=block_rows), :]
            for _, place, count in reversed(runs)
        ],
        axis=0,
    )
    for slot_id in range(slots):
        for source, place, count in runs:
            rows_ref[pl.ds(source * slots + slot_id, count, stride=slots), :] = came_ref[
                pl.ds(place * block_rows + slot_id, count, stride=block_rows), :
            ]
        shifted = pltpu.roll(tail, lane - 3 * slot_id, 1) if slot_id else tail
        tail_ref[pl.ds(slot_id, slabs, stride=slots), :] = shifted
    main_ref[...] = jnp.transpose(rows_ref[...])
    extra = jnp.transpose(tail_ref[...])[:8]
    for comp_id in range(components):
        state_ref[comp_id] = main_ref[comp_id * node_count : (comp_id + 1) * node_count, :]
    geo = [main_ref[field_rows + row_id : field_rows + row_id + 1, :] for row_id in range(8)]
    geo.append(extra[0:1])
    derived_ref[0:8, :] = main_ref[field_rows : field_rows + 8, :]
    derived_ref[8:9, :] = extra[0:1]
    derived_ref[9:10, :] = 1.0 / extra[1:2]
    derived_ref[10:11, :] = 1.0 / extra[2:3]
    total = None
    for axis_id in range(3):
        first, second, third = geo[axis_id], geo[3 + axis_id], geo[6 + axis_id]
        normal = 0.5 * jnp.concatenate([-third, -second, first + second + third, -first], axis=0)
        square = normal * normal
        total = square if total is None else total + square
        normal_rows = jnp.concatenate([normal, normal], axis=0)
        derived_ref[16 + 8 * axis_id : 24 + 8 * axis_id, :] = normal_rows
    length = jnp.sqrt(total)
    derived_ref[40:48, :] = jnp.concatenate([length, length], axis=0)
    inverse = 1.0 / length
    derived_ref[48:56, :] = jnp.concatenate([inverse, inverse], axis=0)


def compact(derived_ref, spread_ref, about_ref, far_ref):
    stacked = jnp.concatenate(split_two(derived_ref[16:64, :]), axis=0)
    found = dot_lanes(stacked, spread_ref[...])
    found = found[:48] + found[48:]
    face = about_ref[1:2, :]
    for block in range(5):
        first_row = 8 * block
        value = found[first_row : first_row + 1]
        for face_id in range(1, faces):
            row_id = first_row + face_id
            value = jnp.where(face == face_id, found[row_id : row_id + 1], value)
        far_ref[block : block + 1, :] = value
    far_ref[5:7, :] = about_ref[0:2, :]
    far_ref[7:8, :] = jnp.zeros((1, remote_count), jnp.float32)


def oriented(planes, orient):
    masks = [orient == turn_id for turn_id in range(6)]
    result = []
    for node_id in range(face_nodes):
        sources = {}
        for turn_id in range(6):
            sources.setdefault(node_perms[turn_id][node_id], []).append(turn_id)
        value = None
        for source, turn_ids in sources.items():
            if value is None:
                value = planes[source]
                continue
            mask = masks[turn_ids[0]]
            for turn_id in turn_ids[1:]:
                mask = mask | masks[turn_id]
            value = jnp.where(mask, planes[source], value)
        result.append(value)
    return result


def face_flux(jump_of, normal, length, inverse):
    jump_h = [jump_of(comp_id) for comp_id in range(3)]
    jump_e = [jump_of(comp_id) for comp_id in range(3, 6)]

    def along(jump):
        total = normal[0] * jump[0] + normal[1] * jump[1] + normal[2] * jump[2]
        return total * inverse

    along_h = along(jump_h)
    along_e = along(jump_e)
    flux_h, flux_e = [], []
    for axis_id in range(3):
        after, last = (axis_id + 1) % 3, (axis_id + 2) % 3
        cross_e = normal[after] * jump_e[last] - normal[last] * jump_e[after]
        cross_h = normal[after] * jump_h[last] - normal[last] * jump_h[after]
        flux_h.append(length * jump_h[axis_id] - normal[axis_id] * along_h - cross_e)
        flux_e.append(length * jump_e[axis_id] - normal[axis_id] * along_e + cross_h)
    return flux_h + flux_e


def lifted_flux(jump_ref, flux_ref, derived_ref, lift_ref):
    groups = faces * face_nodes // 8

    def jump_of(comp_id):
        rows = strided_load(jump_ref, comp_id, faces * face_nodes, 8)
        return rows.reshape(groups, 8, new_count)

    normal = [derived_ref[16 + 8 * axis_id : 24 + 8 * axis_id, :][None] for axis_id in range(3)]
    fluxes = face_flux(jump_of, normal, derived_ref[40:48, :][None], derived_ref[48:56, :][None])
    for comp_id, value in enumerate(fluxes):
        flux_ref[0:40, comp_id * new_count : (comp_id + 1) * new_count] = value.reshape(
            faces * face_nodes, new_count
        )
    flux_ref[40:48, :] = jnp.zeros((8, components * new_count), jnp.float32)
    high, rest = split_two(flux_ref[...])
    return dot_rows(lift_ref[...], jnp.concatenate([high, rest, high], axis=0))


def strided_load(ref, start, size, stride):
    return jnp.concatenate(
        [ref[tile, pl.ds(start, size, stride=stride), :] for tile in range(ref.shape[0])], axis=1
    )


def tiled_store(ref, rows, value):
    for tile in range(ref.shape[0]):
        ref[tile, rows, :] = value[:, tile * lane : (tile + 1) * lane]


def tiled_load(ref, rows):
    return jnp.concatenate([ref[tile, rows, :] for tile in range(tiles)], axis=1)


def column_block(matrix, comp_id):
    return matrix[:24, comp_id * new_count : (comp_id + 1) * new_count]


def local_part(
    state_ref, derived_ref, link_ref, orient_ref, slope_ref, lift_ref, part_ref, nodes_ref, flat_ref, jump_ref, flux_ref
):
    nodes_ref[...] = jnp.zeros(nodes_ref.shape, jnp.float32)
    flat_ref[node_count:32, :] = jnp.zeros((12, components * new_count), jnp.float32)
    for comp_id in range(components):
        current = state_ref[comp_id]
        tiled_store(nodes_ref, pl.ds(comp_id, node_count, stride=8), current)
        flat_ref[0:node_count, comp_id * new_count : (comp_id + 1) * new_count] = current
    stacked = jnp.concatenate(split_two(tiled_load(nodes_ref, slice(None))), axis=0)
    rows = lax.broadcasted_iota(jnp.int32, (new_count, new_count), 0)
    comp_rows = lax.broadcasted_iota(jnp.int32, (8, new_count), 0)
    wall_gain = jnp.where(comp_rows >= 3, -2.0, 0.0)
    for face_id in range(faces):
        link = link_ref[face_id : face_id + 1, :]
        orient = orient_ref[face_id : face_id + 1, :]
        owner = face_of(link)
        element = jnp.where(link < column_count, link - new_count * owner, -1)
        found = dot_rows(stacked, one_hot(rows == element))
        found = found[: 8 * node_count] + found[8 * node_count :]
        owner_masks = [owner == other for other in range(faces)]
        planes = []
        for node_id in range(face_nodes):
            value = None
            for other in range(faces):
                first_row = 8 * face_mask[other][node_id]
                plane = found[first_row : first_row + 8]
                value = plane if value is None else jnp.where(owner_masks[other], plane, value)
            planes.append(value)
        outside = oriented(planes, orient)
        wall = orient == 6
        for node_id in range(face_nodes):
            first_row = 8 * face_mask[face_id][node_id]
            inside = tiled_load(nodes_ref, slice(first_row, first_row + 8))
            jump = jnp.where(wall, wall_gain * inside, outside[node_id] - inside)
            target = 8 * (node_id * faces + face_id)
            tiled_store(jump_ref, slice(target, target + 8), jump)
    lifted = lifted_flux(jump_ref, flux_ref, derived_ref, lift_ref)
    high, rest = split_two(flat_ref[...])
    slopes = dot_rows(slope_ref[...], jnp.concatenate([high, rest, high], axis=0))
    inverse_jac = [
        [derived_ref[3 * row_id + axis_id : 3 * row_id + axis_id + 1, :] for axis_id in range(3)]
        for row_id in range(3)
    ]

    def gradient(axis_id, comp_id):
        columns = slice(comp_id * new_count, (comp_id + 1) * new_count)
        return (
            inverse_jac[0][axis_id] * slopes[0:24, columns]
            + inverse_jac[1][axis_id] * slopes[24:48, columns]
            + inverse_jac[2][axis_id] * slopes[48:72, columns]
        )

    inverse_eps = derived_ref[9:10, :]
    inverse_mu = derived_ref[10:11, :]
    for axis_id in range(3):
        after, last = (axis_id + 1) % 3, (axis_id + 2) % 3
        curl_h = gradient(after, last) - gradient(last, after)
        curl_e = gradient(after, 3 + last) - gradient(last, 3 + after)
        change_h = (column_block(lifted, axis_id) - curl_e) * inverse_mu
        change_e = (column_block(lifted, 3 + axis_id) + curl_h) * inverse_eps
        part_ref[axis_id] = change_h[:node_count]
        part_ref[3 + axis_id] = change_e[:node_count]


def arrive_kernel(
    came_ref,
    link_ref,
    orient_ref,
    slope_ref,
    lift_ref,
    spread_ref,
    about_ref,
    state_ref,
    derived_ref,
    far_ref,
    part_ref,
    rows_ref,
    tail_ref,
    main_ref,
    *scratches,
):
    derived_ref[...] = jnp.zeros(derived_ref.shape, jnp.float32)
    unpack(came_ref, state_ref, derived_ref, rows_ref, tail_ref, main_ref)
    compact(derived_ref, spread_ref, about_ref, far_ref)
    local_part(state_ref, derived_ref, link_ref, orient_ref, slope_ref, lift_ref, part_ref, *scratches)


def local_kernel(*refs):
    local_part(*refs)


def remote_part(came_ref, far_ref, spread_ref, lift_ref, derived_ref, turned_ref, table_ref, jump_ref, flux_ref):
    turned_ref[...] = jnp.transpose(came_ref[...])
    table_ref[...] = jnp.zeros(table_ref.shape, jnp.float32)
    for half in range(2):
        for node_id in range(face_nodes):
            first_row = half * half_lane + node_id * components
            table_ref[half, 8 * node_id : 8 * node_id + components, :] = turned_ref[
                first_row : first_row + components, :
            ]
    planes = [
        jnp.concatenate(
            [table_ref[half, 8 * node_id : 8 * node_id + 8, :] for half in range(2)], axis=1
        )
        for node_id in range(face_nodes)
    ]
    outside = oriented(planes, far_ref[5:6, :])
    for node_id in range(face_nodes):
        tiled_store(jump_ref, slice(8 * node_id, 8 * node_id + 8), outside[node_id])
    fluxes = face_flux(
        lambda comp_id: strided_load(jump_ref, comp_id, face_nodes, 8),
        [far_ref[axis_id : axis_id + 1, :] for axis_id in range(3)],
        far_ref[3:4, :],
        far_ref[4:5, :],
    )
    flux_ref[...] = jnp.zeros(flux_ref.shape, jnp.float32)
    face = far_ref[6:7, :]
    for face_id in range(faces):
        here = face == face_id
        for comp_id, value in enumerate(fluxes):
            columns = slice(comp_id * remote_count, (comp_id + 1) * remote_count)
            flux_ref[16 * face_id : 16 * face_id + face_nodes, columns] = jnp.where(here, value, 0.0)
    high, rest = split_two(flux_ref[...])
    lifted = dot_rows(lift_ref[...], jnp.concatenate([high, rest, high], axis=0))
    stacked = jnp.concatenate(
        [
            lifted[:24, comp_id * remote_count : (comp_id + 1) * remote_count]
            for comp_id in range(components)
        ],
        axis=0,
    )
    placed = dot_rows(jnp.concatenate(split_two(stacked), axis=0), spread_ref[...])
    rows = 24 * components
    placed = placed[:rows] + placed[rows:]
    inverse_eps = derived_ref[9:10, :]
    inverse_mu = derived_ref[10:11, :]
    return [
        (placed[24 * comp_id : 24 * comp_id + 24] * (inverse_mu if comp_id < 3 else inverse_eps))[
            :node_count
        ]
        for comp_id in range(components)
    ]


def first_kernel(
    came_ref,
    part_ref,
    state_ref,
    derived_ref,
    far_ref,
    spread_ref,
    lift_ref,
    pick_ref,
    face_ref,
    select_ref,
    residual_ref,
    middle_ref,
    trace_ref,
    main_ref,
    *scratches,
):
    changes = remote_part(came_ref, far_ref, spread_ref, lift_ref, derived_ref, *scratches)
    main_ref[components * node_count :, :] = jnp.zeros((8, new_count), jnp.float32)
    for comp_id in range(components):
        residual = time_step * (part_ref[comp_id] + changes[comp_id])
        middle = state_ref[comp_id] + section_b1 * residual
        residual_ref[comp_id] = residual
        middle_ref[comp_id] = middle
        main_ref[comp_id * node_count : (comp_id + 1) * node_count, :] = middle
    parts = jnp.concatenate(split_two(main_ref[...]), axis=0)
    trace_rows(dot_lanes(pick_ref[...], parts), face_ref[...], select_ref, trace_ref)


def second_kernel(
    came_ref,
    part_ref,
    middle_ref,
    first_ref,
    derived_ref,
    far_ref,
    spread_ref,
    lift_ref,
    advanced_ref,
    residual_ref,
    *scratches,
):
    changes = remote_part(came_ref, far_ref, spread_ref, lift_ref, derived_ref, *scratches)
    for comp_id in range(components):
        residual = section_a2 * first_ref[comp_id] + time_step * (
            part_ref[comp_id] + changes[comp_id]
        )
        residual_ref[comp_id] = residual
        advanced_ref[comp_id] = middle_ref[comp_id] + section_b2 * residual


def floats(*shape):
    return jax.ShapeDtypeStruct(shape, jnp.float32)


def near(*shape):
    return pltpu.VMEM(shape, jnp.float32)


def halves(*shape):
    return jax.ShapeDtypeStruct(shape, jnp.bfloat16)


def scratch(*shape):
    return pltpu.VMEM(shape, jnp.float32)


def run(kernel, name, outs, scratches, operands, in_specs=None):
    return pl.pallas_call(
        kernel,
        name=name,
        out_shape=outs,
        in_specs=in_specs or [pl.BlockSpec(memory_space=pltpu.VMEM)] * len(operands),
        scratch_shapes=scratches,
        compiler_params=pltpu.CompilerParams(vmem_limit_bytes=24 * 2**20),
        cost_estimate=pl.CostEstimate(flops=10**8, bytes_accessed=10**6, transcendentals=0),
    )(*operands)


def shards(fields, geometry, migrate_list, trace_list, face_link, face_orient):
    slopes = slope_operand()
    lift = lift_operand()
    remote_lift = remote_lift_operand()
    select = select_operand()
    state_shape = floats(components, node_count, new_count)
    trace_shape = near(remote_count // 2, lane)
    local_scratch = [
        scratch(tiles, 8 * node_count, lane),
        scratch(32, components * new_count),
        scratch(tiles, 8 * faces * face_nodes, lane),
        scratch(48, components * new_count),
    ]
    remote_scratch = [
        scratch(lane, lane),
        scratch(2, 8 * face_nodes, lane),
        scratch(2, 8 * face_nodes, lane),
        scratch(16 * faces, components * remote_count),
    ]
    parcel = run(
        pack_kernel,
        "pack",
        near(slabs * block_rows, lane),
        [
            scratch(components, node_count, old_count),
            scratch(11, old_count),
            pltpu.VMEM((slots, 1, slabs), jnp.int32),
            scratch(144, old_count),
            pltpu.SemaphoreType.DMA((3,)),
        ],
        [
            pltpu.with_memory_space_constraint(operand, pltpu.HBM)
            for operand in (fields, geometry, jnp.transpose(migrate_list, (2, 0, 1)))
        ],
        [pl.BlockSpec(memory_space=pltpu.HBM)] * 3,
    )
    arrived = lax.all_to_all(
        parcel.reshape(slabs, block_rows * lane), "slab", split_axis=0, concat_axis=0, tiled=True,
        axis_index_groups=[slab_order],
    ).reshape(slabs * block_rows, lane)
    came_pick, slot_pick, trace_face, spread, about = run(
        plan_kernel,
        "plan",
        (
            halves(remote_count, 4 * lane),
            halves(remote_count, new_count),
            jax.ShapeDtypeStruct((remote_count, lane), jnp.int32),
            halves(remote_count, new_count),
            floats(8, remote_count),
        ),
        [pltpu.VMEM((remote_count, lane), jnp.int32)],
        (trace_list, face_link, face_orient),
    )
    outgoing = run(
        start_kernel, "start", trace_shape, [], (arrived, came_pick, trace_face, select)
    )

    def exchange(rows):
        blocks = rows.reshape(subs, traces // 2, lane)
        came = lax.all_to_all(
            blocks, "sub", split_axis=0, concat_axis=0, tiled=True, axis_index_groups=[sub_order]
        )
        return came.reshape(remote_count // 2, lane)

    incoming = exchange(outgoing)
    state, derived, far, part = run(
        arrive_kernel,
        "arrive",
        (state_shape, floats(64, new_count), floats(8, remote_count), state_shape),
        [scratch(new_count, lane), scratch(new_count, lane), scratch(lane, new_count)]
        + local_scratch,
        (arrived, face_link, face_orient, slopes, lift, spread, about),
    )
    first_res, middle, outgoing = run(
        first_kernel,
        "first",
        (state_shape, state_shape, trace_shape),
        [scratch(lane, new_count)] + remote_scratch,
        (
            incoming,
            part,
            state,
            derived,
            far,
            spread,
            remote_lift,
            slot_pick,
            trace_face,
            select,
        ),
    )
    incoming = exchange(outgoing)
    part = run(
        local_kernel,
        "local",
        state_shape,
        local_scratch,
        (middle, derived, face_link, face_orient, slopes, lift),
    )
    return run(
        second_kernel,
        "second",
        (state_shape, state_shape),
        remote_scratch,
        (incoming, part, middle, first_res, derived, far, spread, remote_lift),
    )


def solution(mesh):
    return jax.shard_map(
        shards,
        mesh=mesh,
        in_specs=(
            P(None, None, ("slab", "sub")),
            P(None, ("slab", "sub")),
            P(("slab", "sub"), None, None),
            P(("slab", "sub"), None, None),
            P(None, ("slab", "sub")),
            P(None, ("slab", "sub")),
        ),
        out_specs=(P(None, None, ("slab", "sub")), P(None, None, ("slab", "sub"))),
        check_vma=False,
    )
```

```python
import math

import jax
import jax.numpy as jnp
import ml_dtypes
import numpy as np
from jax import lax
from jax.experimental import pallas as pl
from jax.experimental.pallas import tpu as pltpu
from jax.sharding import PartitionSpec as P

time_step = 0.004
section_a2 = -0.4178904745
section_b1 = 0.1496590219993
section_b2 = 0.3792103129999
coordinate_perms = ((0, 1, 2), (1, 2, 0), (2, 0, 1), (0, 2, 1), (2, 1, 0), (1, 0, 2))
components = 6
node_count = 20
face_nodes = 10
faces = 4
old_count = 256
slots = 12
slabs = 32
subs = 16
traces = 16
new_count = slots * slabs
column_count = faces * new_count
remote_count = subs * traces
lane = 128
half_lane = lane // 2
tiles = new_count // lane
block_rows = slots + 1
slab_first = 21
sub_first = 10
slab_order = [(slab_first + place) % slabs for place in range(slabs)]
sub_order = [(sub_first + place) % subs for place in range(subs)]


def volume_triples():
    result_list = []
    for first_idx in range(4):
        for second_idx in range(4 - first_idx):
            for third_idx in range(4 - first_idx - second_idx):
                result_list.append((first_idx, second_idx, third_idx))
    return result_list


def planar_pairs():
    result_list = []
    for first_idx in range(4):
        for second_idx in range(4 - first_idx):
            result_list.append((first_idx, second_idx))
    return result_list


def monomial_matrix(points, powers):
    result_rows = []
    for point_item in points:
        row_values = []
        for power_item in powers:
            product_value = 1.0
            for axis_id in range(len(power_item)):
                product_value = product_value * point_item[axis_id] ** power_item[axis_id]
            row_values.append(product_value)
        result_rows.append(row_values)
    return result_rows


def mat_mul(left_rows, right_rows):
    inner_count = len(right_rows)
    col_count = len(right_rows[0])
    return [
        [
            sum((left_row[k_id] * right_rows[k_id][c_id] for k_id in range(inner_count)))
            for c_id in range(col_count)
        ]
        for left_row in left_rows
    ]


def transposed(matrix_rows):
    return [list(row_item) for row_item in zip(*matrix_rows)]


def invert(matrix_rows):
    order = len(matrix_rows)
    work_rows = [
        list(matrix_rows[r_id]) + [1.0 if r_id == c_id else 0.0 for c_id in range(order)]
        for r_id in range(order)
    ]
    for col_id in range(order):
        pivot_row = max(range(col_id, order), key=lambda r_id: abs(work_rows[r_id][col_id]))
        work_rows[col_id], work_rows[pivot_row] = (work_rows[pivot_row], work_rows[col_id])
        pivot_value = work_rows[col_id][col_id]
        work_rows[col_id] = [value / pivot_value for value in work_rows[col_id]]
        for r_id in range(order):
            if r_id != col_id:
                factor = work_rows[r_id][col_id]
                if factor != 0.0:
                    work_rows[r_id] = [
                        work_rows[r_id][c_id] - factor * work_rows[col_id][c_id]
                        for c_id in range(2 * order)
                    ]
    return [row_item[order:] for row_item in work_rows]


def moment_matrix(powers, extra_dim):
    total_terms = len(powers)
    result_matrix = [[0.0] * total_terms for _ in range(total_terms)]
    for row_id in range(total_terms):
        for col_id in range(total_terms):
            joined = [
                powers[row_id][a_id] + powers[col_id][a_id] for a_id in range(len(powers[row_id]))
            ]
            numerator = 1.0
            for exponent in joined:
                numerator = numerator * math.factorial(exponent)
            result_matrix[row_id][col_id] = numerator / math.factorial(sum(joined) + extra_dim)
    return result_matrix


def dg_tables():
    triples = volume_triples()
    points = [tuple((value / 3.0 for value in triple)) for triple in triples]
    inverse = invert(monomial_matrix(points, triples))
    slopes = []
    for axis_id in range(3):
        lowered = [
            tuple(
                (max(triple[a_id] - 1, 0) if a_id == axis_id else triple[a_id] for a_id in range(3))
            )
            for triple in triples
        ]
        base_rows = monomial_matrix(points, lowered)
        slope_values = [
            [triples[c_id][axis_id] * base_rows[r_id][c_id] for c_id in range(20)]
            for r_id in range(20)
        ]
        slopes.append(mat_mul(slope_values, inverse))
    volume_mass = mat_mul(mat_mul(transposed(inverse), moment_matrix(triples, 3)), inverse)
    planar = planar_pairs()
    face_points = [tuple((value / 3.0 for value in pair_item)) for pair_item in planar]
    face_inverse = invert(monomial_matrix(face_points, planar))
    face_mass = mat_mul(mat_mul(transposed(face_inverse), moment_matrix(planar, 2)), face_inverse)
    face_axes = ((0, 1), (0, 2), (0, 1), (1, 2))
    face_mask = [[0] * 10 for _ in range(4)]
    for face_id in range(4):
        for node_id, triple in enumerate(triples):
            on_face = (
                triple[2] == 0,
                triple[1] == 0,
                triple[0] + triple[1] + triple[2] == 3,
                triple[0] == 0,
            )[face_id]
            if on_face:
                key_pair = (triple[face_axes[face_id][0]], triple[face_axes[face_id][1]])
                face_mask[face_id][planar.index(key_pair)] = node_id
    surface = [[0.0] * 40 for _ in range(20)]
    for face_id in range(4):
        for row_id in range(10):
            for col_id in range(10):
                surface[face_mask[face_id][row_id]][face_id * 10 + col_id] += face_mass[row_id][
                    col_id
                ]
    lifting = mat_mul(invert(volume_mass), surface)
    lift_alt = [
        [lifting[n_id][f_id * 10 + j_id] for j_id in range(10) for f_id in range(4)]
        for n_id in range(20)
    ]
    node_perms = []
    for turn_id in range(6):
        perm_row = []
        for pair_item in planar:
            triple_face = (pair_item[0], pair_item[1], 3 - pair_item[0] - pair_item[1])
            moved_triple = [triple_face[coordinate_perms[turn_id][axis_id]] for axis_id in range(3)]
            perm_row.append(planar.index((moved_triple[0], moved_triple[1])))
        node_perms.append(perm_row)
    node_picks = [face_mask[f_id][j_id] for j_id in range(10) for f_id in range(4)]
    return slopes, lifting, face_mask, node_perms


def bf16_pair(matrix):
    wide = np.asarray(matrix, np.float32)
    high = wide.astype(ml_dtypes.bfloat16)
    rest = (wide - high.astype(np.float32)).astype(ml_dtypes.bfloat16)
    return high, rest


slope_table, lift_table, face_mask, node_perms = dg_tables()


def slope_operand():
    stacked = np.zeros((80, 32), np.float64)
    for axis_id in range(3):
        first_row = axis_id * 24
        stacked[first_row : first_row + node_count, :node_count] = slope_table[axis_id]
    high, rest = bf16_pair(stacked)
    return jnp.asarray(np.concatenate([high, high, rest], axis=1))


def lift_operand():
    stacked = np.zeros((32, 48), np.float64)
    for face_id in range(faces):
        for node_id in range(face_nodes):
            for row_id in range(node_count):
                stacked[row_id, node_id * faces + face_id] = lift_table[row_id][
                    face_id * face_nodes + node_id
                ]
    high, rest = bf16_pair(stacked)
    return jnp.asarray(np.concatenate([high, high, rest], axis=1))


def remote_lift_operand():
    stacked = np.zeros((24 * faces, 16), np.float64)
    for face_id in range(faces):
        for node_id in range(face_nodes):
            for row_id in range(node_count):
                stacked[24 * face_id + row_id, node_id] = lift_table[row_id][
                    face_id * face_nodes + node_id
                ]
    high, rest = bf16_pair(stacked)
    return jnp.asarray(np.concatenate([high, high, rest], axis=1))


def select_operand():
    table = np.zeros((2 * lane, faces * half_lane), np.float32)
    for face_id in range(faces):
        for part_id in range(2):
            for node_id in range(face_nodes):
                for comp_id in range(components):
                    row_id = part_id * lane + comp_id * node_count + face_mask[face_id][node_id]
                    table[row_id, face_id * half_lane + node_id * components + comp_id] = 1.0
    return jnp.asarray(table.astype(ml_dtypes.bfloat16))


def split_two(value):
    high = value.astype(jnp.bfloat16)
    rest = (value - high.astype(jnp.float32)).astype(jnp.bfloat16)
    return high, rest


def dot_rows(left, right):
    return lax.dot_general(
        left, right, (((1,), (0,)), ((), ())), preferred_element_type=jnp.float32
    )


def dot_lanes(left, right):
    return lax.dot_general(
        left, right, (((1,), (1,)), ((), ())), preferred_element_type=jnp.float32
    )


def one_hot(mask):
    return jnp.where(mask, 1.0, 0.0).astype(jnp.bfloat16)


def face_of(codes):
    return sum((codes >= step * new_count).astype(jnp.int32) for step in range(1, faces))


def pack_kernel(fields_ref, geometry_ref, list_ref, out_ref, took_ref, geo_ref, codes_ref, held_ref, sems):
    field_rows = components * node_count
    copies = [
        pltpu.make_async_copy(list_ref, codes_ref, sems.at[0]),
        pltpu.make_async_copy(fields_ref, took_ref, sems.at[1]),
        pltpu.make_async_copy(geometry_ref, geo_ref, sems.at[2]),
    ]
    for copy in copies:
        copy.start()
    copies[0].wait()
    turned = jnp.concatenate([codes_ref[slot_id] for slot_id in range(slots)], axis=0)
    turned = jnp.concatenate([turned, jnp.zeros((lane - slots, slabs), jnp.int32)], axis=0)
    turned = jnp.concatenate([turned, jnp.zeros((lane, lane - slabs), jnp.int32)], axis=1)
    codes = jnp.transpose(turned)[:slabs]
    codes = jnp.concatenate([codes[slab_first:], codes[:slab_first]], axis=0)
    lanes = lax.broadcasted_iota(jnp.int32, (slabs, old_count), 1)
    picks = jnp.concatenate(
        [one_hot(codes[:, slot_id : slot_id + 1] == lanes) for slot_id in range(slots)], axis=0
    )
    copies[1].wait()
    copies[2].wait()
    for comp_id in range(components):
        held_ref[comp_id * node_count : (comp_id + 1) * node_count, :] = took_ref[comp_id]
    held_ref[field_rows : field_rows + 11, :] = geo_ref[...]
    held_ref[field_rows + 11 :, :] = jnp.zeros((13, old_count), jnp.float32)
    parts = jnp.concatenate(split_two(held_ref[...]), axis=1)
    parts = jnp.concatenate([parts, jnp.zeros((112, 2 * old_count), jnp.bfloat16)], axis=0)
    moved = dot_lanes(jnp.concatenate([picks, picks], axis=1), parts)
    short = lax.broadcasted_iota(jnp.int32, (slabs, lane), 1)
    diagonal = (short == field_rows) | (short == field_rows + 4)
    tail = jnp.zeros((slabs, lane), jnp.float32)
    for slot_id in range(slots):
        empty = codes[:, slot_id : slot_id + 1] < 0
        block = moved[slot_id * slabs : (slot_id + 1) * slabs]
        out_ref[pl.ds(slot_id, slabs, stride=block_rows), :] = jnp.where(
            empty & diagonal, 1.0, block[:, :lane]
        )
        ending = jnp.where(empty & (short < 3), 1.0, block[:, lane:])
        if slot_id:
            ending = pltpu.roll(ending, 3 * slot_id, 1)
        tail = tail + ending
    out_ref[pl.ds(slots, slabs, stride=block_rows), :] = tail


def trace_codes(list_ref, codes_ref):
    codes = list_ref[0]
    codes = jnp.concatenate([codes[sub_first:], codes[:sub_first]], axis=0)
    half = traces // 2
    for idx in range(traces):
        rows = pl.ds((idx // half) * lane + idx % half, subs, stride=half)
        codes_ref[rows, :] = jnp.broadcast_to(codes[:, idx : idx + 1], (subs, lane))
    codes = codes_ref[...]
    face = face_of(codes)
    return face, codes - new_count * face


def lane_picks(chosen, count):
    lanes = lax.broadcasted_iota(jnp.int32, (remote_count, lane), 1)
    return jnp.concatenate(
        [one_hot(chosen == lanes + tile * lane) for tile in range(count)], axis=1
    )


def plan(list_ref, link_ref, orient_ref, slot_pick_ref, face_ref, spread_ref, about_ref, codes_ref):
    face, element = trace_codes(list_ref, codes_ref)
    face_ref[...] = face
    slot_pick_ref[...] = lane_picks(element, tiles)
    rows = lax.broadcasted_iota(jnp.int32, (remote_count, new_count), 0)
    about_rows = lax.broadcasted_iota(jnp.int32, (16, new_count), 0)
    about = None
    spread = None
    for face_id in range(faces):
        far = link_ref[face_id : face_id + 1, :] - column_count
        orient = orient_ref[face_id : face_id + 1, :]
        place = ((far >> 4) + subs - sub_first) & (subs - 1)
        column = ((far >> 3) & 1) * lane + place * 8 + (far & 7)
        column = jnp.where((far >= 0) & (orient < 6), column, -1)
        picks = one_hot(rows == column)
        facts = jnp.where(about_rows == 0, orient, jnp.where(about_rows == 1, face_id, 0))
        term = dot_lanes(facts.astype(jnp.float32).astype(jnp.bfloat16), picks)
        about = term if about is None else about + term
        spread = picks if spread is None else spread + picks
    spread_ref[...] = spread
    about_ref[...] = about[:8]


def trace_rows(found, face, select_ref, trace_ref):
    wide = dot_rows(found.astype(jnp.bfloat16), select_ref[...])
    near = jnp.where(face >= 2, wide[:, lane:], wide[:, :lane])
    odd = (face & 1) == 1
    half = remote_count // 2
    upper, lower = near[:half], near[half:]
    upper = jnp.where(odd[:half], pltpu.roll(upper, half_lane, 1), upper)
    lower = jnp.where(odd[half:], lower, pltpu.roll(lower, half_lane, 1))
    lanes = lax.broadcasted_iota(jnp.int32, (half, lane), 1)
    trace_ref[...] = jnp.where(lanes < half_lane, upper, lower)


def start_kernel(came_ref, list_ref, select_ref, trace_ref, codes_ref):
    face, element = trace_codes(list_ref, codes_ref)
    source = (element * 5462) >> 16
    place = (source + slabs - slab_first) & (slabs - 1)
    picks = lane_picks(place * block_rows + element - source * slots, tiles + 1)
    parts = jnp.concatenate(split_two(came_ref[...]), axis=1)
    parts = jnp.concatenate(
        [parts, jnp.zeros((4 * lane - slabs * block_rows, 2 * lane), jnp.bfloat16)], axis=0
    )
    trace_rows(dot_rows(picks, parts), face, select_ref, trace_ref)


def unpack(came_ref, state_ref, derived_ref, rows_ref, tail_ref, main_ref):
    field_rows = components * node_count
    runs = ((slab_first, 0, slabs - slab_first), (0, slabs - slab_first, slab_first))
    tail = jnp.concatenate(
        [
            came_ref[pl.ds(place * block_rows + slots, count, stride=block_rows), :]
            for _, place, count in reversed(runs)
        ],
        axis=0,
    )
    for slot_id in range(slots):
        for source, place, count in runs:
            rows_ref[pl.ds(source * slots + slot_id, count, stride=slots), :] = came_ref[
                pl.ds(place * block_rows + slot_id, count, stride=block_rows), :
            ]
        shifted = pltpu.roll(tail, lane - 3 * slot_id, 1) if slot_id else tail
        tail_ref[pl.ds(slot_id, slabs, stride=slots), :] = shifted
    main_ref[...] = jnp.transpose(rows_ref[...])
    extra = jnp.transpose(tail_ref[...])[:8]
    for comp_id in range(components):
        state_ref[comp_id] = main_ref[comp_id * node_count : (comp_id + 1) * node_count, :]
    geo = [main_ref[field_rows + row_id : field_rows + row_id + 1, :] for row_id in range(8)]
    geo.append(extra[0:1])
    derived_ref[0:8, :] = main_ref[field_rows : field_rows + 8, :]
    derived_ref[8:9, :] = extra[0:1]
    derived_ref[9:10, :] = 1.0 / extra[1:2]
    derived_ref[10:11, :] = 1.0 / extra[2:3]
    total = None
    for axis_id in range(3):
        first, second, third = geo[axis_id], geo[3 + axis_id], geo[6 + axis_id]
        normal = 0.5 * jnp.concatenate([-third, -second, first + second + third, -first], axis=0)
        square = normal * normal
        total = square if total is None else total + square
        normal_rows = jnp.concatenate([normal, normal], axis=0)
        derived_ref[16 + 8 * axis_id : 24 + 8 * axis_id, :] = normal_rows
    length = jnp.sqrt(total)
    derived_ref[40:48, :] = jnp.concatenate([length, length], axis=0)
    inverse = 1.0 / length
    derived_ref[48:56, :] = jnp.concatenate([inverse, inverse], axis=0)


def compact(derived_ref, spread_ref, about_ref, far_ref):
    stacked = jnp.concatenate(split_two(derived_ref[16:64, :]), axis=0)
    found = dot_lanes(stacked, spread_ref[...])
    found = found[:48] + found[48:]
    face = about_ref[1:2, :]
    for block in range(5):
        first_row = 8 * block
        value = found[first_row : first_row + 1]
        for face_id in range(1, faces):
            row_id = first_row + face_id
            value = jnp.where(face == face_id, found[row_id : row_id + 1], value)
        far_ref[block : block + 1, :] = value
    far_ref[5:7, :] = about_ref[0:2, :]
    far_ref[7:8, :] = jnp.zeros((1, remote_count), jnp.float32)


def oriented(planes, orient):
    masks = [orient == turn_id for turn_id in range(6)]
    result = []
    for node_id in range(face_nodes):
        sources = {}
        for turn_id in range(6):
            sources.setdefault(node_perms[turn_id][node_id], []).append(turn_id)
        value = None
        for source, turn_ids in sources.items():
            if value is None:
                value = planes[source]
                continue
            mask = masks[turn_ids[0]]
            for turn_id in turn_ids[1:]:
                mask = mask | masks[turn_id]
            value = jnp.where(mask, planes[source], value)
        result.append(value)
    return result


def face_flux(jump_of, normal, length, inverse):
    jump_h = [jump_of(comp_id) for comp_id in range(3)]
    jump_e = [jump_of(comp_id) for comp_id in range(3, 6)]

    def along(jump):
        total = normal[0] * jump[0] + normal[1] * jump[1] + normal[2] * jump[2]
        return total * inverse

    along_h = along(jump_h)
    along_e = along(jump_e)
    flux_h, flux_e = [], []
    for axis_id in range(3):
        after, last = (axis_id + 1) % 3, (axis_id + 2) % 3
        cross_e = normal[after] * jump_e[last] - normal[last] * jump_e[after]
        cross_h = normal[after] * jump_h[last] - normal[last] * jump_h[after]
        flux_h.append(length * jump_h[axis_id] - normal[axis_id] * along_h - cross_e)
        flux_e.append(length * jump_e[axis_id] - normal[axis_id] * along_e + cross_h)
    return flux_h + flux_e


def lifted_flux(jump_ref, flux_ref, derived_ref, lift_ref):
    groups = faces * face_nodes // 8

    def jump_of(comp_id):
        rows = strided_load(jump_ref, comp_id, faces * face_nodes, 8)
        return rows.reshape(groups, 8, new_count)

    normal = [derived_ref[16 + 8 * axis_id : 24 + 8 * axis_id, :][None] for axis_id in range(3)]
    fluxes = face_flux(jump_of, normal, derived_ref[40:48, :][None], derived_ref[48:56, :][None])
    for comp_id, value in enumerate(fluxes):
        flux_ref[0:40, comp_id * new_count : (comp_id + 1) * new_count] = value.reshape(
            faces * face_nodes, new_count
        )
    flux_ref[40:48, :] = jnp.zeros((8, components * new_count), jnp.float32)
    high, rest = split_two(flux_ref[...])
    return dot_rows(lift_ref[...], jnp.concatenate([high, rest, high], axis=0))


def strided_load(ref, start, size, stride):
    return jnp.concatenate(
        [ref[tile, pl.ds(start, size, stride=stride), :] for tile in range(ref.shape[0])], axis=1
    )


def tiled_store(ref, rows, value):
    for tile in range(ref.shape[0]):
        ref[tile, rows, :] = value[:, tile * lane : (tile + 1) * lane]


def tiled_load(ref, rows):
    return jnp.concatenate([ref[tile, rows, :] for tile in range(tiles)], axis=1)


def column_block(matrix, comp_id):
    return matrix[:24, comp_id * new_count : (comp_id + 1) * new_count]


def local_part(
    state_ref, derived_ref, link_ref, orient_ref, slope_ref, lift_ref, part_ref, nodes_ref, flat_ref, jump_ref, flux_ref
):
    nodes_ref[...] = jnp.zeros(nodes_ref.shape, jnp.float32)
    flat_ref[node_count:32, :] = jnp.zeros((12, components * new_count), jnp.float32)
    for comp_id in range(components):
        current = state_ref[comp_id]
        tiled_store(nodes_ref, pl.ds(comp_id, node_count, stride=8), current)
        flat_ref[0:node_count, comp_id * new_count : (comp_id + 1) * new_count] = current
    stacked = jnp.concatenate(split_two(tiled_load(nodes_ref, slice(None))), axis=0)
    rows = lax.broadcasted_iota(jnp.int32, (new_count, new_count), 0)
    comp_rows = lax.broadcasted_iota(jnp.int32, (8, new_count), 0)
    wall_gain = jnp.where(comp_rows >= 3, -2.0, 0.0)
    for face_id in range(faces):
        link = link_ref[face_id : face_id + 1, :]
        orient = orient_ref[face_id : face_id + 1, :]
        owner = face_of(link)
        element = jnp.where(link < column_count, link - new_count * owner, -1)
        found = dot_rows(stacked, one_hot(rows == element))
        found = found[: 8 * node_count] + found[8 * node_count :]
        owner_masks = [owner == other for other in range(faces)]
        planes = []
        for node_id in range(face_nodes):
            value = None
            for other in range(faces):
                first_row = 8 * face_mask[other][node_id]
                plane = found[first_row : first_row + 8]
                value = plane if value is None else jnp.where(owner_masks[other], plane, value)
            planes.append(value)
        outside = oriented(planes, orient)
        wall = orient == 6
        for node_id in range(face_nodes):
            first_row = 8 * face_mask[face_id][node_id]
            inside = tiled_load(nodes_ref, slice(first_row, first_row + 8))
            jump = jnp.where(wall, wall_gain * inside, outside[node_id] - inside)
            target = 8 * (node_id * faces + face_id)
            tiled_store(jump_ref, slice(target, target + 8), jump)
    lifted = lifted_flux(jump_ref, flux_ref, derived_ref, lift_ref)
    high, rest = split_two(flat_ref[...])
    slopes = dot_rows(slope_ref[...], jnp.concatenate([high, rest, high], axis=0))
    inverse_jac = [
        [derived_ref[3 * row_id + axis_id : 3 * row_id + axis_id + 1, :] for axis_id in range(3)]
        for row_id in range(3)
    ]

    def gradient(axis_id, comp_id):
        columns = slice(comp_id * new_count, (comp_id + 1) * new_count)
        return (
            inverse_jac[0][axis_id] * slopes[0:24, columns]
            + inverse_jac[1][axis_id] * slopes[24:48, columns]
            + inverse_jac[2][axis_id] * slopes[48:72, columns]
        )

    inverse_eps = derived_ref[9:10, :]
    inverse_mu = derived_ref[10:11, :]
    for axis_id in range(3):
        after, last = (axis_id + 1) % 3, (axis_id + 2) % 3
        curl_h = gradient(after, last) - gradient(last, after)
        curl_e = gradient(after, 3 + last) - gradient(last, 3 + after)
        change_h = (column_block(lifted, axis_id) - curl_e) * inverse_mu
        change_e = (column_block(lifted, 3 + axis_id) + curl_h) * inverse_eps
        part_ref[axis_id] = change_h[:node_count]
        part_ref[3 + axis_id] = change_e[:node_count]


def arrive_kernel(
    came_ref,
    link_ref,
    orient_ref,
    slope_ref,
    lift_ref,
    list_ref,
    state_ref,
    derived_ref,
    far_ref,
    part_ref,
    slot_pick_ref,
    face_ref,
    spread_ref,
    rows_ref,
    tail_ref,
    main_ref,
    about_ref,
    codes_ref,
    *scratches,
):
    plan(list_ref, link_ref, orient_ref, slot_pick_ref, face_ref, spread_ref, about_ref, codes_ref)
    derived_ref[...] = jnp.zeros(derived_ref.shape, jnp.float32)
    unpack(came_ref, state_ref, derived_ref, rows_ref, tail_ref, main_ref)
    compact(derived_ref, spread_ref, about_ref, far_ref)
    local_part(state_ref, derived_ref, link_ref, orient_ref, slope_ref, lift_ref, part_ref, *scratches)


def local_kernel(*refs):
    local_part(*refs)


def remote_part(came_ref, far_ref, spread_ref, lift_ref, derived_ref, turned_ref, jump_ref):
    turned_ref[...] = jnp.transpose(came_ref[...])
    planes = []
    for node_id in range(face_nodes):
        first_row = node_id * components
        halves_of = [
            turned_ref[half * half_lane + first_row : half * half_lane + first_row + 8, :]
            for half in range(2)
        ]
        planes.append(jnp.concatenate(halves_of, axis=1))
    outside = oriented(planes, far_ref[5:6, :])
    for node_id in range(face_nodes):
        tiled_store(jump_ref, slice(8 * node_id, 8 * node_id + 8), outside[node_id])
    blank = jnp.zeros((8 * (16 - face_nodes), remote_count), jnp.float32)
    tiled_store(jump_ref, slice(8 * face_nodes, 128), blank)
    fluxes = face_flux(
        lambda comp_id: strided_load(jump_ref, comp_id, 16, 8),
        [far_ref[axis_id : axis_id + 1, :] for axis_id in range(3)],
        far_ref[3:4, :],
        far_ref[4:5, :],
    )
    high, rest = split_two(jnp.concatenate(fluxes, axis=1))
    lifted = dot_rows(lift_ref[...], jnp.concatenate([high, rest, high], axis=0))
    face = far_ref[6:7, :]
    blocks = []
    for comp_id in range(components):
        columns = slice(comp_id * remote_count, (comp_id + 1) * remote_count)
        block = lifted[:24, columns]
        for face_id in range(1, faces):
            block = jnp.where(
                face == face_id, lifted[24 * face_id : 24 * face_id + 24, columns], block
            )
        blocks.append(block)
    stacked = jnp.concatenate(blocks, axis=0)
    placed = dot_rows(jnp.concatenate(split_two(stacked), axis=0), spread_ref[...])
    rows = 24 * components
    placed = placed[:rows] + placed[rows:]
    inverse_eps = derived_ref[9:10, :]
    inverse_mu = derived_ref[10:11, :]
    return [
        (placed[24 * comp_id : 24 * comp_id + 24] * (inverse_mu if comp_id < 3 else inverse_eps))[
            :node_count
        ]
        for comp_id in range(components)
    ]


def first_kernel(
    came_ref,
    part_ref,
    state_ref,
    derived_ref,
    far_ref,
    spread_ref,
    lift_ref,
    pick_ref,
    face_ref,
    select_ref,
    residual_ref,
    middle_ref,
    trace_ref,
    main_ref,
    *scratches,
):
    changes = remote_part(came_ref, far_ref, spread_ref, lift_ref, derived_ref, *scratches)
    main_ref[components * node_count :, :] = jnp.zeros((8, new_count), jnp.float32)
    for comp_id in range(components):
        residual = time_step * (part_ref[comp_id] + changes[comp_id])
        middle = state_ref[comp_id] + section_b1 * residual
        residual_ref[comp_id] = residual
        middle_ref[comp_id] = middle
        main_ref[comp_id * node_count : (comp_id + 1) * node_count, :] = middle
    parts = jnp.concatenate(split_two(main_ref[...]), axis=0)
    trace_rows(dot_lanes(pick_ref[...], parts), face_ref[...], select_ref, trace_ref)


def second_kernel(
    came_ref,
    part_ref,
    middle_ref,
    first_ref,
    derived_ref,
    far_ref,
    spread_ref,
    lift_ref,
    advanced_ref,
    residual_ref,
    *scratches,
):
    changes = remote_part(came_ref, far_ref, spread_ref, lift_ref, derived_ref, *scratches)
    for comp_id in range(components):
        residual = section_a2 * first_ref[comp_id] + time_step * (
            part_ref[comp_id] + changes[comp_id]
        )
        residual_ref[comp_id] = residual
        advanced_ref[comp_id] = middle_ref[comp_id] + section_b2 * residual


def floats(*shape):
    return jax.ShapeDtypeStruct(shape, jnp.float32)


def near(*shape):
    return pltpu.VMEM(shape, jnp.float32)


def halves(*shape):
    return jax.ShapeDtypeStruct(shape, jnp.bfloat16)


def scratch(*shape):
    return pltpu.VMEM(shape, jnp.float32)


def run(kernel, name, outs, scratches, operands, in_specs=None):
    return pl.pallas_call(
        kernel,
        name=name,
        out_shape=outs,
        in_specs=in_specs or [pl.BlockSpec(memory_space=pltpu.VMEM)] * len(operands),
        scratch_shapes=scratches,
        compiler_params=pltpu.CompilerParams(vmem_limit_bytes=24 * 2**20),
        cost_estimate=pl.CostEstimate(flops=10**8, bytes_accessed=10**6, transcendentals=0),
    )(*operands)


def shards(fields, geometry, migrate_list, trace_list, face_link, face_orient):
    slopes = slope_operand()
    lift = lift_operand()
    remote_lift = remote_lift_operand()
    select = select_operand()
    state_shape = floats(components, node_count, new_count)
    trace_shape = near(remote_count // 2, lane)
    local_scratch = [
        scratch(tiles, 8 * node_count, lane),
        scratch(32, components * new_count),
        scratch(tiles, 8 * faces * face_nodes, lane),
        scratch(48, components * new_count),
    ]
    remote_scratch = [scratch(lane, lane), scratch(2, lane, lane)]
    parcel = run(
        pack_kernel,
        "pack",
        near(slabs * block_rows, lane),
        [
            scratch(components, node_count, old_count),
            scratch(11, old_count),
            pltpu.VMEM((slots, 1, slabs), jnp.int32),
            scratch(144, old_count),
            pltpu.SemaphoreType.DMA((3,)),
        ],
        [
            pltpu.with_memory_space_constraint(operand, pltpu.HBM)
            for operand in (fields, geometry, jnp.transpose(migrate_list, (2, 0, 1)))
        ],
        [pl.BlockSpec(memory_space=pltpu.HBM)] * 3,
    )
    arrived = lax.all_to_all(
        parcel.reshape(slabs, block_rows * lane), "slab", split_axis=0, concat_axis=0, tiled=True,
        axis_index_groups=[slab_order],
    ).reshape(slabs * block_rows, lane)
    code_scratch = pltpu.VMEM((remote_count, lane), jnp.int32)
    outgoing = run(
        start_kernel, "start", trace_shape, [code_scratch], (arrived, trace_list, select)
    )

    def exchange(rows):
        blocks = rows.reshape(subs, traces // 2, lane)
        came = lax.all_to_all(
            blocks, "sub", split_axis=0, concat_axis=0, tiled=True, axis_index_groups=[sub_order]
        )
        return came.reshape(remote_count // 2, lane)

    incoming = exchange(outgoing)
    state, derived, far, part, slot_pick, trace_face, spread = run(
        arrive_kernel,
        "arrive",
        (
            state_shape,
            floats(64, new_count),
            floats(8, remote_count),
            state_shape,
            halves(remote_count, new_count),
            jax.ShapeDtypeStruct((remote_count, lane), jnp.int32),
            halves(remote_count, new_count),
        ),
        [
            scratch(new_count, lane),
            scratch(new_count, lane),
            scratch(lane, new_count),
            scratch(8, remote_count),
            code_scratch,
        ]
        + local_scratch,
        (arrived, face_link, face_orient, slopes, lift, trace_list),
    )
    first_res, middle, outgoing = run(
        first_kernel,
        "first",
        (state_shape, state_shape, trace_shape),
        [scratch(lane, new_count)] + remote_scratch,
        (
            incoming,
            part,
            state,
            derived,
            far,
            spread,
            remote_lift,
            slot_pick,
            trace_face,
            select,
        ),
    )
    incoming = exchange(outgoing)
    part = run(
        local_kernel,
        "local",
        state_shape,
        local_scratch,
        (middle, derived, face_link, face_orient, slopes, lift),
    )
    return run(
        second_kernel,
        "second",
        (state_shape, state_shape),
        remote_scratch,
        (incoming, part, middle, first_res, derived, far, spread, remote_lift),
    )


def solution(mesh):
    return jax.shard_map(
        shards,
        mesh=mesh,
        in_specs=(
            P(None, None, ("slab", "sub")),
            P(None, ("slab", "sub")),
            P(("slab", "sub"), None, None),
            P(("slab", "sub"), None, None),
            P(None, ("slab", "sub")),
            P(None, ("slab", "sub")),
        ),
        out_specs=(P(None, None, ("slab", "sub")), P(None, None, ("slab", "sub"))),
        check_vma=False,
    )
```

```python
import math

import jax
import jax.numpy as jnp
import ml_dtypes
import numpy as np
from jax import lax
from jax.experimental import pallas as pl
from jax.experimental.pallas import tpu as pltpu
from jax.sharding import PartitionSpec as P

time_step = 0.004
section_a2 = -0.4178904745
section_b1 = 0.1496590219993
section_b2 = 0.3792103129999
coordinate_perms = ((0, 1, 2), (1, 2, 0), (2, 0, 1), (0, 2, 1), (2, 1, 0), (1, 0, 2))
components = 6
node_count = 20
face_nodes = 10
faces = 4
old_count = 256
slots = 12
slabs = 32
subs = 16
traces = 16
new_count = slots * slabs
column_count = faces * new_count
remote_count = subs * traces
lane = 128
half_lane = lane // 2
tiles = new_count // lane
block_rows = slots + 1
slab_first = 21
sub_first = 10
slab_order = [(slab_first + place) % slabs for place in range(slabs)]
sub_order = [(sub_first + place) % subs for place in range(subs)]


def volume_triples():
    result_list = []
    for first_idx in range(4):
        for second_idx in range(4 - first_idx):
            for third_idx in range(4 - first_idx - second_idx):
                result_list.append((first_idx, second_idx, third_idx))
    return result_list


def planar_pairs():
    result_list = []
    for first_idx in range(4):
        for second_idx in range(4 - first_idx):
            result_list.append((first_idx, second_idx))
    return result_list


def monomial_matrix(points, powers):
    result_rows = []
    for point_item in points:
        row_values = []
        for power_item in powers:
            product_value = 1.0
            for axis_id in range(len(power_item)):
                product_value = product_value * point_item[axis_id] ** power_item[axis_id]
            row_values.append(product_value)
        result_rows.append(row_values)
    return result_rows


def mat_mul(left_rows, right_rows):
    inner_count = len(right_rows)
    col_count = len(right_rows[0])
    return [
        [
            sum((left_row[k_id] * right_rows[k_id][c_id] for k_id in range(inner_count)))
            for c_id in range(col_count)
        ]
        for left_row in left_rows
    ]


def transposed(matrix_rows):
    return [list(row_item) for row_item in zip(*matrix_rows)]


def invert(matrix_rows):
    order = len(matrix_rows)
    work_rows = [
        list(matrix_rows[r_id]) + [1.0 if r_id == c_id else 0.0 for c_id in range(order)]
        for r_id in range(order)
    ]
    for col_id in range(order):
        pivot_row = max(range(col_id, order), key=lambda r_id: abs(work_rows[r_id][col_id]))
        work_rows[col_id], work_rows[pivot_row] = (work_rows[pivot_row], work_rows[col_id])
        pivot_value = work_rows[col_id][col_id]
        work_rows[col_id] = [value / pivot_value for value in work_rows[col_id]]
        for r_id in range(order):
            if r_id != col_id:
                factor = work_rows[r_id][col_id]
                if factor != 0.0:
                    work_rows[r_id] = [
                        work_rows[r_id][c_id] - factor * work_rows[col_id][c_id]
                        for c_id in range(2 * order)
                    ]
    return [row_item[order:] for row_item in work_rows]


def moment_matrix(powers, extra_dim):
    total_terms = len(powers)
    result_matrix = [[0.0] * total_terms for _ in range(total_terms)]
    for row_id in range(total_terms):
        for col_id in range(total_terms):
            joined = [
                powers[row_id][a_id] + powers[col_id][a_id] for a_id in range(len(powers[row_id]))
            ]
            numerator = 1.0
            for exponent in joined:
                numerator = numerator * math.factorial(exponent)
            result_matrix[row_id][col_id] = numerator / math.factorial(sum(joined) + extra_dim)
    return result_matrix


def dg_tables():
    triples = volume_triples()
    points = [tuple((value / 3.0 for value in triple)) for triple in triples]
    inverse = invert(monomial_matrix(points, triples))
    slopes = []
    for axis_id in range(3):
        lowered = [
            tuple(
                (max(triple[a_id] - 1, 0) if a_id == axis_id else triple[a_id] for a_id in range(3))
            )
            for triple in triples
        ]
        base_rows = monomial_matrix(points, lowered)
        slope_values = [
            [triples[c_id][axis_id] * base_rows[r_id][c_id] for c_id in range(20)]
            for r_id in range(20)
        ]
        slopes.append(mat_mul(slope_values, inverse))
    volume_mass = mat_mul(mat_mul(transposed(inverse), moment_matrix(triples, 3)), inverse)
    planar = planar_pairs()
    face_points = [tuple((value / 3.0 for value in pair_item)) for pair_item in planar]
    face_inverse = invert(monomial_matrix(face_points, planar))
    face_mass = mat_mul(mat_mul(transposed(face_inverse), moment_matrix(planar, 2)), face_inverse)
    face_axes = ((0, 1), (0, 2), (0, 1), (1, 2))
    face_mask = [[0] * 10 for _ in range(4)]
    for face_id in range(4):
        for node_id, triple in enumerate(triples):
            on_face = (
                triple[2] == 0,
                triple[1] == 0,
                triple[0] + triple[1] + triple[2] == 3,
                triple[0] == 0,
            )[face_id]
            if on_face:
                key_pair = (triple[face_axes[face_id][0]], triple[face_axes[face_id][1]])
                face_mask[face_id][planar.index(key_pair)] = node_id
    surface = [[0.0] * 40 for _ in range(20)]
    for face_id in range(4):
        for row_id in range(10):
            for col_id in range(10):
                surface[face_mask[face_id][row_id]][face_id * 10 + col_id] += face_mass[row_id][
                    col_id
                ]
    lifting = mat_mul(invert(volume_mass), surface)
    lift_alt = [
        [lifting[n_id][f_id * 10 + j_id] for j_id in range(10) for f_id in range(4)]
        for n_id in range(20)
    ]
    node_perms = []
    for turn_id in range(6):
        perm_row = []
        for pair_item in planar:
            triple_face = (pair_item[0], pair_item[1], 3 - pair_item[0] - pair_item[1])
            moved_triple = [triple_face[coordinate_perms[turn_id][axis_id]] for axis_id in range(3)]
            perm_row.append(planar.index((moved_triple[0], moved_triple[1])))
        node_perms.append(perm_row)
    node_picks = [face_mask[f_id][j_id] for j_id in range(10) for f_id in range(4)]
    return slopes, lifting, face_mask, node_perms


def bf16_pair(matrix):
    wide = np.asarray(matrix, np.float32)
    high = wide.astype(ml_dtypes.bfloat16)
    rest = (wide - high.astype(np.float32)).astype(ml_dtypes.bfloat16)
    return high, rest


slope_table, lift_table, face_mask, node_perms = dg_tables()


def slope_operand():
    stacked = np.zeros((80, 32), np.float64)
    for axis_id in range(3):
        first_row = axis_id * 24
        stacked[first_row : first_row + node_count, :node_count] = slope_table[axis_id]
    high, rest = bf16_pair(stacked)
    return jnp.asarray(np.concatenate([high, high, rest], axis=1))


def lift_operand():
    stacked = np.zeros((32, 48), np.float64)
    for face_id in range(faces):
        for node_id in range(face_nodes):
            for row_id in range(node_count):
                stacked[row_id, node_id * faces + face_id] = lift_table[row_id][
                    face_id * face_nodes + node_id
                ]
    high, rest = bf16_pair(stacked)
    return jnp.asarray(np.concatenate([high, high, rest], axis=1))


def remote_lift_operand():
    stacked = np.zeros((24 * faces, 16), np.float64)
    for face_id in range(faces):
        for node_id in range(face_nodes):
            for row_id in range(node_count):
                stacked[24 * face_id + row_id, node_id] = lift_table[row_id][
                    face_id * face_nodes + node_id
                ]
    high, rest = bf16_pair(stacked)
    return jnp.asarray(np.concatenate([high, high, rest], axis=1))


def split_two(value):
    high = value.astype(jnp.bfloat16)
    rest = (value - high.astype(jnp.float32)).astype(jnp.bfloat16)
    return high, rest


def dot_rows(left, right):
    return lax.dot_general(
        left, right, (((1,), (0,)), ((), ())), preferred_element_type=jnp.float32
    )


def dot_lanes(left, right):
    return lax.dot_general(
        left, right, (((1,), (1,)), ((), ())), preferred_element_type=jnp.float32
    )


def one_hot(mask):
    return jnp.where(mask, 1.0, 0.0).astype(jnp.bfloat16)


def face_of(codes):
    return sum((codes >= step * new_count).astype(jnp.int32) for step in range(1, faces))


def pack_kernel(fields_ref, geometry_ref, list_ref, out_ref, took_ref, geo_ref, codes_ref, held_ref, sems):
    field_rows = components * node_count
    copies = [
        pltpu.make_async_copy(list_ref, codes_ref, sems.at[0]),
        pltpu.make_async_copy(fields_ref, took_ref, sems.at[1]),
        pltpu.make_async_copy(geometry_ref, geo_ref, sems.at[2]),
    ]
    for copy in copies:
        copy.start()
    copies[0].wait()
    turned = jnp.concatenate([codes_ref[slot_id] for slot_id in range(slots)], axis=0)
    turned = jnp.concatenate([turned, jnp.zeros((lane - slots, slabs), jnp.int32)], axis=0)
    turned = jnp.concatenate([turned, jnp.zeros((lane, lane - slabs), jnp.int32)], axis=1)
    codes = jnp.transpose(turned)[:slabs]
    codes = jnp.concatenate([codes[slab_first:], codes[:slab_first]], axis=0)
    lanes = lax.broadcasted_iota(jnp.int32, (slabs, old_count), 1)
    picks = jnp.concatenate(
        [one_hot(codes[:, slot_id : slot_id + 1] == lanes) for slot_id in range(slots)], axis=0
    )
    copies[1].wait()
    copies[2].wait()
    for comp_id in range(components):
        held_ref[comp_id * node_count : (comp_id + 1) * node_count, :] = took_ref[comp_id]
    held_ref[field_rows : field_rows + 11, :] = geo_ref[...]
    held_ref[field_rows + 11 :, :] = jnp.zeros((13, old_count), jnp.float32)
    parts = jnp.concatenate(split_two(held_ref[...]), axis=1)
    parts = jnp.concatenate([parts, jnp.zeros((112, 2 * old_count), jnp.bfloat16)], axis=0)
    moved = dot_lanes(jnp.concatenate([picks, picks], axis=1), parts)
    short = lax.broadcasted_iota(jnp.int32, (slabs, lane), 1)
    diagonal = (short == field_rows) | (short == field_rows + 4)
    tail = jnp.zeros((slabs, lane), jnp.float32)
    for slot_id in range(slots):
        empty = codes[:, slot_id : slot_id + 1] < 0
        block = moved[slot_id * slabs : (slot_id + 1) * slabs]
        out_ref[pl.ds(slot_id, slabs, stride=block_rows), :] = jnp.where(
            empty & diagonal, 1.0, block[:, :lane]
        )
        ending = jnp.where(empty & (short < 3), 1.0, block[:, lane:])
        if slot_id:
            ending = pltpu.roll(ending, 3 * slot_id, 1)
        tail = tail + ending
    out_ref[pl.ds(slots, slabs, stride=block_rows), :] = tail


def trace_codes(list_ref, codes_ref):
    codes = list_ref[0]
    codes = jnp.concatenate([codes[sub_first:], codes[:sub_first]], axis=0)
    half = traces // 2
    for idx in range(traces):
        rows = pl.ds((idx // half) * lane + idx % half, subs, stride=half)
        codes_ref[rows, :] = jnp.broadcast_to(codes[:, idx : idx + 1], (subs, lane))
    codes = codes_ref[...]
    face = face_of(codes)
    return face, codes - new_count * face


def lane_picks(chosen, count):
    lanes = lax.broadcasted_iota(jnp.int32, (remote_count, lane), 1)
    return jnp.concatenate(
        [one_hot(chosen == lanes + tile * lane) for tile in range(count)], axis=1
    )


def plan(list_ref, link_ref, orient_ref, chosen_ref, spread_ref, about_ref, codes_ref):
    face, element = trace_codes(list_ref, codes_ref)
    chosen_ref[...] = node_lanes(face)
    slot_picks = lane_picks(element, tiles)
    rows = lax.broadcasted_iota(jnp.int32, (remote_count, new_count), 0)
    about_rows = lax.broadcasted_iota(jnp.int32, (16, new_count), 0)
    about = None
    spread = None
    for face_id in range(faces):
        far = link_ref[face_id : face_id + 1, :] - column_count
        orient = orient_ref[face_id : face_id + 1, :]
        place = ((far >> 4) + subs - sub_first) & (subs - 1)
        column = ((far >> 3) & 1) * lane + place * 8 + (far & 7)
        column = jnp.where((far >= 0) & (orient < 6), column, -1)
        picks = one_hot(rows == column)
        facts = jnp.where(about_rows == 0, orient, jnp.where(about_rows == 1, face_id, 0))
        term = dot_lanes(facts.astype(jnp.float32).astype(jnp.bfloat16), picks)
        about = term if about is None else about + term
        spread = picks if spread is None else spread + picks
    spread_ref[...] = spread
    about_ref[...] = about[:8]
    return slot_picks


def node_lanes(face):
    lanes = lax.broadcasted_iota(jnp.int32, (1, lane), 1) % half_lane
    node = lanes // components
    comp = lanes - node * components
    tables = []
    for face_id in range(faces):
        row = jnp.zeros((1, lane), jnp.int32)
        for node_id in range(face_nodes):
            row = jnp.where(node == node_id, face_mask[face_id][node_id], row)
        tables.append(comp * node_count + row)
    chosen = tables[0]
    for face_id in range(1, faces):
        chosen = jnp.where(face == face_id, tables[face_id], chosen)
    return chosen


def trace_rows(found, chosen):
    turned = jnp.take_along_axis(found, chosen, axis=1, mode="promise_in_bounds")
    half = remote_count // 2
    lanes = lax.broadcasted_iota(jnp.int32, (half, lane), 1)
    return jnp.where(lanes < half_lane, turned[:half], turned[half:])


def start_kernel(came_ref, list_ref, trace_ref, codes_ref):
    face, element = trace_codes(list_ref, codes_ref)
    source = (element * 5462) >> 16
    place = (source + slabs - slab_first) & (slabs - 1)
    picks = lane_picks(place * block_rows + element - source * slots, tiles + 1)
    parts = jnp.concatenate(split_two(came_ref[...]), axis=1)
    parts = jnp.concatenate(
        [parts, jnp.zeros((4 * lane - slabs * block_rows, 2 * lane), jnp.bfloat16)], axis=0
    )
    found = dot_rows(picks, parts)
    trace_ref[...] = trace_rows(found[:, :lane] + found[:, lane:], node_lanes(face))


def unpack(came_ref, state_ref, derived_ref, rows_ref, tail_ref, main_ref):
    field_rows = components * node_count
    runs = ((slab_first, 0, slabs - slab_first), (0, slabs - slab_first, slab_first))
    tail = jnp.concatenate(
        [
            came_ref[pl.ds(place * block_rows + slots, count, stride=block_rows), :]
            for _, place, count in reversed(runs)
        ],
        axis=0,
    )
    for slot_id in range(slots):
        for source, place, count in runs:
            rows_ref[pl.ds(source * slots + slot_id, count, stride=slots), :] = came_ref[
                pl.ds(place * block_rows + slot_id, count, stride=block_rows), :
            ]
        shifted = pltpu.roll(tail, lane - 3 * slot_id, 1) if slot_id else tail
        tail_ref[pl.ds(slot_id, slabs, stride=slots), :] = shifted
    main_ref[...] = jnp.transpose(rows_ref[...])
    extra = jnp.transpose(tail_ref[...])[:8]
    for comp_id in range(components):
        state_ref[comp_id] = main_ref[comp_id * node_count : (comp_id + 1) * node_count, :]
    geo = [main_ref[field_rows + row_id : field_rows + row_id + 1, :] for row_id in range(8)]
    geo.append(extra[0:1])
    derived_ref[0:8, :] = main_ref[field_rows : field_rows + 8, :]
    derived_ref[8:9, :] = extra[0:1]
    derived_ref[9:10, :] = 1.0 / extra[1:2]
    derived_ref[10:11, :] = 1.0 / extra[2:3]
    total = None
    for axis_id in range(3):
        first, second, third = geo[axis_id], geo[3 + axis_id], geo[6 + axis_id]
        normal = 0.5 * jnp.concatenate([-third, -second, first + second + third, -first], axis=0)
        square = normal * normal
        total = square if total is None else total + square
        normal_rows = jnp.concatenate([normal, normal], axis=0)
        derived_ref[16 + 8 * axis_id : 24 + 8 * axis_id, :] = normal_rows
    length = jnp.sqrt(total)
    derived_ref[40:48, :] = jnp.concatenate([length, length], axis=0)
    inverse = 1.0 / length
    derived_ref[48:56, :] = jnp.concatenate([inverse, inverse], axis=0)


def compact(derived_ref, spread_ref, about_ref, far_ref):
    stacked = jnp.concatenate(split_two(derived_ref[16:64, :]), axis=0)
    found = dot_lanes(stacked, spread_ref[...])
    found = found[:48] + found[48:]
    face = about_ref[1:2, :]
    for block in range(5):
        first_row = 8 * block
        value = found[first_row : first_row + 1]
        for face_id in range(1, faces):
            row_id = first_row + face_id
            value = jnp.where(face == face_id, found[row_id : row_id + 1], value)
        far_ref[block : block + 1, :] = value
    far_ref[5:7, :] = about_ref[0:2, :]
    far_ref[7:8, :] = jnp.zeros((1, remote_count), jnp.float32)


def oriented(planes, orient):
    masks = [orient == turn_id for turn_id in range(6)]
    result = []
    for node_id in range(face_nodes):
        sources = {}
        for turn_id in range(6):
            sources.setdefault(node_perms[turn_id][node_id], []).append(turn_id)
        value = None
        for source, turn_ids in sources.items():
            if value is None:
                value = planes[source]
                continue
            mask = masks[turn_ids[0]]
            for turn_id in turn_ids[1:]:
                mask = mask | masks[turn_id]
            value = jnp.where(mask, planes[source], value)
        result.append(value)
    return result


def face_flux(jump_of, normal, length, inverse):
    jump_h = [jump_of(comp_id) for comp_id in range(3)]
    jump_e = [jump_of(comp_id) for comp_id in range(3, 6)]

    def along(jump):
        total = normal[0] * jump[0] + normal[1] * jump[1] + normal[2] * jump[2]
        return total * inverse

    along_h = along(jump_h)
    along_e = along(jump_e)
    flux_h, flux_e = [], []
    for axis_id in range(3):
        after, last = (axis_id + 1) % 3, (axis_id + 2) % 3
        cross_e = normal[after] * jump_e[last] - normal[last] * jump_e[after]
        cross_h = normal[after] * jump_h[last] - normal[last] * jump_h[after]
        flux_h.append(length * jump_h[axis_id] - normal[axis_id] * along_h - cross_e)
        flux_e.append(length * jump_e[axis_id] - normal[axis_id] * along_e + cross_h)
    return flux_h + flux_e


def lifted_flux(jump_ref, flux_ref, derived_ref, lift_ref):
    groups = faces * face_nodes // 8

    def jump_of(comp_id):
        rows = strided_load(jump_ref, comp_id, faces * face_nodes, 8)
        return rows.reshape(groups, 8, new_count)

    normal = [derived_ref[16 + 8 * axis_id : 24 + 8 * axis_id, :][None] for axis_id in range(3)]
    fluxes = face_flux(jump_of, normal, derived_ref[40:48, :][None], derived_ref[48:56, :][None])
    for comp_id, value in enumerate(fluxes):
        flux_ref[0:40, comp_id * new_count : (comp_id + 1) * new_count] = value.reshape(
            faces * face_nodes, new_count
        )
    flux_ref[40:48, :] = jnp.zeros((8, components * new_count), jnp.float32)
    high, rest = split_two(flux_ref[...])
    return dot_rows(lift_ref[...], jnp.concatenate([high, rest, high], axis=0))


def strided_load(ref, start, size, stride):
    return jnp.concatenate(
        [ref[tile, pl.ds(start, size, stride=stride), :] for tile in range(ref.shape[0])], axis=1
    )


def tiled_store(ref, rows, value):
    for tile in range(ref.shape[0]):
        ref[tile, rows, :] = value[:, tile * lane : (tile + 1) * lane]


def tiled_load(ref, rows):
    return jnp.concatenate([ref[tile, rows, :] for tile in range(tiles)], axis=1)


def column_block(matrix, comp_id):
    return matrix[:24, comp_id * new_count : (comp_id + 1) * new_count]


def local_part(
    state_ref, derived_ref, link_ref, orient_ref, slope_ref, lift_ref, part_ref, nodes_ref, flat_ref, jump_ref, flux_ref
):
    nodes_ref[...] = jnp.zeros(nodes_ref.shape, jnp.float32)
    flat_ref[node_count:32, :] = jnp.zeros((12, components * new_count), jnp.float32)
    for comp_id in range(components):
        current = state_ref[comp_id]
        tiled_store(nodes_ref, pl.ds(comp_id, node_count, stride=8), current)
        flat_ref[0:node_count, comp_id * new_count : (comp_id + 1) * new_count] = current
    stacked = jnp.concatenate(split_two(tiled_load(nodes_ref, slice(None))), axis=1)
    rows = lax.broadcasted_iota(jnp.int32, (new_count, new_count), 0)
    links = [link_ref[face_id : face_id + 1, :] for face_id in range(faces)]
    owners = [face_of(link) for link in links]
    picks = [
        one_hot(rows == jnp.where(link < column_count, link - new_count * owner, -1))
        for link, owner in zip(links, owners)
    ]
    found_pairs = []
    for first in range(0, faces, 2):
        both = jnp.concatenate(picks[first : first + 2], axis=1)
        found_pairs.append(dot_rows(stacked, jnp.concatenate([both, both], axis=0)))
    comp_rows = lax.broadcasted_iota(jnp.int32, (8, new_count), 0)
    wall_gain = jnp.where(comp_rows >= 3, -2.0, 0.0)
    for face_id in range(faces):
        orient = orient_ref[face_id : face_id + 1, :]
        first_column = (face_id % 2) * new_count
        found = found_pairs[face_id // 2][:, first_column : first_column + new_count]
        owner_masks = [owners[face_id] == other for other in range(faces)]
        planes = []
        for node_id in range(face_nodes):
            value = None
            for other in range(faces):
                first_row = 8 * face_mask[other][node_id]
                plane = found[first_row : first_row + 8]
                value = plane if value is None else jnp.where(owner_masks[other], plane, value)
            planes.append(value)
        outside = oriented(planes, orient)
        wall = orient == 6
        for node_id in range(face_nodes):
            first_row = 8 * face_mask[face_id][node_id]
            inside = tiled_load(nodes_ref, slice(first_row, first_row + 8))
            jump = jnp.where(wall, wall_gain * inside, outside[node_id] - inside)
            target = 8 * (node_id * faces + face_id)
            tiled_store(jump_ref, slice(target, target + 8), jump)
    lifted = lifted_flux(jump_ref, flux_ref, derived_ref, lift_ref)
    high, rest = split_two(flat_ref[...])
    slopes = dot_rows(slope_ref[...], jnp.concatenate([high, rest, high], axis=0))
    inverse_jac = [
        [derived_ref[3 * row_id + axis_id : 3 * row_id + axis_id + 1, :] for axis_id in range(3)]
        for row_id in range(3)
    ]

    def gradient(axis_id, comp_id):
        columns = slice(comp_id * new_count, (comp_id + 1) * new_count)
        return (
            inverse_jac[0][axis_id] * slopes[0:24, columns]
            + inverse_jac[1][axis_id] * slopes[24:48, columns]
            + inverse_jac[2][axis_id] * slopes[48:72, columns]
        )

    inverse_eps = derived_ref[9:10, :]
    inverse_mu = derived_ref[10:11, :]
    for axis_id in range(3):
        after, last = (axis_id + 1) % 3, (axis_id + 2) % 3
        curl_h = gradient(after, last) - gradient(last, after)
        curl_e = gradient(after, 3 + last) - gradient(last, 3 + after)
        change_h = (column_block(lifted, axis_id) - curl_e) * inverse_mu
        change_e = (column_block(lifted, 3 + axis_id) + curl_h) * inverse_eps
        part_ref[axis_id] = change_h[:node_count]
        part_ref[3 + axis_id] = change_e[:node_count]


def arrive_kernel(
    came_ref,
    link_ref,
    orient_ref,
    slope_ref,
    lift_ref,
    list_ref,
    state_ref,
    derived_ref,
    far_ref,
    part_ref,
    chosen_ref,
    spread_ref,
    shared_ref,
    known_ref,
    scale_ref,
    rows_ref,
    tail_ref,
    main_ref,
    about_ref,
    codes_ref,
    *scratches,
):
    picks = plan(list_ref, link_ref, orient_ref, chosen_ref, spread_ref, about_ref, codes_ref)
    shared_ref[...] = dot_lanes(picks, spread_ref[...]).astype(jnp.bfloat16)
    derived_ref[...] = jnp.zeros(derived_ref.shape, jnp.float32)
    unpack(came_ref, state_ref, derived_ref, rows_ref, tail_ref, main_ref)
    compact(derived_ref, spread_ref, about_ref, far_ref)
    local_part(state_ref, derived_ref, link_ref, orient_ref, slope_ref, lift_ref, part_ref, *scratches)
    field_rows = components * node_count
    gain = section_b1 * time_step
    for comp_id in range(components):
        main_ref[comp_id * node_count : (comp_id + 1) * node_count, :] = (
            state_ref[comp_id] + gain * part_ref[comp_id]
        )
    main_ref[field_rows : field_rows + 1, :] = gain * derived_ref[10:11, :]
    main_ref[field_rows + 1 : field_rows + 2, :] = gain * derived_ref[9:10, :]
    main_ref[field_rows + 2 :, :] = jnp.zeros((6, new_count), jnp.float32)
    found = dot_lanes(picks, jnp.concatenate(split_two(main_ref[...]), axis=0))
    found = found[:, :lane] + found[:, lane:]
    known_ref[...] = trace_rows(found, chosen_ref[...])
    lanes = lax.broadcasted_iota(jnp.int32, (remote_count, lane), 1) % half_lane
    comp = lanes - (lanes // components) * components
    scale_ref[...] = trace_rows(found, jnp.where(comp < 3, field_rows, field_rows + 1))


def local_kernel(*refs):
    local_part(*refs)


def remote_part(came_ref, far_ref, lift_ref, turned_ref, jump_ref):
    turned_ref[...] = jnp.transpose(came_ref[...])
    planes = []
    for node_id in range(face_nodes):
        first_row = node_id * components
        halves_of = [
            turned_ref[half * half_lane + first_row : half * half_lane + first_row + 8, :]
            for half in range(2)
        ]
        planes.append(jnp.concatenate(halves_of, axis=1))
    outside = oriented(planes, far_ref[5:6, :])
    for node_id in range(face_nodes):
        tiled_store(jump_ref, slice(8 * node_id, 8 * node_id + 8), outside[node_id])
    blank = jnp.zeros((8 * (16 - face_nodes), remote_count), jnp.float32)
    tiled_store(jump_ref, slice(8 * face_nodes, 128), blank)
    fluxes = face_flux(
        lambda comp_id: strided_load(jump_ref, comp_id, 16, 8),
        [far_ref[axis_id : axis_id + 1, :] for axis_id in range(3)],
        far_ref[3:4, :],
        far_ref[4:5, :],
    )
    high, rest = split_two(jnp.concatenate(fluxes, axis=1))
    lifted = dot_rows(lift_ref[...], jnp.concatenate([high, rest, high], axis=0))
    face = far_ref[6:7, :]
    blocks = []
    for comp_id in range(components):
        columns = slice(comp_id * remote_count, (comp_id + 1) * remote_count)
        block = lifted[:24, columns]
        for face_id in range(1, faces):
            block = jnp.where(
                face == face_id, lifted[24 * face_id : 24 * face_id + 24, columns], block
            )
        blocks.append(block)
    return blocks


def placed_part(blocks, spread_ref, derived_ref):
    stacked = jnp.concatenate(blocks, axis=0)
    placed = dot_rows(jnp.concatenate(split_two(stacked), axis=0), spread_ref[...])
    rows = 24 * components
    placed = placed[:rows] + placed[rows:]
    inverse_eps = derived_ref[9:10, :]
    inverse_mu = derived_ref[10:11, :]
    return [
        (placed[24 * comp_id : 24 * comp_id + 24] * (inverse_mu if comp_id < 3 else inverse_eps))[
            :node_count
        ]
        for comp_id in range(components)
    ]


def first_kernel(
    came_ref,
    part_ref,
    state_ref,
    derived_ref,
    far_ref,
    spread_ref,
    lift_ref,
    shared_ref,
    known_ref,
    scale_ref,
    chosen_ref,
    residual_ref,
    middle_ref,
    trace_ref,
    send_ref,
    sem,
    packed_ref,
    *scratches,
):
    blocks = remote_part(came_ref, far_ref, lift_ref, *scratches)
    for comp_id, block in enumerate(blocks):
        packed_ref[comp_id * node_count : (comp_id + 1) * node_count, :] = block[:node_count]
    packed_ref[components * node_count :, :] = jnp.zeros((8, remote_count), jnp.float32)
    found = dot_lanes(shared_ref[...], jnp.concatenate(split_two(packed_ref[...]), axis=0))
    found = trace_rows(found[:, :lane] + found[:, lane:], chosen_ref[...])
    send_ref[...] = known_ref[...] + scale_ref[...] * found
    copy = pltpu.make_async_copy(send_ref, trace_ref, sem)
    copy.start()
    changes = placed_part(blocks, spread_ref, derived_ref)
    for comp_id in range(components):
        residual = time_step * (part_ref[comp_id] + changes[comp_id])
        residual_ref[comp_id] = residual
        middle_ref[comp_id] = state_ref[comp_id] + section_b1 * residual
    copy.wait()


def second_kernel(
    came_ref,
    part_ref,
    middle_ref,
    first_ref,
    derived_ref,
    far_ref,
    spread_ref,
    lift_ref,
    advanced_ref,
    residual_ref,
    *scratches,
):
    blocks = remote_part(came_ref, far_ref, lift_ref, *scratches)
    changes = placed_part(blocks, spread_ref, derived_ref)
    for comp_id in range(components):
        residual = section_a2 * first_ref[comp_id] + time_step * (
            part_ref[comp_id] + changes[comp_id]
        )
        residual_ref[comp_id] = residual
        advanced_ref[comp_id] = middle_ref[comp_id] + section_b2 * residual


def floats(*shape):
    return jax.ShapeDtypeStruct(shape, jnp.float32)


def halves(*shape):
    return jax.ShapeDtypeStruct(shape, jnp.bfloat16)


def scratch(*shape):
    return pltpu.VMEM(shape, jnp.float32)


fast = pl.BlockSpec(memory_space=pltpu.VMEM)
free = pl.BlockSpec(memory_space=pl.ANY)


def run(kernel, name, outs, scratches, operands, in_specs=None, out_specs=None):
    return pl.pallas_call(
        kernel,
        name=name,
        out_shape=outs,
        in_specs=in_specs or [fast] * len(operands),
        out_specs=out_specs or jax.tree.map(lambda _: fast, outs),
        scratch_shapes=scratches,
        compiler_params=pltpu.CompilerParams(vmem_limit_bytes=24 * 2**20),
        cost_estimate=pl.CostEstimate(flops=10**8, bytes_accessed=10**6, transcendentals=0),
    )(*operands)


def shards(fields, geometry, migrate_list, trace_list, face_link, face_orient):
    slopes = slope_operand()
    lift = lift_operand()
    remote_lift = remote_lift_operand()
    state_shape = floats(components, node_count, new_count)
    trace_shape = floats(remote_count // 2, lane)
    local_scratch = [
        scratch(tiles, 8 * node_count, lane),
        scratch(32, components * new_count),
        scratch(tiles, 8 * faces * face_nodes, lane),
        scratch(48, components * new_count),
    ]
    remote_scratch = [scratch(lane, lane), scratch(2, lane, lane)]
    parcel = run(
        pack_kernel,
        "pack",
        floats(slabs * block_rows, lane),
        [
            scratch(components, node_count, old_count),
            scratch(11, old_count),
            pltpu.VMEM((slots, 1, slabs), jnp.int32),
            scratch(144, old_count),
            pltpu.SemaphoreType.DMA((3,)),
        ],
        [
            pltpu.with_memory_space_constraint(operand, pltpu.HBM)
            for operand in (fields, geometry, jnp.transpose(migrate_list, (2, 0, 1)))
        ],
        [pl.BlockSpec(memory_space=pltpu.HBM)] * 3,
    )
    arrived = lax.all_to_all(
        parcel.reshape(slabs, block_rows * lane), "slab", split_axis=0, concat_axis=0, tiled=True,
        axis_index_groups=[slab_order],
    ).reshape(slabs * block_rows, lane)
    code_scratch = pltpu.VMEM((remote_count, lane), jnp.int32)
    outgoing = run(
        start_kernel, "start", trace_shape, [code_scratch], (arrived, trace_list)
    )

    def exchange(rows):
        blocks = rows.reshape(subs, traces // 2, lane)
        came = lax.all_to_all(
            blocks, "sub", split_axis=0, concat_axis=0, tiled=True, axis_index_groups=[sub_order]
        )
        return came.reshape(remote_count // 2, lane)

    incoming = exchange(outgoing)
    state, derived, far, part, chosen, spread, shared, known, scale = run(
        arrive_kernel,
        "arrive",
        (
            state_shape,
            floats(64, new_count),
            floats(8, remote_count),
            state_shape,
            jax.ShapeDtypeStruct((remote_count, lane), jnp.int32),
            halves(remote_count, new_count),
            halves(remote_count, remote_count),
            floats(remote_count // 2, lane),
            floats(remote_count // 2, lane),
        ),
        [
            scratch(new_count, lane),
            scratch(new_count, lane),
            scratch(lane, new_count),
            scratch(8, remote_count),
            code_scratch,
        ]
        + local_scratch,
        (arrived, face_link, face_orient, slopes, lift, trace_list),
    )
    first_res, middle, outgoing = run(
        first_kernel,
        "first",
        (state_shape, state_shape, trace_shape),
        [scratch(remote_count // 2, lane), pltpu.SemaphoreType.DMA, scratch(lane, remote_count)]
        + remote_scratch,
        (
            incoming,
            part,
            state,
            derived,
            far,
            spread,
            remote_lift,
            shared,
            known,
            scale,
            chosen,
        ),
        out_specs=(fast, fast, free),
    )
    incoming = exchange(outgoing)
    part = run(
        local_kernel,
        "local",
        state_shape,
        local_scratch,
        (middle, derived, face_link, face_orient, slopes, lift),
    )
    return run(
        second_kernel,
        "second",
        (state_shape, state_shape),
        remote_scratch,
        (incoming, part, middle, first_res, derived, far, spread, remote_lift),
    )


def solution(mesh):
    return jax.shard_map(
        shards,
        mesh=mesh,
        in_specs=(
            P(None, None, ("slab", "sub")),
            P(None, ("slab", "sub")),
            P(("slab", "sub"), None, None),
            P(("slab", "sub"), None, None),
            P(None, ("slab", "sub")),
            P(None, ("slab", "sub")),
        ),
        out_specs=(P(None, None, ("slab", "sub")), P(None, None, ("slab", "sub"))),
        check_vma=False,
    )
```

```python
import math

import jax
import jax.numpy as jnp
import ml_dtypes
import numpy as np
from jax import lax
from jax.experimental import pallas as pl
from jax.experimental.pallas import tpu as pltpu
from jax.sharding import PartitionSpec as P

time_step = 0.004
section_a2 = -0.4178904745
section_b1 = 0.1496590219993
section_b2 = 0.3792103129999
coordinate_perms = ((0, 1, 2), (1, 2, 0), (2, 0, 1), (0, 2, 1), (2, 1, 0), (1, 0, 2))
components = 6
node_count = 20
face_nodes = 10
faces = 4
old_count = 256
slots = 12
slabs = 32
subs = 16
traces = 16
new_count = slots * slabs
column_count = faces * new_count
remote_count = subs * traces
lane = 128
half_lane = lane // 2
tiles = new_count // lane
block_rows = slots + 1
slab_first = 21
sub_first = 10
slab_order = [(slab_first + place) % slabs for place in range(slabs)]
sub_order = [(sub_first + place) % subs for place in range(subs)]


def volume_triples():
    result_list = []
    for first_idx in range(4):
        for second_idx in range(4 - first_idx):
            for third_idx in range(4 - first_idx - second_idx):
                result_list.append((first_idx, second_idx, third_idx))
    return result_list


def planar_pairs():
    result_list = []
    for first_idx in range(4):
        for second_idx in range(4 - first_idx):
            result_list.append((first_idx, second_idx))
    return result_list


def monomial_matrix(points, powers):
    result_rows = []
    for point_item in points:
        row_values = []
        for power_item in powers:
            product_value = 1.0
            for axis_id in range(len(power_item)):
                product_value = product_value * point_item[axis_id] ** power_item[axis_id]
            row_values.append(product_value)
        result_rows.append(row_values)
    return result_rows


def mat_mul(left_rows, right_rows):
    inner_count = len(right_rows)
    col_count = len(right_rows[0])
    return [
        [
            sum((left_row[k_id] * right_rows[k_id][c_id] for k_id in range(inner_count)))
            for c_id in range(col_count)
        ]
        for left_row in left_rows
    ]


def transposed(matrix_rows):
    return [list(row_item) for row_item in zip(*matrix_rows)]


def invert(matrix_rows):
    order = len(matrix_rows)
    work_rows = [
        list(matrix_rows[r_id]) + [1.0 if r_id == c_id else 0.0 for c_id in range(order)]
        for r_id in range(order)
    ]
    for col_id in range(order):
        pivot_row = max(range(col_id, order), key=lambda r_id: abs(work_rows[r_id][col_id]))
        work_rows[col_id], work_rows[pivot_row] = (work_rows[pivot_row], work_rows[col_id])
        pivot_value = work_rows[col_id][col_id]
        work_rows[col_id] = [value / pivot_value for value in work_rows[col_id]]
        for r_id in range(order):
            if r_id != col_id:
                factor = work_rows[r_id][col_id]
                if factor != 0.0:
                    work_rows[r_id] = [
                        work_rows[r_id][c_id] - factor * work_rows[col_id][c_id]
                        for c_id in range(2 * order)
                    ]
    return [row_item[order:] for row_item in work_rows]


def moment_matrix(powers, extra_dim):
    total_terms = len(powers)
    result_matrix = [[0.0] * total_terms for _ in range(total_terms)]
    for row_id in range(total_terms):
        for col_id in range(total_terms):
            joined = [
                powers[row_id][a_id] + powers[col_id][a_id] for a_id in range(len(powers[row_id]))
            ]
            numerator = 1.0
            for exponent in joined:
                numerator = numerator * math.factorial(exponent)
            result_matrix[row_id][col_id] = numerator / math.factorial(sum(joined) + extra_dim)
    return result_matrix


def dg_tables():
    triples = volume_triples()
    points = [tuple((value / 3.0 for value in triple)) for triple in triples]
    inverse = invert(monomial_matrix(points, triples))
    slopes = []
    for axis_id in range(3):
        lowered = [
            tuple(
                (max(triple[a_id] - 1, 0) if a_id == axis_id else triple[a_id] for a_id in range(3))
            )
            for triple in triples
        ]
        base_rows = monomial_matrix(points, lowered)
        slope_values = [
            [triples[c_id][axis_id] * base_rows[r_id][c_id] for c_id in range(20)]
            for r_id in range(20)
        ]
        slopes.append(mat_mul(slope_values, inverse))
    volume_mass = mat_mul(mat_mul(transposed(inverse), moment_matrix(triples, 3)), inverse)
    planar = planar_pairs()
    face_points = [tuple((value / 3.0 for value in pair_item)) for pair_item in planar]
    face_inverse = invert(monomial_matrix(face_points, planar))
    face_mass = mat_mul(mat_mul(transposed(face_inverse), moment_matrix(planar, 2)), face_inverse)
    face_axes = ((0, 1), (0, 2), (0, 1), (1, 2))
    face_mask = [[0] * 10 for _ in range(4)]
    for face_id in range(4):
        for node_id, triple in enumerate(triples):
            on_face = (
                triple[2] == 0,
                triple[1] == 0,
                triple[0] + triple[1] + triple[2] == 3,
                triple[0] == 0,
            )[face_id]
            if on_face:
                key_pair = (triple[face_axes[face_id][0]], triple[face_axes[face_id][1]])
                face_mask[face_id][planar.index(key_pair)] = node_id
    surface = [[0.0] * 40 for _ in range(20)]
    for face_id in range(4):
        for row_id in range(10):
            for col_id in range(10):
                surface[face_mask[face_id][row_id]][face_id * 10 + col_id] += face_mass[row_id][
                    col_id
                ]
    lifting = mat_mul(invert(volume_mass), surface)
    lift_alt = [
        [lifting[n_id][f_id * 10 + j_id] for j_id in range(10) for f_id in range(4)]
        for n_id in range(20)
    ]
    node_perms = []
    for turn_id in range(6):
        perm_row = []
        for pair_item in planar:
            triple_face = (pair_item[0], pair_item[1], 3 - pair_item[0] - pair_item[1])
            moved_triple = [triple_face[coordinate_perms[turn_id][axis_id]] for axis_id in range(3)]
            perm_row.append(planar.index((moved_triple[0], moved_triple[1])))
        node_perms.append(perm_row)
    node_picks = [face_mask[f_id][j_id] for j_id in range(10) for f_id in range(4)]
    return slopes, lifting, face_mask, node_perms


def bf16_terms(matrix):
    rest = np.asarray(matrix, np.float64)
    parts = []
    for _ in range(3):
        part = rest.astype(np.float32).astype(ml_dtypes.bfloat16)
        parts.append(part)
        rest = rest - part.astype(np.float64)
    order = (0, 0, 1, 0, 1, 2)
    return jnp.asarray(np.concatenate([parts[place] for place in order], axis=1))


slope_table, lift_table, face_mask, node_perms = dg_tables()


def slope_operand():
    stacked = np.zeros((80, 32), np.float64)
    for axis_id in range(3):
        first_row = axis_id * 24
        stacked[first_row : first_row + node_count, :node_count] = slope_table[axis_id]
    return bf16_terms(stacked)


def lift_operand():
    stacked = np.zeros((32, 48), np.float64)
    for face_id in range(faces):
        for node_id in range(face_nodes):
            for row_id in range(node_count):
                stacked[row_id, node_id * faces + face_id] = lift_table[row_id][
                    face_id * face_nodes + node_id
                ]
    return bf16_terms(stacked)


def remote_lift_operand():
    stacked = np.zeros((24 * faces, 16), np.float64)
    for face_id in range(faces):
        for node_id in range(face_nodes):
            for row_id in range(node_count):
                stacked[24 * face_id + row_id, node_id] = lift_table[row_id][
                    face_id * face_nodes + node_id
                ]
    return bf16_terms(stacked)


def split_two(value):
    high = value.astype(jnp.bfloat16)
    rest = (value - high.astype(jnp.float32)).astype(jnp.bfloat16)
    return high, rest


def split_three(value):
    high = value.astype(jnp.bfloat16)
    left = value - high.astype(jnp.float32)
    middle = left.astype(jnp.bfloat16)
    rest = (left - middle.astype(jnp.float32)).astype(jnp.bfloat16)
    return high, middle, rest


def table_terms(value):
    high, middle, rest = split_three(value)
    return jnp.concatenate([high, middle, high, rest, middle, high], axis=0)


def three_lanes(found):
    return found[:, :lane] + found[:, lane : 2 * lane] + found[:, 2 * lane :]


def dot_rows(left, right):
    return lax.dot_general(
        left, right, (((1,), (0,)), ((), ())), preferred_element_type=jnp.float32
    )


def dot_lanes(left, right):
    return lax.dot_general(
        left, right, (((1,), (1,)), ((), ())), preferred_element_type=jnp.float32
    )


def one_hot(mask):
    return jnp.where(mask, 1.0, 0.0).astype(jnp.bfloat16)


def face_of(codes):
    return sum((codes >= step * new_count).astype(jnp.int32) for step in range(1, faces))


def pack_kernel(fields_ref, geometry_ref, list_ref, out_ref, took_ref, geo_ref, codes_ref, held_ref, sems):
    field_rows = components * node_count
    copies = [
        pltpu.make_async_copy(list_ref, codes_ref, sems.at[0]),
        pltpu.make_async_copy(fields_ref, took_ref, sems.at[1]),
        pltpu.make_async_copy(geometry_ref, geo_ref, sems.at[2]),
    ]
    for copy in copies:
        copy.start()
    copies[0].wait()
    turned = jnp.concatenate([codes_ref[slot_id] for slot_id in range(slots)], axis=0)
    turned = jnp.concatenate([turned, jnp.zeros((lane - slots, slabs), jnp.int32)], axis=0)
    turned = jnp.concatenate([turned, jnp.zeros((lane, lane - slabs), jnp.int32)], axis=1)
    codes = jnp.transpose(turned)[:slabs]
    codes = jnp.concatenate([codes[slab_first:], codes[:slab_first]], axis=0)
    lanes = lax.broadcasted_iota(jnp.int32, (slabs, old_count), 1)
    picks = jnp.concatenate(
        [one_hot(codes[:, slot_id : slot_id + 1] == lanes) for slot_id in range(slots)], axis=0
    )
    copies[1].wait()
    copies[2].wait()
    for comp_id in range(components):
        held_ref[comp_id * node_count : (comp_id + 1) * node_count, :] = took_ref[comp_id]
    held_ref[field_rows : field_rows + 11, :] = geo_ref[...]
    held_ref[field_rows + 11 :, :] = jnp.zeros((13, old_count), jnp.float32)
    parts = jnp.concatenate(split_three(held_ref[...]), axis=1)
    parts = jnp.concatenate([parts, jnp.zeros((112, 3 * old_count), jnp.bfloat16)], axis=0)
    moved = dot_lanes(jnp.concatenate([picks, picks, picks], axis=1), parts)
    short = lax.broadcasted_iota(jnp.int32, (slabs, lane), 1)
    diagonal = (short == field_rows) | (short == field_rows + 4)
    tail = jnp.zeros((slabs, lane), jnp.float32)
    for slot_id in range(slots):
        empty = codes[:, slot_id : slot_id + 1] < 0
        block = moved[slot_id * slabs : (slot_id + 1) * slabs]
        out_ref[pl.ds(slot_id, slabs, stride=block_rows), :] = jnp.where(
            empty & diagonal, 1.0, block[:, :lane]
        )
        ending = jnp.where(empty & (short < 3), 1.0, block[:, lane:])
        if slot_id:
            ending = pltpu.roll(ending, 3 * slot_id, 1)
        tail = tail + ending
    out_ref[pl.ds(slots, slabs, stride=block_rows), :] = tail


def trace_codes(list_ref, codes_ref):
    codes = list_ref[0]
    codes = jnp.concatenate([codes[sub_first:], codes[:sub_first]], axis=0)
    half = traces // 2
    for idx in range(traces):
        rows = pl.ds((idx // half) * lane + idx % half, subs, stride=half)
        codes_ref[rows, :] = jnp.broadcast_to(codes[:, idx : idx + 1], (subs, lane))
    codes = codes_ref[...]
    face = face_of(codes)
    return face, codes - new_count * face


def lane_picks(chosen, count):
    lanes = lax.broadcasted_iota(jnp.int32, (remote_count, lane), 1)
    return jnp.concatenate(
        [one_hot(chosen == lanes + tile * lane) for tile in range(count)], axis=1
    )


def plan(list_ref, link_ref, orient_ref, chosen_ref, spread_ref, about_ref, codes_ref):
    face, element = trace_codes(list_ref, codes_ref)
    chosen_ref[...] = node_lanes(face)
    slot_picks = lane_picks(element, tiles)
    rows = lax.broadcasted_iota(jnp.int32, (remote_count, new_count), 0)
    about_rows = lax.broadcasted_iota(jnp.int32, (16, new_count), 0)
    about = None
    spread = None
    for face_id in range(faces):
        far = link_ref[face_id : face_id + 1, :] - column_count
        orient = orient_ref[face_id : face_id + 1, :]
        place = ((far >> 4) + subs - sub_first) & (subs - 1)
        column = ((far >> 3) & 1) * lane + place * 8 + (far & 7)
        column = jnp.where((far >= 0) & (orient < 6), column, -1)
        picks = one_hot(rows == column)
        facts = jnp.where(about_rows == 0, orient, jnp.where(about_rows == 1, face_id, 0))
        term = dot_lanes(facts.astype(jnp.float32).astype(jnp.bfloat16), picks)
        about = term if about is None else about + term
        spread = picks if spread is None else spread + picks
    spread_ref[...] = spread
    about_ref[...] = about[:8]
    return slot_picks


def node_lanes(face):
    lanes = lax.broadcasted_iota(jnp.int32, (1, lane), 1) % half_lane
    node = lanes // components
    comp = lanes - node * components
    tables = []
    for face_id in range(faces):
        row = jnp.zeros((1, lane), jnp.int32)
        for node_id in range(face_nodes):
            row = jnp.where(node == node_id, face_mask[face_id][node_id], row)
        tables.append(comp * node_count + row)
    chosen = tables[0]
    for face_id in range(1, faces):
        chosen = jnp.where(face == face_id, tables[face_id], chosen)
    return chosen


def trace_rows(found, chosen):
    turned = jnp.take_along_axis(found, chosen, axis=1, mode="promise_in_bounds")
    half = remote_count // 2
    lanes = lax.broadcasted_iota(jnp.int32, (half, lane), 1)
    return jnp.where(lanes < half_lane, turned[:half], turned[half:])


def start_kernel(came_ref, list_ref, trace_ref, codes_ref):
    face, element = trace_codes(list_ref, codes_ref)
    source = (element * 5462) >> 16
    place = (source + slabs - slab_first) & (slabs - 1)
    picks = lane_picks(place * block_rows + element - source * slots, tiles + 1)
    parts = jnp.concatenate(split_three(came_ref[...]), axis=1)
    parts = jnp.concatenate(
        [parts, jnp.zeros((4 * lane - slabs * block_rows, 3 * lane), jnp.bfloat16)], axis=0
    )
    trace_ref[...] = trace_rows(three_lanes(dot_rows(picks, parts)), node_lanes(face))


def unpack(came_ref, state_ref, derived_ref, rows_ref, tail_ref, main_ref):
    field_rows = components * node_count
    runs = ((slab_first, 0, slabs - slab_first), (0, slabs - slab_first, slab_first))
    tail = jnp.concatenate(
        [
            came_ref[pl.ds(place * block_rows + slots, count, stride=block_rows), :]
            for _, place, count in reversed(runs)
        ],
        axis=0,
    )
    for slot_id in range(slots):
        for source, place, count in runs:
            rows_ref[pl.ds(source * slots + slot_id, count, stride=slots), :] = came_ref[
                pl.ds(place * block_rows + slot_id, count, stride=block_rows), :
            ]
        shifted = pltpu.roll(tail, lane - 3 * slot_id, 1) if slot_id else tail
        tail_ref[pl.ds(slot_id, slabs, stride=slots), :] = shifted
    main_ref[...] = jnp.transpose(rows_ref[...])
    extra = jnp.transpose(tail_ref[...])[:8]
    for comp_id in range(components):
        state_ref[comp_id] = main_ref[comp_id * node_count : (comp_id + 1) * node_count, :]
    geo = [main_ref[field_rows + row_id : field_rows + row_id + 1, :] for row_id in range(8)]
    geo.append(extra[0:1])
    derived_ref[0:8, :] = main_ref[field_rows : field_rows + 8, :]
    derived_ref[8:9, :] = extra[0:1]
    derived_ref[9:10, :] = 1.0 / extra[1:2]
    derived_ref[10:11, :] = 1.0 / extra[2:3]
    total = None
    for axis_id in range(3):
        first, second, third = geo[axis_id], geo[3 + axis_id], geo[6 + axis_id]
        normal = 0.5 * jnp.concatenate([-third, -second, first + second + third, -first], axis=0)
        square = normal * normal
        total = square if total is None else total + square
        normal_rows = jnp.concatenate([normal, normal], axis=0)
        derived_ref[16 + 8 * axis_id : 24 + 8 * axis_id, :] = normal_rows
    length = jnp.sqrt(total)
    derived_ref[40:48, :] = jnp.concatenate([length, length], axis=0)
    inverse = 1.0 / length
    derived_ref[48:56, :] = jnp.concatenate([inverse, inverse], axis=0)


def compact(derived_ref, spread_ref, about_ref, far_ref):
    stacked = jnp.concatenate(split_three(derived_ref[16:64, :]), axis=0)
    found = dot_lanes(stacked, spread_ref[...])
    found = found[:48] + found[48:96] + found[96:]
    face = about_ref[1:2, :]
    for block in range(5):
        first_row = 8 * block
        value = found[first_row : first_row + 1]
        for face_id in range(1, faces):
            row_id = first_row + face_id
            value = jnp.where(face == face_id, found[row_id : row_id + 1], value)
        far_ref[block : block + 1, :] = value
    far_ref[5:7, :] = about_ref[0:2, :]
    far_ref[7:8, :] = jnp.zeros((1, remote_count), jnp.float32)


def oriented(planes, orient):
    masks = [orient == turn_id for turn_id in range(6)]
    result = []
    for node_id in range(face_nodes):
        sources = {}
        for turn_id in range(6):
            sources.setdefault(node_perms[turn_id][node_id], []).append(turn_id)
        value = None
        for source, turn_ids in sources.items():
            if value is None:
                value = planes[source]
                continue
            mask = masks[turn_ids[0]]
            for turn_id in turn_ids[1:]:
                mask = mask | masks[turn_id]
            value = jnp.where(mask, planes[source], value)
        result.append(value)
    return result


def face_flux(jump_of, normal, length, inverse):
    jump_h = [jump_of(comp_id) for comp_id in range(3)]
    jump_e = [jump_of(comp_id) for comp_id in range(3, 6)]

    def along(jump):
        total = normal[0] * jump[0] + normal[1] * jump[1] + normal[2] * jump[2]
        return total * inverse

    along_h = along(jump_h)
    along_e = along(jump_e)
    flux_h, flux_e = [], []
    for axis_id in range(3):
        after, last = (axis_id + 1) % 3, (axis_id + 2) % 3
        cross_e = normal[after] * jump_e[last] - normal[last] * jump_e[after]
        cross_h = normal[after] * jump_h[last] - normal[last] * jump_h[after]
        flux_h.append(length * jump_h[axis_id] - normal[axis_id] * along_h - cross_e)
        flux_e.append(length * jump_e[axis_id] - normal[axis_id] * along_e + cross_h)
    return flux_h + flux_e


def lifted_flux(jump_ref, flux_ref, derived_ref, lift_ref):
    groups = faces * face_nodes // 8

    def jump_of(comp_id):
        rows = strided_load(jump_ref, comp_id, faces * face_nodes, 8)
        return rows.reshape(groups, 8, new_count)

    normal = [derived_ref[16 + 8 * axis_id : 24 + 8 * axis_id, :][None] for axis_id in range(3)]
    fluxes = face_flux(jump_of, normal, derived_ref[40:48, :][None], derived_ref[48:56, :][None])
    for comp_id, value in enumerate(fluxes):
        flux_ref[0:40, comp_id * new_count : (comp_id + 1) * new_count] = value.reshape(
            faces * face_nodes, new_count
        )
    flux_ref[40:48, :] = jnp.zeros((8, components * new_count), jnp.float32)
    return dot_rows(lift_ref[...], table_terms(flux_ref[...]))


def strided_load(ref, start, size, stride):
    return jnp.concatenate(
        [ref[tile, pl.ds(start, size, stride=stride), :] for tile in range(ref.shape[0])], axis=1
    )


def tiled_store(ref, rows, value):
    for tile in range(ref.shape[0]):
        ref[tile, rows, :] = value[:, tile * lane : (tile + 1) * lane]


def tiled_load(ref, rows):
    return jnp.concatenate([ref[tile, rows, :] for tile in range(tiles)], axis=1)


def column_block(matrix, comp_id):
    return matrix[:24, comp_id * new_count : (comp_id + 1) * new_count]


def local_part(
    state_ref, derived_ref, link_ref, orient_ref, slope_ref, lift_ref, part_ref, nodes_ref, flat_ref, jump_ref, flux_ref
):
    nodes_ref[...] = jnp.zeros(nodes_ref.shape, jnp.float32)
    flat_ref[node_count:32, :] = jnp.zeros((12, components * new_count), jnp.float32)
    for comp_id in range(components):
        current = state_ref[comp_id]
        tiled_store(nodes_ref, pl.ds(comp_id, node_count, stride=8), current)
        flat_ref[0:node_count, comp_id * new_count : (comp_id + 1) * new_count] = current
    stacked = jnp.concatenate(split_three(tiled_load(nodes_ref, slice(None))), axis=1)
    rows = lax.broadcasted_iota(jnp.int32, (new_count, new_count), 0)
    links = [link_ref[face_id : face_id + 1, :] for face_id in range(faces)]
    owners = [face_of(link) for link in links]
    picks = [
        one_hot(rows == jnp.where(link < column_count, link - new_count * owner, -1))
        for link, owner in zip(links, owners)
    ]
    found_pairs = []
    for first in range(0, faces, 2):
        both = jnp.concatenate(picks[first : first + 2], axis=1)
        found_pairs.append(dot_rows(stacked, jnp.concatenate([both, both, both], axis=0)))
    comp_rows = lax.broadcasted_iota(jnp.int32, (8, new_count), 0)
    wall_gain = jnp.where(comp_rows >= 3, -2.0, 0.0)
    for face_id in range(faces):
        orient = orient_ref[face_id : face_id + 1, :]
        first_column = (face_id % 2) * new_count
        found = found_pairs[face_id // 2][:, first_column : first_column + new_count]
        owner_masks = [owners[face_id] == other for other in range(faces)]
        planes = []
        for node_id in range(face_nodes):
            value = None
            for other in range(faces):
                first_row = 8 * face_mask[other][node_id]
                plane = found[first_row : first_row + 8]
                value = plane if value is None else jnp.where(owner_masks[other], plane, value)
            planes.append(value)
        outside = oriented(planes, orient)
        wall = orient == 6
        for node_id in range(face_nodes):
            first_row = 8 * face_mask[face_id][node_id]
            inside = tiled_load(nodes_ref, slice(first_row, first_row + 8))
            jump = jnp.where(wall, wall_gain * inside, outside[node_id] - inside)
            target = 8 * (node_id * faces + face_id)
            tiled_store(jump_ref, slice(target, target + 8), jump)
    lifted = lifted_flux(jump_ref, flux_ref, derived_ref, lift_ref)
    slopes = dot_rows(slope_ref[...], table_terms(flat_ref[...]))
    inverse_jac = [
        [derived_ref[3 * row_id + axis_id : 3 * row_id + axis_id + 1, :] for axis_id in range(3)]
        for row_id in range(3)
    ]

    def gradient(axis_id, comp_id):
        columns = slice(comp_id * new_count, (comp_id + 1) * new_count)
        return (
            inverse_jac[0][axis_id] * slopes[0:24, columns]
            + inverse_jac[1][axis_id] * slopes[24:48, columns]
            + inverse_jac[2][axis_id] * slopes[48:72, columns]
        )

    inverse_eps = derived_ref[9:10, :]
    inverse_mu = derived_ref[10:11, :]
    for axis_id in range(3):
        after, last = (axis_id + 1) % 3, (axis_id + 2) % 3
        curl_h = gradient(after, last) - gradient(last, after)
        curl_e = gradient(after, 3 + last) - gradient(last, 3 + after)
        change_h = (column_block(lifted, axis_id) - curl_e) * inverse_mu
        change_e = (column_block(lifted, 3 + axis_id) + curl_h) * inverse_eps
        part_ref[axis_id] = change_h[:node_count]
        part_ref[3 + axis_id] = change_e[:node_count]


def arrive_kernel(
    came_ref,
    link_ref,
    orient_ref,
    slope_ref,
    lift_ref,
    list_ref,
    state_ref,
    derived_ref,
    far_ref,
    part_ref,
    chosen_ref,
    spread_ref,
    shared_ref,
    known_ref,
    scale_ref,
    rows_ref,
    tail_ref,
    main_ref,
    about_ref,
    codes_ref,
    *scratches,
):
    picks = plan(list_ref, link_ref, orient_ref, chosen_ref, spread_ref, about_ref, codes_ref)
    shared_ref[...] = dot_lanes(picks, spread_ref[...]).astype(jnp.bfloat16)
    derived_ref[...] = jnp.zeros(derived_ref.shape, jnp.float32)
    unpack(came_ref, state_ref, derived_ref, rows_ref, tail_ref, main_ref)
    compact(derived_ref, spread_ref, about_ref, far_ref)
    local_part(state_ref, derived_ref, link_ref, orient_ref, slope_ref, lift_ref, part_ref, *scratches)
    field_rows = components * node_count
    gain = section_b1 * time_step
    for comp_id in range(components):
        main_ref[comp_id * node_count : (comp_id + 1) * node_count, :] = (
            state_ref[comp_id] + gain * part_ref[comp_id]
        )
    main_ref[field_rows : field_rows + 1, :] = gain * derived_ref[10:11, :]
    main_ref[field_rows + 1 : field_rows + 2, :] = gain * derived_ref[9:10, :]
    main_ref[field_rows + 2 :, :] = jnp.zeros((6, new_count), jnp.float32)
    found = three_lanes(dot_lanes(picks, jnp.concatenate(split_three(main_ref[...]), axis=0)))
    known_ref[...] = trace_rows(found, chosen_ref[...])
    lanes = lax.broadcasted_iota(jnp.int32, (remote_count, lane), 1) % half_lane
    comp = lanes - (lanes // components) * components
    scale_ref[...] = trace_rows(found, jnp.where(comp < 3, field_rows, field_rows + 1))


def local_kernel(*refs):
    local_part(*refs)


def remote_part(came_ref, far_ref, lift_ref, turned_ref, jump_ref):
    turned_ref[...] = jnp.transpose(came_ref[...])
    planes = []
    for node_id in range(face_nodes):
        first_row = node_id * components
        halves_of = [
            turned_ref[half * half_lane + first_row : half * half_lane + first_row + 8, :]
            for half in range(2)
        ]
        planes.append(jnp.concatenate(halves_of, axis=1))
    outside = oriented(planes, far_ref[5:6, :])
    for node_id in range(face_nodes):
        tiled_store(jump_ref, slice(8 * node_id, 8 * node_id + 8), outside[node_id])
    blank = jnp.zeros((8 * (16 - face_nodes), remote_count), jnp.float32)
    tiled_store(jump_ref, slice(8 * face_nodes, 128), blank)
    fluxes = face_flux(
        lambda comp_id: strided_load(jump_ref, comp_id, 16, 8),
        [far_ref[axis_id : axis_id + 1, :] for axis_id in range(3)],
        far_ref[3:4, :],
        far_ref[4:5, :],
    )
    lifted = dot_rows(lift_ref[...], table_terms(jnp.concatenate(fluxes, axis=1)))
    face = far_ref[6:7, :]
    blocks = []
    for comp_id in range(components):
        columns = slice(comp_id * remote_count, (comp_id + 1) * remote_count)
        block = lifted[:24, columns]
        for face_id in range(1, faces):
            block = jnp.where(
                face == face_id, lifted[24 * face_id : 24 * face_id + 24, columns], block
            )
        blocks.append(block)
    return blocks


def placed_part(blocks, spread_ref, derived_ref, wanted):
    stacked = jnp.concatenate([blocks[comp_id] for comp_id in wanted], axis=0)
    rows = stacked.shape[0]
    parts = split_three(stacked)
    if rows % 16:
        blank = jnp.zeros((8, remote_count), jnp.float32)
        parts = split_three(jnp.concatenate([stacked, blank], axis=0))
    step = parts[0].shape[0]
    placed = dot_rows(jnp.concatenate(parts, axis=0), spread_ref[...])
    placed = placed[:rows] + placed[step : step + rows] + placed[2 * step : 2 * step + rows]
    scales = [derived_ref[10:11, :] if comp_id < 3 else derived_ref[9:10, :] for comp_id in wanted]
    return [
        (placed[24 * place : 24 * place + 24] * scale)[:node_count]
        for place, scale in enumerate(scales)
    ]


def first_kernel(
    came_ref,
    part_ref,
    state_ref,
    derived_ref,
    far_ref,
    spread_ref,
    lift_ref,
    shared_ref,
    known_ref,
    scale_ref,
    chosen_ref,
    residual_ref,
    middle_ref,
    trace_ref,
    send_ref,
    sem,
    packed_ref,
    *scratches,
):
    blocks = remote_part(came_ref, far_ref, lift_ref, *scratches)
    for comp_id, block in enumerate(blocks):
        packed_ref[comp_id * node_count : (comp_id + 1) * node_count, :] = block[:node_count]
    packed_ref[components * node_count :, :] = jnp.zeros((8, remote_count), jnp.float32)
    found = dot_lanes(shared_ref[...], jnp.concatenate(split_two(packed_ref[...]), axis=0))
    found = trace_rows(found[:, :lane] + found[:, lane:], chosen_ref[...])
    send_ref[...] = known_ref[...] + scale_ref[...] * found
    copy = pltpu.make_async_copy(send_ref, trace_ref, sem)
    copy.start()
    changes = placed_part(blocks, spread_ref, derived_ref, range(components))
    for comp_id in range(components):
        residual = time_step * (part_ref[comp_id] + changes[comp_id])
        residual_ref[comp_id] = residual
        middle_ref[comp_id] = state_ref[comp_id] + section_b1 * residual
    copy.wait()


def second_kernel(
    came_ref,
    part_ref,
    middle_ref,
    first_ref,
    derived_ref,
    far_ref,
    spread_ref,
    lift_ref,
    advanced_ref,
    residual_ref,
    done_ref,
    sems,
    *scratches,
):
    blocks = remote_part(came_ref, far_ref, lift_ref, *scratches)
    copies = []
    for first in range(0, components, 3):
        changes = placed_part(blocks, spread_ref, derived_ref, range(first, first + 3))
        for comp_id, change in zip(range(first, first + 3), changes):
            residual = section_a2 * first_ref[comp_id] + time_step * (part_ref[comp_id] + change)
            done_ref[0, comp_id] = middle_ref[comp_id] + section_b2 * residual
            done_ref[1, comp_id] = residual
        for place, out_ref in enumerate((advanced_ref, residual_ref)):
            copy = pltpu.make_async_copy(
                done_ref.at[place, pl.ds(first, 3)],
                out_ref.at[pl.ds(first, 3)],
                sems.at[place, first // 3],
            )
            copy.start()
            copies.append(copy)
    for copy in copies:
        copy.wait()


def floats(*shape):
    return jax.ShapeDtypeStruct(shape, jnp.float32)


def halves(*shape):
    return jax.ShapeDtypeStruct(shape, jnp.bfloat16)


def scratch(*shape):
    return pltpu.VMEM(shape, jnp.float32)


fast = pl.BlockSpec(memory_space=pltpu.VMEM)
free = pl.BlockSpec(memory_space=pl.ANY)


def run(kernel, name, outs, scratches, operands, in_specs=None, out_specs=None):
    return pl.pallas_call(
        kernel,
        name=name,
        out_shape=outs,
        in_specs=in_specs or [fast] * len(operands),
        out_specs=out_specs or jax.tree.map(lambda _: fast, outs),
        scratch_shapes=scratches,
        compiler_params=pltpu.CompilerParams(vmem_limit_bytes=24 * 2**20),
        cost_estimate=pl.CostEstimate(flops=10**8, bytes_accessed=10**6, transcendentals=0),
    )(*operands)


def shards(fields, geometry, migrate_list, trace_list, face_link, face_orient):
    slopes = slope_operand()
    lift = lift_operand()
    remote_lift = remote_lift_operand()
    state_shape = floats(components, node_count, new_count)
    trace_shape = floats(remote_count // 2, lane)
    local_scratch = [
        scratch(tiles, 8 * node_count, lane),
        scratch(32, components * new_count),
        scratch(tiles, 8 * faces * face_nodes, lane),
        scratch(48, components * new_count),
    ]
    remote_scratch = [scratch(lane, lane), scratch(2, lane, lane)]
    parcel = run(
        pack_kernel,
        "pack",
        floats(slabs * block_rows, lane),
        [
            scratch(components, node_count, old_count),
            scratch(11, old_count),
            pltpu.VMEM((slots, 1, slabs), jnp.int32),
            scratch(144, old_count),
            pltpu.SemaphoreType.DMA((3,)),
        ],
        [
            pltpu.with_memory_space_constraint(operand, pltpu.HBM)
            for operand in (fields, geometry, jnp.transpose(migrate_list, (2, 0, 1)))
        ],
        [pl.BlockSpec(memory_space=pltpu.HBM)] * 3,
    )
    arrived = lax.all_to_all(
        parcel.reshape(slabs, block_rows * lane), "slab", split_axis=0, concat_axis=0, tiled=True,
        axis_index_groups=[slab_order],
    ).reshape(slabs * block_rows, lane)
    code_scratch = pltpu.VMEM((remote_count, lane), jnp.int32)
    outgoing = run(
        start_kernel, "start", trace_shape, [code_scratch], (arrived, trace_list)
    )

    def exchange(rows):
        blocks = rows.reshape(subs, traces // 2, lane)
        came = lax.all_to_all(
            blocks, "sub", split_axis=0, concat_axis=0, tiled=True, axis_index_groups=[sub_order]
        )
        return came.reshape(remote_count // 2, lane)

    incoming = exchange(outgoing)
    state, derived, far, part, chosen, spread, shared, known, scale = run(
        arrive_kernel,
        "arrive",
        (
            state_shape,
            floats(64, new_count),
            floats(8, remote_count),
            state_shape,
            jax.ShapeDtypeStruct((remote_count, lane), jnp.int32),
            halves(remote_count, new_count),
            halves(remote_count, remote_count),
            floats(remote_count // 2, lane),
            floats(remote_count // 2, lane),
        ),
        [
            scratch(new_count, lane),
            scratch(new_count, lane),
            scratch(lane, new_count),
            scratch(8, remote_count),
            code_scratch,
        ]
        + local_scratch,
        (arrived, face_link, face_orient, slopes, lift, trace_list),
    )
    first_res, middle, outgoing = run(
        first_kernel,
        "first",
        (state_shape, state_shape, trace_shape),
        [scratch(remote_count // 2, lane), pltpu.SemaphoreType.DMA, scratch(lane, remote_count)]
        + remote_scratch,
        (
            incoming,
            part,
            state,
            derived,
            far,
            spread,
            remote_lift,
            shared,
            known,
            scale,
            chosen,
        ),
        out_specs=(fast, fast, free),
    )
    incoming = exchange(outgoing)
    part = run(
        local_kernel,
        "local",
        state_shape,
        local_scratch,
        (middle, derived, face_link, face_orient, slopes, lift),
    )
    return run(
        second_kernel,
        "second",
        (state_shape, state_shape),
        [scratch(2, components, node_count, new_count), pltpu.SemaphoreType.DMA((2, 2))]
        + remote_scratch,
        (incoming, part, middle, first_res, derived, far, spread, remote_lift),
        out_specs=(free, free),
    )


def solution(mesh):
    return jax.shard_map(
        shards,
        mesh=mesh,
        in_specs=(
            P(None, None, ("slab", "sub")),
            P(None, ("slab", "sub")),
            P(("slab", "sub"), None, None),
            P(("slab", "sub"), None, None),
            P(None, ("slab", "sub")),
            P(None, ("slab", "sub")),
        ),
        out_specs=(P(None, None, ("slab", "sub")), P(None, None, ("slab", "sub"))),
        check_vma=False,
    )
```

```python
import math

import jax
import jax.numpy as jnp
import ml_dtypes
import numpy as np
from jax import lax
from jax.experimental import pallas as pl
from jax.experimental.pallas import tpu as pltpu
from jax.sharding import PartitionSpec as P

time_step = 0.004
section_a2 = -0.4178904745
section_b1 = 0.1496590219993
section_b2 = 0.3792103129999
coordinate_perms = ((0, 1, 2), (1, 2, 0), (2, 0, 1), (0, 2, 1), (2, 1, 0), (1, 0, 2))
components = 6
node_count = 20
face_nodes = 10
faces = 4
old_count = 256
slots = 12
slabs = 32
subs = 16
traces = 16
new_count = slots * slabs
column_count = faces * new_count
remote_count = subs * traces
lane = 128
half_lane = lane // 2
tiles = new_count // lane
block_rows = slots + 1
slab_first = 21
sub_first = 10
slab_order = [(slab_first + place) % slabs for place in range(slabs)]
sub_order = [(sub_first + place) % subs for place in range(subs)]


def volume_triples():
    result_list = []
    for first_idx in range(4):
        for second_idx in range(4 - first_idx):
            for third_idx in range(4 - first_idx - second_idx):
                result_list.append((first_idx, second_idx, third_idx))
    return result_list


def planar_pairs():
    result_list = []
    for first_idx in range(4):
        for second_idx in range(4 - first_idx):
            result_list.append((first_idx, second_idx))
    return result_list


def monomial_matrix(points, powers):
    result_rows = []
    for point_item in points:
        row_values = []
        for power_item in powers:
            product_value = 1.0
            for axis_id in range(len(power_item)):
                product_value = product_value * point_item[axis_id] ** power_item[axis_id]
            row_values.append(product_value)
        result_rows.append(row_values)
    return result_rows


def mat_mul(left_rows, right_rows):
    inner_count = len(right_rows)
    col_count = len(right_rows[0])
    return [
        [
            sum((left_row[k_id] * right_rows[k_id][c_id] for k_id in range(inner_count)))
            for c_id in range(col_count)
        ]
        for left_row in left_rows
    ]


def transposed(matrix_rows):
    return [list(row_item) for row_item in zip(*matrix_rows)]


def invert(matrix_rows):
    order = len(matrix_rows)
    work_rows = [
        list(matrix_rows[r_id]) + [1.0 if r_id == c_id else 0.0 for c_id in range(order)]
        for r_id in range(order)
    ]
    for col_id in range(order):
        pivot_row = max(range(col_id, order), key=lambda r_id: abs(work_rows[r_id][col_id]))
        work_rows[col_id], work_rows[pivot_row] = (work_rows[pivot_row], work_rows[col_id])
        pivot_value = work_rows[col_id][col_id]
        work_rows[col_id] = [value / pivot_value for value in work_rows[col_id]]
        for r_id in range(order):
            if r_id != col_id:
                factor = work_rows[r_id][col_id]
                if factor != 0.0:
                    work_rows[r_id] = [
                        work_rows[r_id][c_id] - factor * work_rows[col_id][c_id]
                        for c_id in range(2 * order)
                    ]
    return [row_item[order:] for row_item in work_rows]


def moment_matrix(powers, extra_dim):
    total_terms = len(powers)
    result_matrix = [[0.0] * total_terms for _ in range(total_terms)]
    for row_id in range(total_terms):
        for col_id in range(total_terms):
            joined = [
                powers[row_id][a_id] + powers[col_id][a_id] for a_id in range(len(powers[row_id]))
            ]
            numerator = 1.0
            for exponent in joined:
                numerator = numerator * math.factorial(exponent)
            result_matrix[row_id][col_id] = numerator / math.factorial(sum(joined) + extra_dim)
    return result_matrix


def dg_tables():
    triples = volume_triples()
    points = [tuple((value / 3.0 for value in triple)) for triple in triples]
    inverse = invert(monomial_matrix(points, triples))
    slopes = []
    for axis_id in range(3):
        lowered = [
            tuple(
                (max(triple[a_id] - 1, 0) if a_id == axis_id else triple[a_id] for a_id in range(3))
            )
            for triple in triples
        ]
        base_rows = monomial_matrix(points, lowered)
        slope_values = [
            [triples[c_id][axis_id] * base_rows[r_id][c_id] for c_id in range(20)]
            for r_id in range(20)
        ]
        slopes.append(mat_mul(slope_values, inverse))
    volume_mass = mat_mul(mat_mul(transposed(inverse), moment_matrix(triples, 3)), inverse)
    planar = planar_pairs()
    face_points = [tuple((value / 3.0 for value in pair_item)) for pair_item in planar]
    face_inverse = invert(monomial_matrix(face_points, planar))
    face_mass = mat_mul(mat_mul(transposed(face_inverse), moment_matrix(planar, 2)), face_inverse)
    face_axes = ((0, 1), (0, 2), (0, 1), (1, 2))
    face_mask = [[0] * 10 for _ in range(4)]
    for face_id in range(4):
        for node_id, triple in enumerate(triples):
            on_face = (
                triple[2] == 0,
                triple[1] == 0,
                triple[0] + triple[1] + triple[2] == 3,
                triple[0] == 0,
            )[face_id]
            if on_face:
                key_pair = (triple[face_axes[face_id][0]], triple[face_axes[face_id][1]])
                face_mask[face_id][planar.index(key_pair)] = node_id
    surface = [[0.0] * 40 for _ in range(20)]
    for face_id in range(4):
        for row_id in range(10):
            for col_id in range(10):
                surface[face_mask[face_id][row_id]][face_id * 10 + col_id] += face_mass[row_id][
                    col_id
                ]
    lifting = mat_mul(invert(volume_mass), surface)
    lift_alt = [
        [lifting[n_id][f_id * 10 + j_id] for j_id in range(10) for f_id in range(4)]
        for n_id in range(20)
    ]
    node_perms = []
    for turn_id in range(6):
        perm_row = []
        for pair_item in planar:
            triple_face = (pair_item[0], pair_item[1], 3 - pair_item[0] - pair_item[1])
            moved_triple = [triple_face[coordinate_perms[turn_id][axis_id]] for axis_id in range(3)]
            perm_row.append(planar.index((moved_triple[0], moved_triple[1])))
        node_perms.append(perm_row)
    node_picks = [face_mask[f_id][j_id] for j_id in range(10) for f_id in range(4)]
    return slopes, lifting, face_mask, node_perms


def bf16_terms(matrix):
    rest = np.asarray(matrix, np.float64)
    parts = []
    for _ in range(3):
        part = rest.astype(np.float32).astype(ml_dtypes.bfloat16)
        parts.append(part)
        rest = rest - part.astype(np.float64)
    order = (0, 0, 1, 0, 1, 2)
    return jnp.asarray(np.concatenate([parts[place] for place in order], axis=1))


slope_table, lift_table, face_mask, node_perms = dg_tables()


def slope_operand():
    stacked = np.zeros((80, 32), np.float64)
    for axis_id in range(3):
        first_row = axis_id * 24
        stacked[first_row : first_row + node_count, :node_count] = slope_table[axis_id]
    return bf16_terms(stacked)


def lift_operand():
    stacked = np.zeros((32, 48), np.float64)
    for face_id in range(faces):
        for node_id in range(face_nodes):
            for row_id in range(node_count):
                stacked[row_id, node_id * faces + face_id] = lift_table[row_id][
                    face_id * face_nodes + node_id
                ]
    return bf16_terms(stacked)


def remote_lift_operand():
    stacked = np.zeros((24 * faces, 16), np.float64)
    for face_id in range(faces):
        for node_id in range(face_nodes):
            for row_id in range(node_count):
                stacked[24 * face_id + row_id, node_id] = lift_table[row_id][
                    face_id * face_nodes + node_id
                ]
    return bf16_terms(stacked)


def split_two(value):
    high = value.astype(jnp.bfloat16)
    rest = (value - high.astype(jnp.float32)).astype(jnp.bfloat16)
    return high, rest


def split_three(value):
    high = value.astype(jnp.bfloat16)
    left = value - high.astype(jnp.float32)
    middle = left.astype(jnp.bfloat16)
    rest = (left - middle.astype(jnp.float32)).astype(jnp.bfloat16)
    return high, middle, rest


def table_terms(value):
    high, middle, rest = split_three(value)
    return jnp.concatenate([high, middle, high, rest, middle, high], axis=0)


def three_lanes(found):
    return found[:, :lane] + found[:, lane : 2 * lane] + found[:, 2 * lane :]


def dot_rows(left, right):
    return lax.dot_general(
        left, right, (((1,), (0,)), ((), ())), preferred_element_type=jnp.float32
    )


def dot_lanes(left, right):
    return lax.dot_general(
        left, right, (((1,), (1,)), ((), ())), preferred_element_type=jnp.float32
    )


def one_hot(mask):
    return jnp.where(mask, 1.0, 0.0).astype(jnp.bfloat16)


def face_of(codes):
    return sum((codes >= step * new_count).astype(jnp.int32) for step in range(1, faces))


def pack_kernel(fields_ref, geometry_ref, list_ref, out_ref, took_ref, geo_ref, codes_ref, held_ref, sems):
    field_rows = components * node_count
    copies = [
        pltpu.make_async_copy(list_ref, codes_ref, sems.at[0]),
        pltpu.make_async_copy(fields_ref, took_ref, sems.at[1]),
        pltpu.make_async_copy(geometry_ref, geo_ref, sems.at[2]),
    ]
    for copy in copies:
        copy.start()
    copies[0].wait()
    turned = jnp.concatenate([codes_ref[slot_id] for slot_id in range(slots)], axis=0)
    turned = jnp.concatenate([turned, jnp.zeros((lane - slots, slabs), jnp.int32)], axis=0)
    turned = jnp.concatenate([turned, jnp.zeros((lane, lane - slabs), jnp.int32)], axis=1)
    codes = jnp.transpose(turned)[:slabs]
    codes = jnp.concatenate([codes[slab_first:], codes[:slab_first]], axis=0)
    lanes = lax.broadcasted_iota(jnp.int32, (slabs, old_count), 1)
    picks = jnp.concatenate(
        [one_hot(codes[:, slot_id : slot_id + 1] == lanes) for slot_id in range(slots)], axis=0
    )
    copies[1].wait()
    copies[2].wait()
    for comp_id in range(components):
        held_ref[comp_id * node_count : (comp_id + 1) * node_count, :] = took_ref[comp_id]
    held_ref[field_rows : field_rows + 11, :] = geo_ref[...]
    held_ref[field_rows + 11 :, :] = jnp.zeros((13, old_count), jnp.float32)
    parts = jnp.concatenate(split_three(held_ref[...]), axis=1)
    parts = jnp.concatenate([parts, jnp.zeros((112, 3 * old_count), jnp.bfloat16)], axis=0)
    moved = dot_lanes(jnp.concatenate([picks, picks, picks], axis=1), parts)
    short = lax.broadcasted_iota(jnp.int32, (slabs, lane), 1)
    diagonal = (short == field_rows) | (short == field_rows + 4)
    tail = jnp.zeros((slabs, lane), jnp.float32)
    for slot_id in range(slots):
        empty = codes[:, slot_id : slot_id + 1] < 0
        block = moved[slot_id * slabs : (slot_id + 1) * slabs]
        out_ref[pl.ds(slot_id, slabs, stride=block_rows), :] = jnp.where(
            empty & diagonal, 1.0, block[:, :lane]
        )
        ending = jnp.where(empty & (short < 3), 1.0, block[:, lane:])
        if slot_id:
            ending = pltpu.roll(ending, 3 * slot_id, 1)
        tail = tail + ending
    out_ref[pl.ds(slots, slabs, stride=block_rows), :] = tail


def trace_codes(list_ref, codes_ref):
    codes = list_ref[0]
    codes = jnp.concatenate([codes[sub_first:], codes[:sub_first]], axis=0)
    half = traces // 2
    for idx in range(traces):
        rows = pl.ds((idx // half) * lane + idx % half, subs, stride=half)
        codes_ref[rows, :] = jnp.broadcast_to(codes[:, idx : idx + 1], (subs, lane))
    codes = codes_ref[...]
    face = face_of(codes)
    return face, codes - new_count * face


def lane_picks(chosen, count):
    lanes = lax.broadcasted_iota(jnp.int32, (remote_count, lane), 1)
    return jnp.concatenate(
        [one_hot(chosen == lanes + tile * lane) for tile in range(count)], axis=1
    )


def plan(link_ref, orient_ref, spread_ref, about_ref):
    rows = lax.broadcasted_iota(jnp.int32, (remote_count, new_count), 0)
    about_rows = lax.broadcasted_iota(jnp.int32, (16, new_count), 0)
    about = None
    spread = None
    for face_id in range(faces):
        far = link_ref[face_id : face_id + 1, :] - column_count
        orient = orient_ref[face_id : face_id + 1, :]
        place = ((far >> 4) + subs - sub_first) & (subs - 1)
        column = ((far >> 3) & 1) * lane + place * 8 + (far & 7)
        column = jnp.where((far >= 0) & (orient < 6), column, -1)
        picks = one_hot(rows == column)
        facts = jnp.where(about_rows == 0, orient, jnp.where(about_rows == 1, face_id, 0))
        term = dot_lanes(facts.astype(jnp.float32).astype(jnp.bfloat16), picks)
        about = term if about is None else about + term
        spread = picks if spread is None else spread + picks
    spread_ref[...] = spread
    about_ref[...] = about[:8]


def node_lanes(face):
    lanes = lax.broadcasted_iota(jnp.int32, (1, lane), 1) % half_lane
    node = lanes // components
    comp = lanes - node * components
    tables = []
    for face_id in range(faces):
        row = jnp.zeros((1, lane), jnp.int32)
        for node_id in range(face_nodes):
            row = jnp.where(node == node_id, face_mask[face_id][node_id], row)
        tables.append(comp * node_count + row)
    chosen = tables[0]
    for face_id in range(1, faces):
        chosen = jnp.where(face == face_id, tables[face_id], chosen)
    return chosen


def trace_rows(found, chosen):
    turned = jnp.take_along_axis(found, chosen, axis=1, mode="promise_in_bounds")
    half = remote_count // 2
    lanes = lax.broadcasted_iota(jnp.int32, (half, lane), 1)
    return jnp.where(lanes < half_lane, turned[:half], turned[half:])


def start_kernel(
    came_ref,
    list_ref,
    trace_ref,
    chosen_ref,
    picks_ref,
    send_ref,
    codes_ref,
    sem,
):
    face, element = trace_codes(list_ref, codes_ref)
    chosen = node_lanes(face)
    source = (element * 5462) >> 16
    place = (source + slabs - slab_first) & (slabs - 1)
    picks = lane_picks(place * block_rows + element - source * slots, tiles + 1)
    parts = jnp.concatenate(split_three(came_ref[...]), axis=1)
    parts = jnp.concatenate(
        [parts, jnp.zeros((4 * lane - slabs * block_rows, 3 * lane), jnp.bfloat16)], axis=0
    )
    send_ref[...] = trace_rows(three_lanes(dot_rows(picks, parts)), chosen)
    copy = pltpu.make_async_copy(send_ref, trace_ref, sem)
    copy.start()
    chosen_ref[...] = chosen
    picks_ref[...] = lane_picks(element, tiles)
    copy.wait()


def unpack(came_ref, state_ref, derived_ref, rows_ref, tail_ref, main_ref):
    field_rows = components * node_count
    runs = ((slab_first, 0, slabs - slab_first), (0, slabs - slab_first, slab_first))
    tail = jnp.concatenate(
        [
            came_ref[pl.ds(place * block_rows + slots, count, stride=block_rows), :]
            for _, place, count in reversed(runs)
        ],
        axis=0,
    )
    for slot_id in range(slots):
        for source, place, count in runs:
            rows_ref[pl.ds(source * slots + slot_id, count, stride=slots), :] = came_ref[
                pl.ds(place * block_rows + slot_id, count, stride=block_rows), :
            ]
        shifted = pltpu.roll(tail, lane - 3 * slot_id, 1) if slot_id else tail
        tail_ref[pl.ds(slot_id, slabs, stride=slots), :] = shifted
    main_ref[...] = jnp.transpose(rows_ref[...])
    extra = jnp.transpose(tail_ref[...])[:8]
    for comp_id in range(components):
        state_ref[comp_id] = main_ref[comp_id * node_count : (comp_id + 1) * node_count, :]
    geo = [main_ref[field_rows + row_id : field_rows + row_id + 1, :] for row_id in range(8)]
    geo.append(extra[0:1])
    derived_ref[0:8, :] = main_ref[field_rows : field_rows + 8, :]
    derived_ref[8:9, :] = extra[0:1]
    derived_ref[9:10, :] = 1.0 / extra[1:2]
    derived_ref[10:11, :] = 1.0 / extra[2:3]
    total = None
    for axis_id in range(3):
        first, second, third = geo[axis_id], geo[3 + axis_id], geo[6 + axis_id]
        normal = 0.5 * jnp.concatenate([-third, -second, first + second + third, -first], axis=0)
        square = normal * normal
        total = square if total is None else total + square
        normal_rows = jnp.concatenate([normal, normal], axis=0)
        derived_ref[16 + 8 * axis_id : 24 + 8 * axis_id, :] = normal_rows
    length = jnp.sqrt(total)
    derived_ref[40:48, :] = jnp.concatenate([length, length], axis=0)
    inverse = 1.0 / length
    derived_ref[48:56, :] = jnp.concatenate([inverse, inverse], axis=0)


def compact(derived_ref, spread_ref, about_ref, far_ref):
    stacked = jnp.concatenate(split_three(derived_ref[16:64, :]), axis=0)
    found = dot_lanes(stacked, spread_ref[...])
    found = found[:48] + found[48:96] + found[96:]
    face = about_ref[1:2, :]
    for block in range(5):
        first_row = 8 * block
        value = found[first_row : first_row + 1]
        for face_id in range(1, faces):
            row_id = first_row + face_id
            value = jnp.where(face == face_id, found[row_id : row_id + 1], value)
        far_ref[block : block + 1, :] = value
    far_ref[5:7, :] = about_ref[0:2, :]
    far_ref[7:8, :] = jnp.zeros((1, remote_count), jnp.float32)


def oriented(planes, orient):
    masks = [orient == turn_id for turn_id in range(6)]
    result = []
    for node_id in range(face_nodes):
        sources = {}
        for turn_id in range(6):
            sources.setdefault(node_perms[turn_id][node_id], []).append(turn_id)
        value = None
        for source, turn_ids in sources.items():
            if value is None:
                value = planes[source]
                continue
            mask = masks[turn_ids[0]]
            for turn_id in turn_ids[1:]:
                mask = mask | masks[turn_id]
            value = jnp.where(mask, planes[source], value)
        result.append(value)
    return result


def face_flux(jump_of, normal, length, inverse):
    jump_h = [jump_of(comp_id) for comp_id in range(3)]
    jump_e = [jump_of(comp_id) for comp_id in range(3, 6)]

    def along(jump):
        total = normal[0] * jump[0] + normal[1] * jump[1] + normal[2] * jump[2]
        return total * inverse

    along_h = along(jump_h)
    along_e = along(jump_e)
    flux_h, flux_e = [], []
    for axis_id in range(3):
        after, last = (axis_id + 1) % 3, (axis_id + 2) % 3
        cross_e = normal[after] * jump_e[last] - normal[last] * jump_e[after]
        cross_h = normal[after] * jump_h[last] - normal[last] * jump_h[after]
        flux_h.append(length * jump_h[axis_id] - normal[axis_id] * along_h - cross_e)
        flux_e.append(length * jump_e[axis_id] - normal[axis_id] * along_e + cross_h)
    return flux_h + flux_e


def lifted_flux(jump_ref, flux_ref, derived_ref, lift_ref):
    groups = faces * face_nodes // 8

    def jump_of(comp_id):
        rows = strided_load(jump_ref, comp_id, faces * face_nodes, 8)
        return rows.reshape(groups, 8, new_count)

    normal = [derived_ref[16 + 8 * axis_id : 24 + 8 * axis_id, :][None] for axis_id in range(3)]
    fluxes = face_flux(jump_of, normal, derived_ref[40:48, :][None], derived_ref[48:56, :][None])
    for comp_id, value in enumerate(fluxes):
        flux_ref[0:40, comp_id * new_count : (comp_id + 1) * new_count] = value.reshape(
            faces * face_nodes, new_count
        )
    flux_ref[40:48, :] = jnp.zeros((8, components * new_count), jnp.float32)
    return dot_rows(lift_ref[...], table_terms(flux_ref[...]))


def strided_load(ref, start, size, stride):
    return jnp.concatenate(
        [ref[tile, pl.ds(start, size, stride=stride), :] for tile in range(ref.shape[0])], axis=1
    )


def tiled_store(ref, rows, value):
    for tile in range(ref.shape[0]):
        ref[tile, rows, :] = value[:, tile * lane : (tile + 1) * lane]


def tiled_load(ref, rows):
    return jnp.concatenate([ref[tile, rows, :] for tile in range(tiles)], axis=1)


def column_block(matrix, comp_id):
    return matrix[:24, comp_id * new_count : (comp_id + 1) * new_count]


def local_part(
    state_ref, derived_ref, link_ref, orient_ref, slope_ref, lift_ref, part_ref, nodes_ref, flat_ref, jump_ref, flux_ref
):
    nodes_ref[...] = jnp.zeros(nodes_ref.shape, jnp.float32)
    flat_ref[node_count:32, :] = jnp.zeros((12, components * new_count), jnp.float32)
    for comp_id in range(components):
        current = state_ref[comp_id]
        tiled_store(nodes_ref, pl.ds(comp_id, node_count, stride=8), current)
        flat_ref[0:node_count, comp_id * new_count : (comp_id + 1) * new_count] = current
    stacked = jnp.concatenate(split_three(tiled_load(nodes_ref, slice(None))), axis=1)
    rows = lax.broadcasted_iota(jnp.int32, (new_count, new_count), 0)
    links = [link_ref[face_id : face_id + 1, :] for face_id in range(faces)]
    owners = [face_of(link) for link in links]
    picks = [
        one_hot(rows == jnp.where(link < column_count, link - new_count * owner, -1))
        for link, owner in zip(links, owners)
    ]
    found_pairs = []
    for first in range(0, faces, 2):
        both = jnp.concatenate(picks[first : first + 2], axis=1)
        found_pairs.append(dot_rows(stacked, jnp.concatenate([both, both, both], axis=0)))
    comp_rows = lax.broadcasted_iota(jnp.int32, (8, new_count), 0)
    wall_gain = jnp.where(comp_rows >= 3, -2.0, 0.0)
    for face_id in range(faces):
        orient = orient_ref[face_id : face_id + 1, :]
        first_column = (face_id % 2) * new_count
        found = found_pairs[face_id // 2][:, first_column : first_column + new_count]
        owner_masks = [owners[face_id] == other for other in range(faces)]
        planes = []
        for node_id in range(face_nodes):
            value = None
            for other in range(faces):
                first_row = 8 * face_mask[other][node_id]
                plane = found[first_row : first_row + 8]
                value = plane if value is None else jnp.where(owner_masks[other], plane, value)
            planes.append(value)
        outside = oriented(planes, orient)
        wall = orient == 6
        for node_id in range(face_nodes):
            first_row = 8 * face_mask[face_id][node_id]
            inside = tiled_load(nodes_ref, slice(first_row, first_row + 8))
            jump = jnp.where(wall, wall_gain * inside, outside[node_id] - inside)
            target = 8 * (node_id * faces + face_id)
            tiled_store(jump_ref, slice(target, target + 8), jump)
    lifted = lifted_flux(jump_ref, flux_ref, derived_ref, lift_ref)
    slopes = dot_rows(slope_ref[...], table_terms(flat_ref[...]))
    inverse_jac = [
        [derived_ref[3 * row_id + axis_id : 3 * row_id + axis_id + 1, :] for axis_id in range(3)]
        for row_id in range(3)
    ]

    def gradient(axis_id, comp_id):
        columns = slice(comp_id * new_count, (comp_id + 1) * new_count)
        return (
            inverse_jac[0][axis_id] * slopes[0:24, columns]
            + inverse_jac[1][axis_id] * slopes[24:48, columns]
            + inverse_jac[2][axis_id] * slopes[48:72, columns]
        )

    inverse_eps = derived_ref[9:10, :]
    inverse_mu = derived_ref[10:11, :]
    for axis_id in range(3):
        after, last = (axis_id + 1) % 3, (axis_id + 2) % 3
        curl_h = gradient(after, last) - gradient(last, after)
        curl_e = gradient(after, 3 + last) - gradient(last, 3 + after)
        change_h = (column_block(lifted, axis_id) - curl_e) * inverse_mu
        change_e = (column_block(lifted, 3 + axis_id) + curl_h) * inverse_eps
        part_ref[axis_id] = change_h[:node_count]
        part_ref[3 + axis_id] = change_e[:node_count]


def arrive_kernel(
    came_ref,
    link_ref,
    orient_ref,
    slope_ref,
    lift_ref,
    chosen_ref,
    picks_ref,
    state_ref,
    derived_ref,
    far_ref,
    part_ref,
    known_ref,
    scale_ref,
    spread_ref,
    shared_ref,
    rows_ref,
    tail_ref,
    main_ref,
    about_ref,
    *scratches,
):
    plan(link_ref, orient_ref, spread_ref, about_ref)
    shared_ref[...] = dot_lanes(picks_ref[...], spread_ref[...]).astype(jnp.bfloat16)
    derived_ref[...] = jnp.zeros(derived_ref.shape, jnp.float32)
    unpack(came_ref, state_ref, derived_ref, rows_ref, tail_ref, main_ref)
    compact(derived_ref, spread_ref, about_ref, far_ref)
    local_part(state_ref, derived_ref, link_ref, orient_ref, slope_ref, lift_ref, part_ref, *scratches)
    field_rows = components * node_count
    gain = section_b1 * time_step
    for comp_id in range(components):
        main_ref[comp_id * node_count : (comp_id + 1) * node_count, :] = (
            state_ref[comp_id] + gain * part_ref[comp_id]
        )
    main_ref[field_rows : field_rows + 1, :] = gain * derived_ref[10:11, :]
    main_ref[field_rows + 1 : field_rows + 2, :] = gain * derived_ref[9:10, :]
    main_ref[field_rows + 2 :, :] = jnp.zeros((6, new_count), jnp.float32)
    found = three_lanes(dot_lanes(picks_ref[...], jnp.concatenate(split_three(main_ref[...]), axis=0)))
    known_ref[...] = trace_rows(found, chosen_ref[...])
    lanes = lax.broadcasted_iota(jnp.int32, (remote_count, lane), 1) % half_lane
    comp = lanes - (lanes // components) * components
    scale_ref[...] = trace_rows(found, jnp.where(comp < 3, field_rows, field_rows + 1))


def local_kernel(*refs):
    local_part(*refs)


def remote_part(came_ref, far_ref, lift_ref, turned_ref, jump_ref):
    turned_ref[...] = jnp.transpose(came_ref[...])
    planes = []
    for node_id in range(face_nodes):
        first_row = node_id * components
        halves_of = [
            turned_ref[half * half_lane + first_row : half * half_lane + first_row + 8, :]
            for half in range(2)
        ]
        planes.append(jnp.concatenate(halves_of, axis=1))
    outside = oriented(planes, far_ref[5:6, :])
    for node_id in range(face_nodes):
        tiled_store(jump_ref, slice(8 * node_id, 8 * node_id + 8), outside[node_id])
    blank = jnp.zeros((8 * (16 - face_nodes), remote_count), jnp.float32)
    tiled_store(jump_ref, slice(8 * face_nodes, 128), blank)
    fluxes = face_flux(
        lambda comp_id: strided_load(jump_ref, comp_id, 16, 8),
        [far_ref[axis_id : axis_id + 1, :] for axis_id in range(3)],
        far_ref[3:4, :],
        far_ref[4:5, :],
    )
    lifted = dot_rows(lift_ref[...], table_terms(jnp.concatenate(fluxes, axis=1)))
    face = far_ref[6:7, :]
    blocks = []
    for comp_id in range(components):
        columns = slice(comp_id * remote_count, (comp_id + 1) * remote_count)
        block = lifted[:24, columns]
        for face_id in range(1, faces):
            block = jnp.where(
                face == face_id, lifted[24 * face_id : 24 * face_id + 24, columns], block
            )
        blocks.append(block)
    return blocks


def placed_part(blocks, spread_ref, derived_ref, wanted):
    stacked = jnp.concatenate([blocks[comp_id] for comp_id in wanted], axis=0)
    rows = stacked.shape[0]
    parts = split_three(stacked)
    if rows % 16:
        blank = jnp.zeros((8, remote_count), jnp.float32)
        parts = split_three(jnp.concatenate([stacked, blank], axis=0))
    step = parts[0].shape[0]
    placed = dot_rows(jnp.concatenate(parts, axis=0), spread_ref[...])
    placed = placed[:rows] + placed[step : step + rows] + placed[2 * step : 2 * step + rows]
    scales = [derived_ref[10:11, :] if comp_id < 3 else derived_ref[9:10, :] for comp_id in wanted]
    return [
        (placed[24 * place : 24 * place + 24] * scale)[:node_count]
        for place, scale in enumerate(scales)
    ]


def first_kernel(
    came_ref,
    part_ref,
    state_ref,
    derived_ref,
    far_ref,
    spread_ref,
    lift_ref,
    shared_ref,
    known_ref,
    scale_ref,
    chosen_ref,
    residual_ref,
    middle_ref,
    trace_ref,
    send_ref,
    sem,
    packed_ref,
    *scratches,
):
    blocks = remote_part(came_ref, far_ref, lift_ref, *scratches)
    for comp_id, block in enumerate(blocks):
        packed_ref[comp_id * node_count : (comp_id + 1) * node_count, :] = block[:node_count]
    packed_ref[components * node_count :, :] = jnp.zeros((8, remote_count), jnp.float32)
    found = dot_lanes(shared_ref[...], jnp.concatenate(split_two(packed_ref[...]), axis=0))
    found = trace_rows(found[:, :lane] + found[:, lane:], chosen_ref[...])
    send_ref[...] = known_ref[...] + scale_ref[...] * found
    copy = pltpu.make_async_copy(send_ref, trace_ref, sem)
    copy.start()
    changes = placed_part(blocks, spread_ref, derived_ref, range(components))
    for comp_id in range(components):
        residual = time_step * (part_ref[comp_id] + changes[comp_id])
        residual_ref[comp_id] = residual
        middle_ref[comp_id] = state_ref[comp_id] + section_b1 * residual
    copy.wait()


def second_kernel(
    came_ref,
    part_ref,
    middle_ref,
    first_ref,
    derived_ref,
    far_ref,
    spread_ref,
    lift_ref,
    advanced_ref,
    residual_ref,
    done_ref,
    sems,
    *scratches,
):
    blocks = remote_part(came_ref, far_ref, lift_ref, *scratches)
    copies = []
    for first in range(0, components, 3):
        changes = placed_part(blocks, spread_ref, derived_ref, range(first, first + 3))
        for comp_id, change in zip(range(first, first + 3), changes):
            residual = section_a2 * first_ref[comp_id] + time_step * (part_ref[comp_id] + change)
            done_ref[0, comp_id] = middle_ref[comp_id] + section_b2 * residual
            done_ref[1, comp_id] = residual
        for place, out_ref in enumerate((advanced_ref, residual_ref)):
            copy = pltpu.make_async_copy(
                done_ref.at[place, pl.ds(first, 3)],
                out_ref.at[pl.ds(first, 3)],
                sems.at[place, first // 3],
            )
            copy.start()
            copies.append(copy)
    for copy in copies:
        copy.wait()


def floats(*shape):
    return jax.ShapeDtypeStruct(shape, jnp.float32)


def halves(*shape):
    return jax.ShapeDtypeStruct(shape, jnp.bfloat16)


def scratch(*shape):
    return pltpu.VMEM(shape, jnp.float32)


fast = pl.BlockSpec(memory_space=pltpu.VMEM)
free = pl.BlockSpec(memory_space=pl.ANY)


def run(kernel, name, outs, scratches, operands, in_specs=None, out_specs=None):
    return pl.pallas_call(
        kernel,
        name=name,
        out_shape=outs,
        in_specs=in_specs or [fast] * len(operands),
        out_specs=out_specs or jax.tree.map(lambda _: fast, outs),
        scratch_shapes=scratches,
        compiler_params=pltpu.CompilerParams(vmem_limit_bytes=24 * 2**20),
        cost_estimate=pl.CostEstimate(flops=10**8, bytes_accessed=10**6, transcendentals=0),
    )(*operands)


def shards(fields, geometry, migrate_list, trace_list, face_link, face_orient):
    slopes = slope_operand()
    lift = lift_operand()
    remote_lift = remote_lift_operand()
    state_shape = floats(components, node_count, new_count)
    trace_shape = floats(remote_count // 2, lane)
    local_scratch = [
        scratch(tiles, 8 * node_count, lane),
        scratch(32, components * new_count),
        scratch(tiles, 8 * faces * face_nodes, lane),
        scratch(48, components * new_count),
    ]
    remote_scratch = [scratch(lane, lane), scratch(2, lane, lane)]
    parcel = run(
        pack_kernel,
        "pack",
        floats(slabs * block_rows, lane),
        [
            scratch(components, node_count, old_count),
            scratch(11, old_count),
            pltpu.VMEM((slots, 1, slabs), jnp.int32),
            scratch(144, old_count),
            pltpu.SemaphoreType.DMA((3,)),
        ],
        [
            pltpu.with_memory_space_constraint(operand, pltpu.HBM)
            for operand in (fields, geometry, jnp.transpose(migrate_list, (2, 0, 1)))
        ],
        [pl.BlockSpec(memory_space=pltpu.HBM)] * 3,
    )
    arrived = lax.all_to_all(
        parcel.reshape(slabs, block_rows * lane), "slab", split_axis=0, concat_axis=0, tiled=True,
        axis_index_groups=[slab_order],
    ).reshape(slabs * block_rows, lane)
    outgoing, chosen, picks = run(
        start_kernel,
        "start",
        (
            trace_shape,
            jax.ShapeDtypeStruct((remote_count, lane), jnp.int32),
            halves(remote_count, new_count),
        ),
        [
            scratch(remote_count // 2, lane),
            pltpu.VMEM((remote_count, lane), jnp.int32),
            pltpu.SemaphoreType.DMA,
        ],
        (arrived, trace_list),
        out_specs=(free, fast, fast),
    )

    def exchange(rows):
        blocks = rows.reshape(subs, traces // 2, lane)
        came = lax.all_to_all(
            blocks, "sub", split_axis=0, concat_axis=0, tiled=True, axis_index_groups=[sub_order]
        )
        return came.reshape(remote_count // 2, lane)

    incoming = exchange(outgoing)
    state, derived, far, part, known, scale, spread, shared = run(
        arrive_kernel,
        "arrive",
        (
            state_shape,
            floats(64, new_count),
            floats(8, remote_count),
            state_shape,
            floats(remote_count // 2, lane),
            floats(remote_count // 2, lane),
            halves(remote_count, new_count),
            halves(remote_count, remote_count),
        ),
        [
            scratch(new_count, lane),
            scratch(new_count, lane),
            scratch(lane, new_count),
            scratch(8, remote_count),
        ]
        + local_scratch,
        (arrived, face_link, face_orient, slopes, lift, chosen, picks),
    )
    first_res, middle, outgoing = run(
        first_kernel,
        "first",
        (state_shape, state_shape, trace_shape),
        [scratch(remote_count // 2, lane), pltpu.SemaphoreType.DMA, scratch(lane, remote_count)]
        + remote_scratch,
        (
            incoming,
            part,
            state,
            derived,
            far,
            spread,
            remote_lift,
            shared,
            known,
            scale,
            chosen,
        ),
        out_specs=(fast, fast, free),
    )
    incoming = exchange(outgoing)
    part = run(
        local_kernel,
        "local",
        state_shape,
        local_scratch,
        (middle, derived, face_link, face_orient, slopes, lift),
    )
    return run(
        second_kernel,
        "second",
        (state_shape, state_shape),
        [scratch(2, components, node_count, new_count), pltpu.SemaphoreType.DMA((2, 2))]
        + remote_scratch,
        (incoming, part, middle, first_res, derived, far, spread, remote_lift),
        out_specs=(free, free),
    )


def solution(mesh):
    return jax.shard_map(
        shards,
        mesh=mesh,
        in_specs=(
            P(None, None, ("slab", "sub")),
            P(None, ("slab", "sub")),
            P(("slab", "sub"), None, None),
            P(("slab", "sub"), None, None),
            P(None, ("slab", "sub")),
            P(None, ("slab", "sub")),
        ),
        out_specs=(P(None, None, ("slab", "sub")), P(None, None, ("slab", "sub"))),
        check_vma=False,
    )
```

```python
import math

import jax
import jax.numpy as jnp
import ml_dtypes
import numpy as np
from jax import lax
from jax.experimental import pallas as pl
from jax.experimental.pallas import tpu as pltpu
from jax.sharding import PartitionSpec as P

time_step = 0.004
section_a2 = -0.4178904745
section_b1 = 0.1496590219993
section_b2 = 0.3792103129999
coordinate_perms = ((0, 1, 2), (1, 2, 0), (2, 0, 1), (0, 2, 1), (2, 1, 0), (1, 0, 2))
components = 6
node_count = 20
face_nodes = 10
faces = 4
old_count = 256
slots = 12
slabs = 32
subs = 16
traces = 16
new_count = slots * slabs
column_count = faces * new_count
remote_count = subs * traces
lane = 128
half_lane = lane // 2
tiles = new_count // lane
block_rows = slots + 1
slab_first = 21
sub_first = 10
slab_order = [
    (slab_first + slabs // 2 * (place // 2 % 2) + place // 4 * 2 + place % 2) % slabs
    for place in range(slabs)
]
slab_runs = []
for start in range(4):
    for place in range(start, slabs, 4):
        if place > start and slab_order[place] == slab_order[place - 4] + 2:
            slab_runs[-1][2] += 1
        else:
            slab_runs.append([slab_order[place], place, 1])
sub_order = [(sub_first + place) % subs for place in range(subs)]


def volume_triples():
    result_list = []
    for first_idx in range(4):
        for second_idx in range(4 - first_idx):
            for third_idx in range(4 - first_idx - second_idx):
                result_list.append((first_idx, second_idx, third_idx))
    return result_list


def planar_pairs():
    result_list = []
    for first_idx in range(4):
        for second_idx in range(4 - first_idx):
            result_list.append((first_idx, second_idx))
    return result_list


def monomial_matrix(points, powers):
    result_rows = []
    for point_item in points:
        row_values = []
        for power_item in powers:
            product_value = 1.0
            for axis_id in range(len(power_item)):
                product_value = product_value * point_item[axis_id] ** power_item[axis_id]
            row_values.append(product_value)
        result_rows.append(row_values)
    return result_rows


def mat_mul(left_rows, right_rows):
    inner_count = len(right_rows)
    col_count = len(right_rows[0])
    return [
        [
            sum((left_row[k_id] * right_rows[k_id][c_id] for k_id in range(inner_count)))
            for c_id in range(col_count)
        ]
        for left_row in left_rows
    ]


def transposed(matrix_rows):
    return [list(row_item) for row_item in zip(*matrix_rows)]


def invert(matrix_rows):
    order = len(matrix_rows)
    work_rows = [
        list(matrix_rows[r_id]) + [1.0 if r_id == c_id else 0.0 for c_id in range(order)]
        for r_id in range(order)
    ]
    for col_id in range(order):
        pivot_row = max(range(col_id, order), key=lambda r_id: abs(work_rows[r_id][col_id]))
        work_rows[col_id], work_rows[pivot_row] = (work_rows[pivot_row], work_rows[col_id])
        pivot_value = work_rows[col_id][col_id]
        work_rows[col_id] = [value / pivot_value for value in work_rows[col_id]]
        for r_id in range(order):
            if r_id != col_id:
                factor = work_rows[r_id][col_id]
                if factor != 0.0:
                    work_rows[r_id] = [
                        work_rows[r_id][c_id] - factor * work_rows[col_id][c_id]
                        for c_id in range(2 * order)
                    ]
    return [row_item[order:] for row_item in work_rows]


def moment_matrix(powers, extra_dim):
    total_terms = len(powers)
    result_matrix = [[0.0] * total_terms for _ in range(total_terms)]
    for row_id in range(total_terms):
        for col_id in range(total_terms):
            joined = [
                powers[row_id][a_id] + powers[col_id][a_id] for a_id in range(len(powers[row_id]))
            ]
            numerator = 1.0
            for exponent in joined:
                numerator = numerator * math.factorial(exponent)
            result_matrix[row_id][col_id] = numerator / math.factorial(sum(joined) + extra_dim)
    return result_matrix


def dg_tables():
    triples = volume_triples()
    points = [tuple((value / 3.0 for value in triple)) for triple in triples]
    inverse = invert(monomial_matrix(points, triples))
    slopes = []
    for axis_id in range(3):
        lowered = [
            tuple(
                (max(triple[a_id] - 1, 0) if a_id == axis_id else triple[a_id] for a_id in range(3))
            )
            for triple in triples
        ]
        base_rows = monomial_matrix(points, lowered)
        slope_values = [
            [triples[c_id][axis_id] * base_rows[r_id][c_id] for c_id in range(20)]
            for r_id in range(20)
        ]
        slopes.append(mat_mul(slope_values, inverse))
    volume_mass = mat_mul(mat_mul(transposed(inverse), moment_matrix(triples, 3)), inverse)
    planar = planar_pairs()
    face_points = [tuple((value / 3.0 for value in pair_item)) for pair_item in planar]
    face_inverse = invert(monomial_matrix(face_points, planar))
    face_mass = mat_mul(mat_mul(transposed(face_inverse), moment_matrix(planar, 2)), face_inverse)
    face_axes = ((0, 1), (0, 2), (0, 1), (1, 2))
    face_mask = [[0] * 10 for _ in range(4)]
    for face_id in range(4):
        for node_id, triple in enumerate(triples):
            on_face = (
                triple[2] == 0,
                triple[1] == 0,
                triple[0] + triple[1] + triple[2] == 3,
                triple[0] == 0,
            )[face_id]
            if on_face:
                key_pair = (triple[face_axes[face_id][0]], triple[face_axes[face_id][1]])
                face_mask[face_id][planar.index(key_pair)] = node_id
    surface = [[0.0] * 40 for _ in range(20)]
    for face_id in range(4):
        for row_id in range(10):
            for col_id in range(10):
                surface[face_mask[face_id][row_id]][face_id * 10 + col_id] += face_mass[row_id][
                    col_id
                ]
    lifting = mat_mul(invert(volume_mass), surface)
    lift_alt = [
        [lifting[n_id][f_id * 10 + j_id] for j_id in range(10) for f_id in range(4)]
        for n_id in range(20)
    ]
    node_perms = []
    for turn_id in range(6):
        perm_row = []
        for pair_item in planar:
            triple_face = (pair_item[0], pair_item[1], 3 - pair_item[0] - pair_item[1])
            moved_triple = [triple_face[coordinate_perms[turn_id][axis_id]] for axis_id in range(3)]
            perm_row.append(planar.index((moved_triple[0], moved_triple[1])))
        node_perms.append(perm_row)
    node_picks = [face_mask[f_id][j_id] for j_id in range(10) for f_id in range(4)]
    return slopes, lifting, face_mask, node_perms


def bf16_terms(matrix):
    rest = np.asarray(matrix, np.float64)
    parts = []
    for _ in range(3):
        part = rest.astype(np.float32).astype(ml_dtypes.bfloat16)
        parts.append(part)
        rest = rest - part.astype(np.float64)
    order = (0, 0, 1, 0, 1, 2)
    return jnp.asarray(np.concatenate([parts[place] for place in order], axis=1))


slope_table, lift_table, face_mask, node_perms = dg_tables()


def slope_operand():
    stacked = np.zeros((80, 32), np.float64)
    for axis_id in range(3):
        first_row = axis_id * 24
        stacked[first_row : first_row + node_count, :node_count] = slope_table[axis_id]
    return bf16_terms(stacked)


def lift_operand():
    stacked = np.zeros((32, 48), np.float64)
    for face_id in range(faces):
        for node_id in range(face_nodes):
            for row_id in range(node_count):
                stacked[row_id, node_id * faces + face_id] = lift_table[row_id][
                    face_id * face_nodes + node_id
                ]
    return bf16_terms(stacked)


def remote_lift_operand():
    stacked = np.zeros((24 * faces, 16), np.float64)
    for face_id in range(faces):
        for node_id in range(face_nodes):
            for row_id in range(node_count):
                stacked[24 * face_id + row_id, node_id] = lift_table[row_id][
                    face_id * face_nodes + node_id
                ]
    return bf16_terms(stacked)


def split_two(value):
    high = value.astype(jnp.bfloat16)
    rest = (value - high.astype(jnp.float32)).astype(jnp.bfloat16)
    return high, rest


def split_three(value):
    high = value.astype(jnp.bfloat16)
    left = value - high.astype(jnp.float32)
    middle = left.astype(jnp.bfloat16)
    rest = (left - middle.astype(jnp.float32)).astype(jnp.bfloat16)
    return high, middle, rest


def table_terms(value):
    high, middle, rest = split_three(value)
    return jnp.concatenate([high, middle, high, rest, middle, high], axis=0)


def three_lanes(found):
    return found[:, :lane] + found[:, lane : 2 * lane] + found[:, 2 * lane :]


def dot_rows(left, right):
    return lax.dot_general(
        left, right, (((1,), (0,)), ((), ())), preferred_element_type=jnp.float32
    )


def dot_lanes(left, right):
    return lax.dot_general(
        left, right, (((1,), (1,)), ((), ())), preferred_element_type=jnp.float32
    )


def one_hot(mask):
    return jnp.where(mask, 1.0, 0.0).astype(jnp.bfloat16)


def face_of(codes):
    return sum((codes >= step * new_count).astype(jnp.int32) for step in range(1, faces))


def pack_kernel(fields_ref, geometry_ref, list_ref, out_ref, took_ref, geo_ref, codes_ref, held_ref, sems):
    field_rows = components * node_count
    copies = [
        pltpu.make_async_copy(list_ref, codes_ref, sems.at[0]),
        pltpu.make_async_copy(fields_ref, took_ref, sems.at[1]),
        pltpu.make_async_copy(geometry_ref, geo_ref, sems.at[2]),
    ]
    for copy in copies:
        copy.start()
    copies[0].wait()
    turned = jnp.concatenate([codes_ref[slot_id] for slot_id in range(slots)], axis=0)
    turned = jnp.concatenate([turned, jnp.zeros((lane - slots, slabs), jnp.int32)], axis=0)
    turned = jnp.concatenate([turned, jnp.zeros((lane, lane - slabs), jnp.int32)], axis=1)
    place = lax.broadcasted_iota(jnp.int32, (lane, lane), 1)
    slab = ((place >> 1) & 1) * (slabs // 2) + (place >> 2) * 2 + (place & 1) + slab_first
    turned = jnp.take_along_axis(turned, slab & (slabs - 1), axis=1, mode="promise_in_bounds")
    codes = jnp.transpose(turned)[:slabs]
    lanes = lax.broadcasted_iota(jnp.int32, (slabs, old_count), 1)
    picks = jnp.concatenate(
        [one_hot(codes[:, slot_id : slot_id + 1] == lanes) for slot_id in range(slots)], axis=0
    )
    copies[1].wait()
    copies[2].wait()
    for comp_id in range(components):
        held_ref[comp_id * node_count : (comp_id + 1) * node_count, :] = took_ref[comp_id]
    held_ref[field_rows : field_rows + 11, :] = geo_ref[...]
    held_ref[field_rows + 11 :, :] = jnp.zeros((13, old_count), jnp.float32)
    parts = jnp.concatenate(split_three(held_ref[...]), axis=1)
    parts = jnp.concatenate([parts, jnp.zeros((112, 3 * old_count), jnp.bfloat16)], axis=0)
    moved = dot_lanes(jnp.concatenate([picks, picks, picks], axis=1), parts)
    short = lax.broadcasted_iota(jnp.int32, (slabs, lane), 1)
    diagonal = (short == field_rows) | (short == field_rows + 4)
    tail = jnp.zeros((slabs, lane), jnp.float32)
    for slot_id in range(slots):
        empty = codes[:, slot_id : slot_id + 1] < 0
        block = moved[slot_id * slabs : (slot_id + 1) * slabs]
        out_ref[pl.ds(slot_id, slabs, stride=block_rows), :] = jnp.where(
            empty & diagonal, 1.0, block[:, :lane]
        )
        ending = jnp.where(empty & (short < 3), 1.0, block[:, lane:])
        if slot_id:
            ending = pltpu.roll(ending, 3 * slot_id, 1)
        tail = tail + ending
    out_ref[pl.ds(slots, slabs, stride=block_rows), :] = tail


def trace_codes(list_ref, codes_ref):
    codes = list_ref[0]
    codes = jnp.concatenate([codes[sub_first:], codes[:sub_first]], axis=0)
    half = traces // 2
    for idx in range(traces):
        rows = pl.ds((idx // half) * lane + idx % half, subs, stride=half)
        codes_ref[rows, :] = jnp.broadcast_to(codes[:, idx : idx + 1], (subs, lane))
    codes = codes_ref[...]
    face = face_of(codes)
    return face, codes - new_count * face


def lane_picks(chosen, count):
    lanes = lax.broadcasted_iota(jnp.int32, (remote_count, lane), 1)
    return jnp.concatenate(
        [one_hot(chosen == lanes + tile * lane) for tile in range(count)], axis=1
    )


def plan(list_ref, link_ref, orient_ref, chosen_ref, spread_ref, about_ref, codes_ref):
    face, element = trace_codes(list_ref, codes_ref)
    chosen_ref[...] = node_lanes(face)
    slot_picks = lane_picks(element, tiles)
    rows = lax.broadcasted_iota(jnp.int32, (remote_count, new_count), 0)
    about_rows = lax.broadcasted_iota(jnp.int32, (16, new_count), 0)
    about = None
    spread = None
    for face_id in range(faces):
        far = link_ref[face_id : face_id + 1, :] - column_count
        orient = orient_ref[face_id : face_id + 1, :]
        place = ((far >> 4) + subs - sub_first) & (subs - 1)
        column = ((far >> 3) & 1) * lane + place * 8 + (far & 7)
        column = jnp.where((far >= 0) & (orient < 6), column, -1)
        picks = one_hot(rows == column)
        facts = jnp.where(about_rows == 0, orient, jnp.where(about_rows == 1, face_id, 0))
        term = dot_lanes(facts.astype(jnp.float32).astype(jnp.bfloat16), picks)
        about = term if about is None else about + term
        spread = picks if spread is None else spread + picks
    spread_ref[...] = spread
    about_ref[...] = about[:8]
    return slot_picks


def node_lanes(face):
    lanes = lax.broadcasted_iota(jnp.int32, (1, lane), 1) % half_lane
    node = lanes // components
    comp = lanes - node * components
    tables = []
    for face_id in range(faces):
        row = jnp.zeros((1, lane), jnp.int32)
        for node_id in range(face_nodes):
            row = jnp.where(node == node_id, face_mask[face_id][node_id], row)
        tables.append(comp * node_count + row)
    chosen = tables[0]
    for face_id in range(1, faces):
        chosen = jnp.where(face == face_id, tables[face_id], chosen)
    return chosen


def trace_rows(found, chosen):
    turned = jnp.take_along_axis(found, chosen, axis=1, mode="promise_in_bounds")
    half = remote_count // 2
    lanes = lax.broadcasted_iota(jnp.int32, (half, lane), 1)
    return jnp.where(lanes < half_lane, turned[:half], turned[half:])


def start_kernel(came_ref, list_ref, trace_ref, codes_ref):
    face, element = trace_codes(list_ref, codes_ref)
    source = (element * 5462) >> 16
    turn = (source + slabs - slab_first) & (slabs - 1)
    place = ((turn & (slabs // 2 - 1)) >> 1) * 4 + (turn >> 4) * 2 + (turn & 1)
    picks = lane_picks(place * block_rows + element - source * slots, tiles + 1)
    parts = jnp.concatenate(split_three(came_ref[...]), axis=1)
    parts = jnp.concatenate(
        [parts, jnp.zeros((4 * lane - slabs * block_rows, 3 * lane), jnp.bfloat16)], axis=0
    )
    trace_ref[...] = trace_rows(three_lanes(dot_rows(picks, parts)), node_lanes(face))


def unpack(came_ref, state_ref, derived_ref, rows_ref, tail_ref, main_ref):
    field_rows = components * node_count
    for source, place, count in slab_runs:
        tail_ref[pl.ds(source, count, stride=2), :] = came_ref[
            pl.ds(place * block_rows + slots, count, stride=4 * block_rows), :
        ]
    tail = tail_ref[0:slabs, :]
    for slot_id in range(slots):
        for source, place, count in slab_runs:
            rows_ref[pl.ds(source * slots + slot_id, count, stride=2 * slots), :] = came_ref[
                pl.ds(place * block_rows + slot_id, count, stride=4 * block_rows), :
            ]
        shifted = pltpu.roll(tail, lane - 3 * slot_id, 1) if slot_id else tail
        tail_ref[pl.ds(slot_id, slabs, stride=slots), :] = shifted
    main_ref[...] = jnp.transpose(rows_ref[...])
    extra = jnp.transpose(tail_ref[...])[:8]
    for comp_id in range(components):
        state_ref[comp_id] = main_ref[comp_id * node_count : (comp_id + 1) * node_count, :]
    geo = [main_ref[field_rows + row_id : field_rows + row_id + 1, :] for row_id in range(8)]
    geo.append(extra[0:1])
    derived_ref[0:8, :] = main_ref[field_rows : field_rows + 8, :]
    derived_ref[8:9, :] = extra[0:1]
    derived_ref[9:10, :] = 1.0 / extra[1:2]
    derived_ref[10:11, :] = 1.0 / extra[2:3]
    total = None
    for axis_id in range(3):
        first, second, third = geo[axis_id], geo[3 + axis_id], geo[6 + axis_id]
        normal = 0.5 * jnp.concatenate([-third, -second, first + second + third, -first], axis=0)
        square = normal * normal
        total = square if total is None else total + square
        normal_rows = jnp.concatenate([normal, normal], axis=0)
        derived_ref[16 + 8 * axis_id : 24 + 8 * axis_id, :] = normal_rows
    length = jnp.sqrt(total)
    derived_ref[40:48, :] = jnp.concatenate([length, length], axis=0)
    inverse = 1.0 / length
    derived_ref[48:56, :] = jnp.concatenate([inverse, inverse], axis=0)


def compact(derived_ref, spread_ref, about_ref, far_ref):
    stacked = jnp.concatenate(split_three(derived_ref[16:64, :]), axis=0)
    found = dot_lanes(stacked, spread_ref[...])
    found = found[:48] + found[48:96] + found[96:]
    face = about_ref[1:2, :]
    for block in range(5):
        first_row = 8 * block
        value = found[first_row : first_row + 1]
        for face_id in range(1, faces):
            row_id = first_row + face_id
            value = jnp.where(face == face_id, found[row_id : row_id + 1], value)
        far_ref[block : block + 1, :] = value
    far_ref[5:7, :] = about_ref[0:2, :]
    far_ref[7:8, :] = jnp.zeros((1, remote_count), jnp.float32)


def oriented(planes, orient):
    masks = [orient == turn_id for turn_id in range(6)]
    result = []
    for node_id in range(face_nodes):
        sources = {}
        for turn_id in range(6):
            sources.setdefault(node_perms[turn_id][node_id], []).append(turn_id)
        value = None
        for source, turn_ids in sources.items():
            if value is None:
                value = planes[source]
                continue
            mask = masks[turn_ids[0]]
            for turn_id in turn_ids[1:]:
                mask = mask | masks[turn_id]
            value = jnp.where(mask, planes[source], value)
        result.append(value)
    return result


def face_flux(jump_of, normal, length, inverse):
    jump_h = [jump_of(comp_id) for comp_id in range(3)]
    jump_e = [jump_of(comp_id) for comp_id in range(3, 6)]

    def along(jump):
        total = normal[0] * jump[0] + normal[1] * jump[1] + normal[2] * jump[2]
        return total * inverse

    along_h = along(jump_h)
    along_e = along(jump_e)
    flux_h, flux_e = [], []
    for axis_id in range(3):
        after, last = (axis_id + 1) % 3, (axis_id + 2) % 3
        cross_e = normal[after] * jump_e[last] - normal[last] * jump_e[after]
        cross_h = normal[after] * jump_h[last] - normal[last] * jump_h[after]
        flux_h.append(length * jump_h[axis_id] - normal[axis_id] * along_h - cross_e)
        flux_e.append(length * jump_e[axis_id] - normal[axis_id] * along_e + cross_h)
    return flux_h + flux_e


def lifted_flux(jump_ref, flux_ref, derived_ref, lift_ref):
    groups = faces * face_nodes // 8

    def jump_of(comp_id):
        rows = strided_load(jump_ref, comp_id, faces * face_nodes, 8)
        return rows.reshape(groups, 8, new_count)

    normal = [derived_ref[16 + 8 * axis_id : 24 + 8 * axis_id, :][None] for axis_id in range(3)]
    fluxes = face_flux(jump_of, normal, derived_ref[40:48, :][None], derived_ref[48:56, :][None])
    for comp_id, value in enumerate(fluxes):
        flux_ref[0:40, comp_id * new_count : (comp_id + 1) * new_count] = value.reshape(
            faces * face_nodes, new_count
        )
    flux_ref[40:48, :] = jnp.zeros((8, components * new_count), jnp.float32)
    return dot_rows(lift_ref[...], table_terms(flux_ref[...]))


def strided_load(ref, start, size, stride):
    return jnp.concatenate(
        [ref[tile, pl.ds(start, size, stride=stride), :] for tile in range(ref.shape[0])], axis=1
    )


def tiled_store(ref, rows, value):
    for tile in range(ref.shape[0]):
        ref[tile, rows, :] = value[:, tile * lane : (tile + 1) * lane]


def tiled_load(ref, rows):
    return jnp.concatenate([ref[tile, rows, :] for tile in range(tiles)], axis=1)


def column_block(matrix, comp_id):
    return matrix[:24, comp_id * new_count : (comp_id + 1) * new_count]


def local_part(
    state_ref, derived_ref, link_ref, orient_ref, slope_ref, lift_ref, part_ref, nodes_ref, flat_ref, jump_ref, flux_ref
):
    nodes_ref[...] = jnp.zeros(nodes_ref.shape, jnp.float32)
    flat_ref[node_count:32, :] = jnp.zeros((12, components * new_count), jnp.float32)
    for comp_id in range(components):
        current = state_ref[comp_id]
        tiled_store(nodes_ref, pl.ds(comp_id, node_count, stride=8), current)
        flat_ref[0:node_count, comp_id * new_count : (comp_id + 1) * new_count] = current
    stacked = jnp.concatenate(split_three(tiled_load(nodes_ref, slice(None))), axis=1)
    rows = lax.broadcasted_iota(jnp.int32, (new_count, new_count), 0)
    links = [link_ref[face_id : face_id + 1, :] for face_id in range(faces)]
    owners = [face_of(link) for link in links]
    picks = [
        one_hot(rows == jnp.where(link < column_count, link - new_count * owner, -1))
        for link, owner in zip(links, owners)
    ]
    found_pairs = []
    for first in range(0, faces, 2):
        both = jnp.concatenate(picks[first : first + 2], axis=1)
        found_pairs.append(dot_rows(stacked, jnp.concatenate([both, both, both], axis=0)))
    comp_rows = lax.broadcasted_iota(jnp.int32, (8, new_count), 0)
    wall_gain = jnp.where(comp_rows >= 3, -2.0, 0.0)
    for face_id in range(faces):
        orient = orient_ref[face_id : face_id + 1, :]
        first_column = (face_id % 2) * new_count
        found = found_pairs[face_id // 2][:, first_column : first_column + new_count]
        owner_masks = [owners[face_id] == other for other in range(faces)]
        planes = []
        for node_id in range(face_nodes):
            value = None
            for other in range(faces):
                first_row = 8 * face_mask[other][node_id]
                plane = found[first_row : first_row + 8]
                value = plane if value is None else jnp.where(owner_masks[other], plane, value)
            planes.append(value)
        outside = oriented(planes, orient)
        wall = orient == 6
        for node_id in range(face_nodes):
            first_row = 8 * face_mask[face_id][node_id]
            inside = tiled_load(nodes_ref, slice(first_row, first_row + 8))
            jump = jnp.where(wall, wall_gain * inside, outside[node_id] - inside)
            target = 8 * (node_id * faces + face_id)
            tiled_store(jump_ref, slice(target, target + 8), jump)
    lifted = lifted_flux(jump_ref, flux_ref, derived_ref, lift_ref)
    slopes = dot_rows(slope_ref[...], table_terms(flat_ref[...]))
    inverse_jac = [
        [derived_ref[3 * row_id + axis_id : 3 * row_id + axis_id + 1, :] for axis_id in range(3)]
        for row_id in range(3)
    ]

    def gradient(axis_id, comp_id):
        columns = slice(comp_id * new_count, (comp_id + 1) * new_count)
        return (
            inverse_jac[0][axis_id] * slopes[0:24, columns]
            + inverse_jac[1][axis_id] * slopes[24:48, columns]
            + inverse_jac[2][axis_id] * slopes[48:72, columns]
        )

    inverse_eps = derived_ref[9:10, :]
    inverse_mu = derived_ref[10:11, :]
    for axis_id in range(3):
        after, last = (axis_id + 1) % 3, (axis_id + 2) % 3
        curl_h = gradient(after, last) - gradient(last, after)
        curl_e = gradient(after, 3 + last) - gradient(last, 3 + after)
        change_h = (column_block(lifted, axis_id) - curl_e) * inverse_mu
        change_e = (column_block(lifted, 3 + axis_id) + curl_h) * inverse_eps
        part_ref[axis_id] = change_h[:node_count]
        part_ref[3 + axis_id] = change_e[:node_count]


def arrive_kernel(
    came_ref,
    link_ref,
    orient_ref,
    slope_ref,
    lift_ref,
    list_ref,
    state_ref,
    derived_ref,
    far_ref,
    part_ref,
    chosen_ref,
    spread_ref,
    shared_ref,
    known_ref,
    scale_ref,
    rows_ref,
    tail_ref,
    main_ref,
    about_ref,
    codes_ref,
    *scratches,
):
    picks = plan(list_ref, link_ref, orient_ref, chosen_ref, spread_ref, about_ref, codes_ref)
    shared_ref[...] = dot_lanes(picks, spread_ref[...]).astype(jnp.bfloat16)
    derived_ref[...] = jnp.zeros(derived_ref.shape, jnp.float32)
    unpack(came_ref, state_ref, derived_ref, rows_ref, tail_ref, main_ref)
    compact(derived_ref, spread_ref, about_ref, far_ref)
    local_part(state_ref, derived_ref, link_ref, orient_ref, slope_ref, lift_ref, part_ref, *scratches)
    field_rows = components * node_count
    gain = section_b1 * time_step
    for comp_id in range(components):
        main_ref[comp_id * node_count : (comp_id + 1) * node_count, :] = (
            state_ref[comp_id] + gain * part_ref[comp_id]
        )
    main_ref[field_rows : field_rows + 1, :] = gain * derived_ref[10:11, :]
    main_ref[field_rows + 1 : field_rows + 2, :] = gain * derived_ref[9:10, :]
    main_ref[field_rows + 2 :, :] = jnp.zeros((6, new_count), jnp.float32)
    found = three_lanes(dot_lanes(picks, jnp.concatenate(split_three(main_ref[...]), axis=0)))
    known_ref[...] = trace_rows(found, chosen_ref[...])
    lanes = lax.broadcasted_iota(jnp.int32, (remote_count, lane), 1) % half_lane
    comp = lanes - (lanes // components) * components
    scale_ref[...] = trace_rows(found, jnp.where(comp < 3, field_rows, field_rows + 1))


def local_kernel(*refs):
    local_part(*refs)


def remote_part(came_ref, far_ref, lift_ref, turned_ref, jump_ref):
    turned_ref[...] = jnp.transpose(came_ref[...])
    planes = []
    for node_id in range(face_nodes):
        first_row = node_id * components
        halves_of = [
            turned_ref[half * half_lane + first_row : half * half_lane + first_row + 8, :]
            for half in range(2)
        ]
        planes.append(jnp.concatenate(halves_of, axis=1))
    outside = oriented(planes, far_ref[5:6, :])
    for node_id in range(face_nodes):
        tiled_store(jump_ref, slice(8 * node_id, 8 * node_id + 8), outside[node_id])
    blank = jnp.zeros((8 * (16 - face_nodes), remote_count), jnp.float32)
    tiled_store(jump_ref, slice(8 * face_nodes, 128), blank)
    fluxes = face_flux(
        lambda comp_id: strided_load(jump_ref, comp_id, 16, 8),
        [far_ref[axis_id : axis_id + 1, :] for axis_id in range(3)],
        far_ref[3:4, :],
        far_ref[4:5, :],
    )
    lifted = dot_rows(lift_ref[...], table_terms(jnp.concatenate(fluxes, axis=1)))
    face = far_ref[6:7, :]
    blocks = []
    for comp_id in range(components):
        columns = slice(comp_id * remote_count, (comp_id + 1) * remote_count)
        block = lifted[:24, columns]
        for face_id in range(1, faces):
            block = jnp.where(
                face == face_id, lifted[24 * face_id : 24 * face_id + 24, columns], block
            )
        blocks.append(block)
    return blocks


def placed_part(blocks, spread_ref, derived_ref, wanted):
    stacked = jnp.concatenate([blocks[comp_id] for comp_id in wanted], axis=0)
    rows = stacked.shape[0]
    parts = split_three(stacked)
    if rows % 16:
        blank = jnp.zeros((8, remote_count), jnp.float32)
        parts = split_three(jnp.concatenate([stacked, blank], axis=0))
    step = parts[0].shape[0]
    placed = dot_rows(jnp.concatenate(parts, axis=0), spread_ref[...])
    placed = placed[:rows] + placed[step : step + rows] + placed[2 * step : 2 * step + rows]
    scales = [derived_ref[10:11, :] if comp_id < 3 else derived_ref[9:10, :] for comp_id in wanted]
    return [
        (placed[24 * place : 24 * place + 24] * scale)[:node_count]
        for place, scale in enumerate(scales)
    ]


def first_kernel(
    came_ref,
    part_ref,
    state_ref,
    derived_ref,
    far_ref,
    spread_ref,
    lift_ref,
    shared_ref,
    known_ref,
    scale_ref,
    chosen_ref,
    residual_ref,
    middle_ref,
    trace_ref,
    send_ref,
    sem,
    packed_ref,
    *scratches,
):
    blocks = remote_part(came_ref, far_ref, lift_ref, *scratches)
    for comp_id, block in enumerate(blocks):
        packed_ref[comp_id * node_count : (comp_id + 1) * node_count, :] = block[:node_count]
    packed_ref[components * node_count :, :] = jnp.zeros((8, remote_count), jnp.float32)
    found = dot_lanes(shared_ref[...], jnp.concatenate(split_two(packed_ref[...]), axis=0))
    found = trace_rows(found[:, :lane] + found[:, lane:], chosen_ref[...])
    send_ref[...] = known_ref[...] + scale_ref[...] * found
    copy = pltpu.make_async_copy(send_ref, trace_ref, sem)
    copy.start()
    changes = placed_part(blocks, spread_ref, derived_ref, range(components))
    for comp_id in range(components):
        residual = time_step * (part_ref[comp_id] + changes[comp_id])
        residual_ref[comp_id] = residual
        middle_ref[comp_id] = state_ref[comp_id] + section_b1 * residual
    copy.wait()


def second_kernel(
    came_ref,
    part_ref,
    middle_ref,
    first_ref,
    derived_ref,
    far_ref,
    spread_ref,
    lift_ref,
    advanced_ref,
    residual_ref,
    done_ref,
    sems,
    *scratches,
):
    blocks = remote_part(came_ref, far_ref, lift_ref, *scratches)
    copies = []
    for first in range(0, components, 3):
        changes = placed_part(blocks, spread_ref, derived_ref, range(first, first + 3))
        for comp_id, change in zip(range(first, first + 3), changes):
            residual = section_a2 * first_ref[comp_id] + time_step * (part_ref[comp_id] + change)
            done_ref[0, comp_id] = middle_ref[comp_id] + section_b2 * residual
            done_ref[1, comp_id] = residual
        for place, out_ref in enumerate((advanced_ref, residual_ref)):
            copy = pltpu.make_async_copy(
                done_ref.at[place, pl.ds(first, 3)],
                out_ref.at[pl.ds(first, 3)],
                sems.at[place, first // 3],
            )
            copy.start()
            copies.append(copy)
    for copy in copies:
        copy.wait()


def floats(*shape):
    return jax.ShapeDtypeStruct(shape, jnp.float32)


def halves(*shape):
    return jax.ShapeDtypeStruct(shape, jnp.bfloat16)


def scratch(*shape):
    return pltpu.VMEM(shape, jnp.float32)


fast = pl.BlockSpec(memory_space=pltpu.VMEM)
free = pl.BlockSpec(memory_space=pl.ANY)


def run(kernel, name, outs, scratches, operands, in_specs=None, out_specs=None):
    return pl.pallas_call(
        kernel,
        name=name,
        out_shape=outs,
        in_specs=in_specs or [fast] * len(operands),
        out_specs=out_specs or jax.tree.map(lambda _: fast, outs),
        scratch_shapes=scratches,
        compiler_params=pltpu.CompilerParams(vmem_limit_bytes=24 * 2**20),
        cost_estimate=pl.CostEstimate(flops=10**8, bytes_accessed=10**6, transcendentals=0),
    )(*operands)


def shards(fields, geometry, migrate_list, trace_list, face_link, face_orient):
    slopes = slope_operand()
    lift = lift_operand()
    remote_lift = remote_lift_operand()
    state_shape = floats(components, node_count, new_count)
    trace_shape = floats(remote_count // 2, lane)
    local_scratch = [
        scratch(tiles, 8 * node_count, lane),
        scratch(32, components * new_count),
        scratch(tiles, 8 * faces * face_nodes, lane),
        scratch(48, components * new_count),
    ]
    remote_scratch = [scratch(lane, lane), scratch(2, lane, lane)]
    parcel = run(
        pack_kernel,
        "pack",
        floats(slabs * block_rows, lane),
        [
            scratch(components, node_count, old_count),
            scratch(11, old_count),
            pltpu.VMEM((slots, 1, slabs), jnp.int32),
            scratch(144, old_count),
            pltpu.SemaphoreType.DMA((3,)),
        ],
        [
            pltpu.with_memory_space_constraint(operand, pltpu.HBM)
            for operand in (fields, geometry, jnp.transpose(migrate_list, (2, 0, 1)))
        ],
        [pl.BlockSpec(memory_space=pltpu.HBM)] * 3,
    )
    arrived = lax.all_to_all(
        parcel.reshape(slabs, block_rows * lane), "slab", split_axis=0, concat_axis=0, tiled=True,
        axis_index_groups=[slab_order],
    ).reshape(slabs * block_rows, lane)
    code_scratch = pltpu.VMEM((remote_count, lane), jnp.int32)
    outgoing = run(
        start_kernel, "start", trace_shape, [code_scratch], (arrived, trace_list)
    )

    def exchange(rows):
        blocks = rows.reshape(subs, traces // 2, lane)
        came = lax.all_to_all(
            blocks, "sub", split_axis=0, concat_axis=0, tiled=True, axis_index_groups=[sub_order]
        )
        return came.reshape(remote_count // 2, lane)

    incoming = exchange(outgoing)
    state, derived, far, part, chosen, spread, shared, known, scale = run(
        arrive_kernel,
        "arrive",
        (
            state_shape,
            floats(64, new_count),
            floats(8, remote_count),
            state_shape,
            jax.ShapeDtypeStruct((remote_count, lane), jnp.int32),
            halves(remote_count, new_count),
            halves(remote_count, remote_count),
            floats(remote_count // 2, lane),
            floats(remote_count // 2, lane),
        ),
        [
            scratch(new_count, lane),
            scratch(new_count, lane),
            scratch(lane, new_count),
            scratch(8, remote_count),
            code_scratch,
        ]
        + local_scratch,
        (arrived, face_link, face_orient, slopes, lift, trace_list),
    )
    first_res, middle, outgoing = run(
        first_kernel,
        "first",
        (state_shape, state_shape, trace_shape),
        [scratch(remote_count // 2, lane), pltpu.SemaphoreType.DMA, scratch(lane, remote_count)]
        + remote_scratch,
        (
            incoming,
            part,
            state,
            derived,
            far,
            spread,
            remote_lift,
            shared,
            known,
            scale,
            chosen,
        ),
        out_specs=(fast, fast, free),
    )
    incoming = exchange(outgoing)
    part = run(
        local_kernel,
        "local",
        state_shape,
        local_scratch,
        (middle, derived, face_link, face_orient, slopes, lift),
    )
    return run(
        second_kernel,
        "second",
        (state_shape, state_shape),
        [scratch(2, components, node_count, new_count), pltpu.SemaphoreType.DMA((2, 2))]
        + remote_scratch,
        (incoming, part, middle, first_res, derived, far, spread, remote_lift),
        out_specs=(free, free),
    )


def solution(mesh):
    return jax.shard_map(
        shards,
        mesh=mesh,
        in_specs=(
            P(None, None, ("slab", "sub")),
            P(None, ("slab", "sub")),
            P(("slab", "sub"), None, None),
            P(("slab", "sub"), None, None),
            P(None, ("slab", "sub")),
            P(None, ("slab", "sub")),
        ),
        out_specs=(P(None, None, ("slab", "sub")), P(None, None, ("slab", "sub"))),
        check_vma=False,
    )
```
